32 devices in a mesh: pipe: 2 (over x), ep: 16 (over z, y, core).
Axes of the slice: x: 2, y: 2, z: 4, core: 2. Of those that a mesh axis runs over, the one named last changes fastest.
Arguments:
- entering: bfloat16 [2, 1536, 2048], P(None, 'ep'), may hold values from -6 to 6
- rising_prev: bfloat16 [2, 1536, 2048], P('pipe', 'ep'), may hold values from -6 to 6
- falling_cot: bfloat16 [2, 1536, 2048], P('pipe', 'ep'), may hold values from -6 to 6
- falling_saved: bfloat16 [2, 1536, 2048], P('pipe', 'ep'), may hold values from -6 to 6
- targets: bfloat16 [2, 1536, 2048], P(None, 'ep'), may hold values from -6 to 6
- norm_gain: float32 [2, 2048], P('pipe'), may hold values from 0.5 to 1.5
- exit_gain: float32 [2, 2048], P('pipe'), may hold values from 0.5 to 1.5
- w_gate: bfloat16 [2, 16, 2048, 512], P('pipe', 'ep'), may hold values from -0.125 to 0.125
- w_up: bfloat16 [2, 16, 2048, 512], P('pipe', 'ep'), may hold values from -0.125 to 0.125
- w_down: bfloat16 [2, 16, 512, 2048], P('pipe', 'ep'), may hold values from -0.25 to 0.25
- route_ids: int32 [2, 2, 1536, 8], P(None, 'pipe', 'ep'), may hold values from 0 to 15, all different within a row; in each aligned block of 96 rows (0 to 95, 96 to 191, ..., all dimensions but the last counted through in order) at most 52 rows name the same one
- route_gates: float32 [2, 2, 1536, 8], P(None, 'pipe', 'ep'), may hold values from 0.02 to 0.3
- exit_list: int32 [2, 2], replicated, may hold values 0 or 1
Outputs:
- rising_next: bfloat16 [2, 1536, 2048], P('pipe', 'ep')
- falling_next: bfloat16 [2, 1536, 2048], P('pipe', 'ep')
- exit_loss: float32 [2, 2, 1536], P(None, 'pipe', 'ep')
The draws below stay inside these ranges and needn't reach their ends.
Inputs may be any that keep to these rules, and one draw needn't show every extreme that they name: `route_ids`: in each aligned block of 96 tokens (one device's tokens of one micro-batch at one section) a row names 8 different experts and no expert is named by more than 52 rows; in some blocks an expert is named by exactly 52 rows.
All inputs are finite; a program needn't handle non-finite values.
Results may differ from the reference program's by a relative error of at most 0.0045.
Values may be sent and summed in bfloat16 or wider, within the bound.
No kernel may reach another device: no remote copies, remote signals or barrier semaphores. Data moves between devices by JAX's collectives and lax.ppermute only.
A program may use at most 128 MiB of HBM per device.

```python
import math
import jax
import jax.numpy as jnp
import numpy as np
from jax import lax

D = 2048
TOP = 8
FFW = 512
TOK_DEV = 96
SECTIONS = 2
EXPERTS = 16
TOKENS = 1536
CAP = 52
N_EP = 16


def plant(entries, own_key, smallest, top_value):
    place = [jax.random.randint(jax.random.fold_in(own_key, axis), (), 0, length) for axis, length in enumerate(entries.shape)]
    main_axis = entries.shape.index(max(entries.shape))
    next_to = place[:main_axis] + [(place[main_axis] + 1) % entries.shape[main_axis]] + place[main_axis + 1:]
    return entries.at[tuple(place)].set(smallest).at[tuple(next_to)].set(top_value)


def block_levels(rng, shape, shards, smallest, high):
    def one(axis_at, blocks):
        draws = jax.random.uniform(jax.random.fold_in(jax.random.fold_in(rng, 6), axis_at), (blocks,), jnp.float32, smallest / len(shards), high / len(shards))
        return jnp.repeat(jnp.exp(draws), shape[axis_at] // blocks).reshape((-1,) + (1,) * (len(shape) - axis_at - 1))

    gain = one(*shards[0])
    for cut in shards[1:]:
        gain = gain * one(*cut)
    return gain


def deal_out(key, own, number, rows, number_of, top, limit, skew):
    ranking = jax.random.permutation(key, number_of)
    crowded, common = portions_of(number_of, rows * top, limit, skew, True), portions_of(number_of, rows * top, limit, skew, False)
    places = jnp.arange(number_of)

    def named(tallies, offset_by):
        used = int((tallies > 0).sum())
        fixed = max(1, used // 4)
        passed = fixed + (places - fixed + offset_by * (used - fixed)) % max(1, number_of - fixed)
        return jnp.zeros((number_of,), jnp.int32).at[ranking[jnp.where(places < fixed, places, passed)]].set(jnp.asarray(tallies, jnp.int32))

    tallies = jnp.where(number % 4 == 0, named(crowded, number // 4), named(common, number - number // 4 - 1))
    mixed = jax.random.permutation(jax.random.fold_in(own, 3), number_of)
    donor, receiver = mixed[0:number_of // 2 * 2:2], mixed[1:number_of // 2 * 2:2]
    slack = jnp.minimum(tallies[donor] - 1, limit - tallies[receiver]) // 2
    slack = jnp.where((donor == ranking[0]) | (receiver == ranking[0]) | (tallies[receiver] == 0), 0, jnp.maximum(slack, 0))
    passed = jax.random.randint(jax.random.fold_in(own, 4), (number_of // 2,), 0, 1 << 20) % (slack + 1)
    tallies = tallies.at[donor].add(-passed).at[receiver].add(passed)
    items = jnp.searchsorted(jnp.cumsum(tallies), jnp.arange(rows * top), side="right").astype(jnp.int32)
    grid = items.reshape(top, rows).T
    grid = grid[jax.random.permutation(jax.random.fold_in(own, 1), rows)]
    offset_by = jax.random.randint(jax.random.fold_in(own, 2), (rows, 1), 0, top)
    return jnp.take_along_axis(grid, (jnp.arange(top)[None, :] + offset_by) % top, axis=1)


def portions_of(count, total, reach, slope, full):
    weights = [(1 << 20) // math.isqrt(standing ** slope) + 1 for standing in range(1, count + 1)]
    largest = reach if full else min(reach, max(-(-total // count), total * weights[0] // sum(weights)))
    least = 1 if total - largest >= count - 1 else 0
    counts, rest = [largest] + [least] * (count - 1), total - largest - least * (count - 1)
    while rest > 0:
        candidates = [i for i in range(1, count) if counts[i] < largest] or [i for i in range(1, count) if counts[i] < reach]
        mass, remaining = sum([weights[i] for i in candidates]), rest
        for i in candidates:
            extra = min(reach - counts[i], max(1, remaining * weights[i] // mass), rest)
            counts[i] = counts[i] + extra
            rest = rest - extra
    return np.array(counts)


def noise(own_key, shape, deviation, limit, shards=(), kind=jnp.bfloat16):
    array = deviation * jax.random.normal(own_key, shape, jnp.float32)
    if shards:
        array = array * block_levels(own_key, shape, shards, -0.22, 0.18)
    return jnp.clip(array, -limit, limit).astype(kind)


def setup_inputs(seed: int = 0) -> dict:
    keys = jax.random.split(jax.random.key(seed), 14)
    entering = noise(keys[0], (2, TOKENS, D), 1.0, 6.0, ((1, 16),))
    rising_prev = noise(keys[1], (SECTIONS, TOKENS, D), 1.0, 6.0, ((0, 2), (1, 16)))
    falling_cot = noise(keys[2], (SECTIONS, TOKENS, D), 1.0, 6.0, ((0, 2), (1, 16)))
    falling_saved = noise(keys[3], (SECTIONS, TOKENS, D), 1.0, 6.0, ((0, 2), (1, 16)))
    targets = noise(keys[4], (2, TOKENS, D), 1.0, 6.0, ((1, 16),))
    norm_gain = jnp.clip(0.5 + 1.0 * jax.random.uniform(keys[5], (SECTIONS, D), jnp.float32) ** block_levels(keys[5], (SECTIONS, D), ((0, 2),), -0.2, 0.2), 0.5, 1.5)
    exit_gain = jnp.clip(0.5 + 1.0 * jax.random.uniform(keys[6], (SECTIONS, D), jnp.float32) ** block_levels(keys[6], (SECTIONS, D), ((0, 2),), -0.2, 0.2), 0.5, 1.5)
    w_gate = noise(keys[7], (SECTIONS, EXPERTS, D, FFW), D ** -0.5, 0.125, ((0, 2), (1, 16)))
    w_up = noise(keys[8], (SECTIONS, EXPERTS, D, FFW), D ** -0.5, 0.125, ((0, 2), (1, 16)))
    w_down = noise(keys[9], (SECTIONS, EXPERTS, FFW, D), FFW ** -0.5, 0.25, ((0, 2), (1, 16)))
    route_ids_keys = jax.random.split(jax.random.fold_in(keys[10], 1), 2 * SECTIONS * TOKENS // TOK_DEV)
    route_ids_turns = jax.random.permutation(jax.random.fold_in(keys[10], 3), 2 * SECTIONS * TOKENS // TOK_DEV)
    route_ids = jax.vmap(lambda own, number: deal_out(jax.random.fold_in(keys[10], 2), own, number, TOK_DEV, EXPERTS, TOP, CAP, 2))(route_ids_keys, route_ids_turns).reshape((2, SECTIONS, TOKENS, TOP))
    route_gates = jnp.clip(0.02 + 0.28 * jax.random.uniform(keys[11], (2, SECTIONS, TOKENS, TOP), jnp.float32) ** block_levels(keys[11], (2, SECTIONS, TOKENS, TOP), ((1, 2), (2, 16)), -0.2, 0.2), 0.02, 0.3)
    exit_list = plant((jax.random.randint(keys[12], (2, SECTIONS), 0, 2) < 1).astype(jnp.int32), jax.random.fold_in(keys[12], 1), 0, 1)
    return dict(entering=entering, rising_prev=rising_prev, falling_cot=falling_cot, falling_saved=falling_saved, targets=targets, norm_gain=norm_gain, exit_gain=exit_gain, w_gate=w_gate, w_up=w_up, w_down=w_down, route_ids=route_ids, route_gates=route_gates, exit_list=exit_list)


EPSILON = 1e-06

def normed(values, gain_row):
    return values * lax.rsqrt(lax.optimization_barrier(jnp.mean(values * values, axis=-1, keepdims=True)) + EPSILON) * gain_row

def norm_pullback(values, gain_row, upstream):
    _, pullback = jax.vjp(lambda argument: normed(argument, gain_row), values)
    return pullback(upstream)[0]

def slot_targets(choice_ids):
    blocks_ids = choice_ids.reshape(N_EP, -1)
    onehot = (blocks_ids[:, :, None] == jnp.arange(EXPERTS, dtype=jnp.int32)[None, None, :]).astype(jnp.int32)
    earlier = jnp.cumsum(onehot, axis=1) - onehot
    slot_rank = lax.optimization_barrier(jnp.sum(earlier * onehot, axis=2))
    source = jnp.arange(N_EP, dtype=jnp.int32)[:, None]
    places = blocks_ids * (N_EP * CAP) + source * CAP + slot_rank
    return places.reshape(TOKENS, TOP).astype(jnp.int32)

def fill_slots(places, slot_values):
    empty = jnp.zeros((EXPERTS * N_EP * CAP, D), jnp.bfloat16)
    return empty.at[places.reshape(-1)].set(slot_values.reshape(-1, D))

def expert_forward(row_block, gate_weight, up_weight, down_weight):
    gate_proj = jnp.dot(row_block, gate_weight, preferred_element_type=jnp.float32)
    second = jnp.dot(row_block, up_weight, preferred_element_type=jnp.float32)
    hidden = (jax.nn.silu(gate_proj) * second).astype(jnp.bfloat16)
    return jnp.dot(hidden, down_weight, preferred_element_type=jnp.float32).astype(jnp.bfloat16)

def expert_backward(row_block, upstream, gate_weight, up_weight, down_weight):
    gate_proj = jnp.dot(row_block, gate_weight, preferred_element_type=jnp.float32)
    second = jnp.dot(row_block, up_weight, preferred_element_type=jnp.float32)
    contract = (((1,), (1,)), ((), ()))
    hidden_grad = lax.dot_general(upstream, down_weight, contract, preferred_element_type=jnp.float32)
    sigmoid_part = jax.nn.sigmoid(gate_proj)
    activated = gate_proj * sigmoid_part
    gate_grad = (hidden_grad * second * sigmoid_part * (1.0 + gate_proj * (1.0 - sigmoid_part))).astype(jnp.bfloat16)
    second_grad = (hidden_grad * activated).astype(jnp.bfloat16)
    returned = lax.dot_general(gate_grad, gate_weight, contract, preferred_element_type=jnp.float32)
    returned = returned + lax.dot_general(second_grad, up_weight, contract, preferred_element_type=jnp.float32)
    return returned.astype(jnp.bfloat16)

def through_experts(row_fn, buffers, weights):
    shaped = tuple((buffer.reshape(EXPERTS, N_EP * CAP, D) for buffer in buffers))
    outputs = lax.map(lambda packed: row_fn(*packed), shaped + weights)
    return outputs.reshape(EXPERTS * N_EP * CAP, D)

def reference(entering, rising_prev, falling_cot, falling_saved, targets, norm_gain, exit_gain, w_gate, w_up, w_down, route_ids, route_gates, exit_list):
    rise_out, fall_out, loss_rise, loss_fall = ([], [], [], [])
    for section_index in range(SECTIONS):
        rise_in = entering[0] if section_index == 0 else rising_prev[section_index - 1]
        cotangent = (entering[1] if section_index == 0 else falling_cot[section_index - 1]).astype(jnp.float32)
        head_rise = exit_list[0, section_index].astype(jnp.float32)
        head_fall = exit_list[1, SECTIONS - 1 - section_index].astype(jnp.float32)
        weights = (w_gate[section_index], w_up[section_index], w_down[section_index])
        rise_wide = rise_in.astype(jnp.float32)
        places = slot_targets(route_ids[0, section_index])
        normal_rows = normed(rise_wide, norm_gain[section_index]).astype(jnp.bfloat16)
        buffer = fill_slots(places, jnp.broadcast_to(normal_rows[:, None, :], (TOKENS, TOP, D)))
        outputs = through_experts(expert_forward, (buffer,), weights)
        picked = outputs[places].astype(jnp.float32)
        layer_out = rise_wide + jnp.einsum('tk,tkd->td', route_gates[0, section_index], picked)
        rise_out.append(layer_out.astype(jnp.bfloat16))
        exit_diff = normed(rise_wide, exit_gain[section_index]) - targets[0].astype(jnp.float32)
        loss_rise.append(head_rise * 0.5 * lax.optimization_barrier(jnp.mean(exit_diff * exit_diff, axis=-1)))
        fall_wide = falling_saved[section_index].astype(jnp.float32)
        places = slot_targets(route_ids[1, section_index])
        normal_rows = normed(fall_wide, norm_gain[section_index]).astype(jnp.bfloat16)
        slot_cot = (route_gates[1, section_index][:, :, None] * cotangent[:, None, :]).astype(jnp.bfloat16)
        buffer_rows = fill_slots(places, jnp.broadcast_to(normal_rows[:, None, :], (TOKENS, TOP, D)))
        buffer_cot = fill_slots(places, slot_cot)
        slot_grads = through_experts(expert_backward, (buffer_rows, buffer_cot), weights)
        norm_grad = lax.optimization_barrier(jnp.sum(slot_grads[places].astype(jnp.float32), axis=1))
        exit_diff = normed(fall_wide, exit_gain[section_index]) - targets[1].astype(jnp.float32)
        fall_total = cotangent + norm_pullback(fall_wide, norm_gain[section_index], norm_grad)
        fall_total = fall_total + head_fall * norm_pullback(fall_wide, exit_gain[section_index], exit_diff)
        fall_out.append(fall_total.astype(jnp.bfloat16))
        loss_fall.append(head_fall * 0.5 * lax.optimization_barrier(jnp.mean(exit_diff * exit_diff, axis=-1)))
    exit_loss = jnp.stack([jnp.stack(loss_rise), jnp.stack(loss_fall)])
    return (jnp.stack(rise_out), jnp.stack(fall_out), exit_loss)
```

```python
import jax
import jax.numpy as jnp
from jax import lax
from jax.sharding import PartitionSpec as P

EPSILON = 1e-06


def passed_along(block, axis, distance):
    devices = range(lax.axis_size(axis))
    route = [(i - distance, i) for i in devices if i - distance in devices]
    return lax.ppermute(block, axis, route)


def normed(values, gain_row):
    return (
        values * lax.rsqrt(jnp.mean(values * values, axis=-1, keepdims=True) + EPSILON) * gain_row
    )


def norm_pullback(values, gain_row, upstream):
    _, pullback = jax.vjp(lambda argument: normed(argument, gain_row), values)
    return pullback(upstream)[0]


def dense_gates(choice_ids, gates, experts):
    onehot = choice_ids[:, :, None] == jnp.arange(experts, dtype=jnp.int32)[None, None, :]
    return jnp.sum(jnp.where(onehot, gates[:, :, None], 0.0), axis=1)


def in_parts(row_fn, *arrays, limit=768):
    rows = arrays[0].shape[0]
    if rows <= limit:
        return row_fn(*arrays)
    shaped = [array.reshape((rows // limit, limit) + array.shape[1:]) for array in arrays]
    out = lax.map(lambda packed: row_fn(*packed), shaped)
    return out.reshape((rows,) + out.shape[2:])


def expert_forward(rows, gate_weight, up_weight, down_weight):
    gate_proj = jnp.dot(rows, gate_weight, preferred_element_type=jnp.float32)
    second = jnp.dot(rows, up_weight, preferred_element_type=jnp.float32)
    hidden = (jax.nn.silu(gate_proj) * second).astype(jnp.bfloat16)
    return jnp.dot(hidden, down_weight, preferred_element_type=jnp.float32)


def expert_backward(rows, upstream, gate_weight, up_weight, down_weight):
    gate_proj = jnp.dot(rows, gate_weight, preferred_element_type=jnp.float32)
    second = jnp.dot(rows, up_weight, preferred_element_type=jnp.float32)
    contract = (((1,), (1,)), ((), ()))
    hidden_grad = lax.dot_general(
        upstream, down_weight, contract, preferred_element_type=jnp.float32
    )
    sigmoid_part = jax.nn.sigmoid(gate_proj)
    activated = gate_proj * sigmoid_part
    gate_grad = (
        hidden_grad * second * sigmoid_part * (1.0 + gate_proj * (1.0 - sigmoid_part))
    ).astype(jnp.bfloat16)
    second_grad = (hidden_grad * activated).astype(jnp.bfloat16)
    returned = lax.dot_general(gate_grad, gate_weight, contract, preferred_element_type=jnp.float32)
    return returned + lax.dot_general(
        second_grad, up_weight, contract, preferred_element_type=jnp.float32
    )


def local(
    entering,
    rising_prev,
    falling_cot,
    falling_saved,
    targets,
    norm_gain,
    exit_gain,
    w_gate,
    w_up,
    w_down,
    route_ids,
    route_gates,
    exit_list,
):
    section_index = lax.axis_index("pipe")
    sections = lax.axis_size("pipe")
    sources = lax.axis_size("ep")
    here = lax.axis_index("ep")
    core = here % 2
    groups = [list(range(start, sources, 2)) for start in range(2)]
    norm_row = norm_gain[0]
    exit_row = exit_gain[0]

    def gathered(block):
        return lax.all_gather(block, "ep", axis_index_groups=groups, tiled=True)

    def scattered(block):
        return lax.psum_scatter(
            block, "ep", scatter_dimension=0, axis_index_groups=groups, tiled=True
        )

    own = (w_gate[0, 0], w_up[0, 0], w_down[0, 0])
    swap = [(i, i ^ 1) for i in range(sources)]
    other = lax.ppermute(own, "ep", swap)

    fall_wide = falling_saved[0].astype(jnp.float32)
    fall_normal = normed(fall_wide, norm_row).astype(jnp.bfloat16)
    all_fall = gathered(fall_normal)

    gate_table = jnp.stack(
        [dense_gates(route_ids[m, 0], route_gates[m, 0], sources) for m in range(2)], axis=1
    )
    all_gates = gathered(gate_table)
    gates_own = lax.dynamic_index_in_dim(all_gates, here, 2, keepdims=True)
    gates_other = lax.dynamic_index_in_dim(all_gates, here + 1 - 2 * core, 2, keepdims=True)

    moved_cot, moved_rise = passed_along((falling_cot[0], rising_prev[0]), "pipe", 1)
    at_start = section_index == 0
    cot_in = jnp.where(at_start, entering[1], moved_cot)
    all_cot = gathered(cot_in)
    rise_in = jnp.where(at_start, entering[0], moved_rise)
    rise_wide = rise_in.astype(jnp.float32)
    rise_normal = normed(rise_wide, norm_row).astype(jnp.bfloat16)
    cotangent = cot_in.astype(jnp.float32)
    head_rise = jnp.take(exit_list[0], section_index).astype(jnp.float32)
    head_fall = jnp.take(exit_list[1], sections - 1 - section_index).astype(jnp.float32)

    def pair_backward(rows, upstream, gates_first, gates_second):
        made = 0.0
        for weights, gates in ((own, gates_first), (other, gates_second)):
            slot_cot = (gates[:, 1] * upstream.astype(jnp.float32)).astype(jnp.bfloat16)
            made = made + expert_backward(rows, slot_cot, *weights)
        return made.astype(jnp.bfloat16)

    def pair_forward(rows, gates_first, gates_second):
        made = 0.0
        for weights, gates in ((own, gates_first), (other, gates_second)):
            made = made + gates[:, 0] * expert_forward(rows, *weights)
        return made.astype(jnp.bfloat16)

    made_fall = in_parts(pair_backward, all_fall, all_cot, gates_own, gates_other)
    norm_grad = scattered(made_fall).astype(jnp.float32)
    if sources > 16:
        rise_normal, norm_grad = lax.optimization_barrier((rise_normal, norm_grad))
    all_rise = gathered(rise_normal)
    made_rise = in_parts(pair_forward, all_rise, gates_own, gates_other)
    layer_out = rise_wide + scattered(made_rise).astype(jnp.float32)

    rise_diff = normed(rise_wide, exit_row) - targets[0].astype(jnp.float32)
    loss_rise = head_rise * 0.5 * jnp.mean(rise_diff * rise_diff, axis=-1)
    fall_diff = normed(fall_wide, exit_row) - targets[1].astype(jnp.float32)
    fall_total = cotangent + norm_pullback(fall_wide, norm_row, norm_grad)
    fall_total = fall_total + head_fall * norm_pullback(fall_wide, exit_row, fall_diff)
    loss_fall = head_fall * 0.5 * jnp.mean(fall_diff * fall_diff, axis=-1)
    exit_loss = jnp.stack([loss_rise, loss_fall])[:, None, :]
    return (layer_out.astype(jnp.bfloat16)[None], fall_total.astype(jnp.bfloat16)[None], exit_loss)


def solution(mesh):
    placed = (
        P(None, "ep", None),
        P("pipe", "ep", None),
        P("pipe", "ep", None),
        P("pipe", "ep", None),
        P(None, "ep", None),
        P("pipe", None),
        P("pipe", None),
        P("pipe", "ep", None, None),
        P("pipe", "ep", None, None),
        P("pipe", "ep", None, None),
        P(None, "pipe", "ep", None),
        P(None, "pipe", "ep", None),
        P(),
    )
    return jax.shard_map(
        local,
        mesh=mesh,
        in_specs=placed,
        out_specs=(P("pipe", "ep", None), P("pipe", "ep", None), P(None, "pipe", "ep")),
        check_vma=False,
    )
```

```python
import functools
import jax
import jax.numpy as jnp
from jax import lax
from jax.experimental import pallas as pl
from jax.experimental.pallas import tpu as pltpu
from jax.sharding import PartitionSpec as P

EPSILON = 1e-06
VMEM_LIMIT = 56 * 1024 * 1024
NT = (((1,), (1,)), ((), ()))


def passed_along(block, axis, distance):
    devices = range(lax.axis_size(axis))
    route = [(i - distance, i) for i in devices if i - distance in devices]
    return lax.ppermute(block, axis, route)


def normed(values, gain_row):
    return (
        values * lax.rsqrt(jnp.mean(values * values, axis=-1, keepdims=True) + EPSILON) * gain_row
    )


def norm_pullback(values, gain_row, upstream):
    _, pullback = jax.vjp(lambda argument: normed(argument, gain_row), values)
    return pullback(upstream)[0]


def pack_kernel(experts, rows_ref, gain_ref, ids_ref, gates_ref, out_ref):
    width = rows_ref.shape[1]
    out_ref[:, :width] = normed(rows_ref[...].astype(jnp.float32), gain_ref[...]).astype(
        jnp.bfloat16
    )
    count, extra = rows_ref.shape[0], out_ref.shape[1] - width
    lane = lax.broadcasted_iota(jnp.int32, (count, extra), 1)
    table = jnp.zeros((count, extra), jnp.float32)
    for m in range(2):
        for k in range(ids_ref.shape[2]):
            place = ids_ref[m, :, k : k + 1] + 2 * m * experts
            gate = gates_ref[m, :, k : k + 1]
            high = gate.astype(jnp.bfloat16).astype(jnp.float32)
            table = jnp.where(lane == place, high, table)
            table = jnp.where(lane == place + experts, gate - high, table)
    out_ref[:, width:] = table.astype(jnp.bfloat16)


def packed_rows(rows, gain_row, ids, gates, experts):
    count, width = rows.shape
    extra = -(-4 * experts // 128) * 128
    return pl.pallas_call(
        functools.partial(pack_kernel, experts),
        out_shape=jax.ShapeDtypeStruct((count, width + extra), jnp.bfloat16),
        compiler_params=pltpu.CompilerParams(vmem_limit_bytes=VMEM_LIMIT),
        cost_estimate=pl.CostEstimate(flops=0, bytes_accessed=count * width * 8, transcendentals=0),
    )(rows, gain_row, ids, gates)


def gate_column(table, micro, experts, expert):
    lane = lax.broadcasted_iota(jnp.int32, table.shape, 1)
    place = 2 * micro * experts + expert
    chosen = (lane == place) | (lane == place + experts)
    return jnp.sum(jnp.where(chosen, table, 0.0), axis=1, keepdims=True)


def start_all(copies):
    for copy in copies:
        copy.start()


def wait_all(copies):
    for copy in copies:
        copy.wait()


def block_copies(sources, target, sems, columns=None):
    copies, start = [], 0
    for i, source in enumerate(sources):
        count = source.shape[0]
        view = source if columns is None else source.at[:, columns]
        copies.append(
            pltpu.make_async_copy(view, target.at[pl.ds(start, count)], sems.at[i])
        )
        start += count
    return copies


def write_tiles(tile, outs, columns):
    start = 0
    for out in outs:
        count = out.shape[0]
        out[:, columns] = tile[start : start + count].astype(out.dtype)
        start += count


def forward_kernel(parts, experts, width, tile, names_ref, *refs):
    packed, rows = refs[:parts], refs[parts : 2 * parts]
    weights = refs[2 * parts : 2 * parts + 6]
    outs = refs[2 * parts + 6 : 3 * parts + 6]
    (table, held, hidden, gate_w, up_w, down_w, table_sem, row_sem, weight_sem) = refs[
        3 * parts + 6 :
    ]
    extra = table.shape[1]
    table_copies = block_copies(packed, table, table_sem, pl.ds(width, extra))
    row_copies = block_copies(rows, held, row_sem)
    weight_copies = [
        [
            pltpu.make_async_copy(weights[3 * e + i], target.at[e], weight_sem.at[3 * e + i])
            for i, target in enumerate((gate_w, up_w, down_w))
        ]
        for e in range(2)
    ]
    start_all(row_copies + table_copies)
    start_all(weight_copies[0] + weight_copies[1])
    wait_all(row_copies + table_copies)
    inner = gate_w.shape[2]
    for e in range(2):
        gate = gate_column(table[...].astype(jnp.float32), 0, experts, names_ref[e])
        wait_all(weight_copies[e][:2])

        @pl.loop(0, inner // tile)
        def _(f, e=e, gate=gate):
            columns = pl.ds(pl.multiple_of(f * tile, tile), tile)
            first = jnp.dot(held[...], gate_w[e, :, columns], preferred_element_type=jnp.float32)
            second = jnp.dot(held[...], up_w[e, :, columns], preferred_element_type=jnp.float32)
            made = gate * (jax.nn.silu(first) * second)
            places = pl.ds(pl.multiple_of(e * inner + f * tile, tile), tile)
            hidden[:, places] = made.astype(jnp.bfloat16)

    wait_all([weight_copies[0][2], weight_copies[1][2]])

    @pl.loop(0, width // tile)
    def _(n):
        columns = pl.ds(pl.multiple_of(n * tile, tile), tile)
        total = jnp.dot(
            hidden[:, :inner], down_w[0, :, columns], preferred_element_type=jnp.float32
        ) + jnp.dot(hidden[:, inner:], down_w[1, :, columns], preferred_element_type=jnp.float32)
        write_tiles(total, outs, columns)


def backward_kernel(parts, experts, width, tile, names_ref, *refs):
    packed, cots = refs[:parts], refs[parts : 2 * parts]
    weights = refs[2 * parts : 2 * parts + 6]
    outs = refs[2 * parts + 6 : 3 * parts + 6]
    (held, cot, slot, grads, gate_w, up_w, down_w, row_sem, cot_sem, weight_sem) = refs[
        3 * parts + 6 :
    ]
    row_copies = block_copies(packed, held, row_sem)
    cot_copies = block_copies(cots, cot, cot_sem)
    weight_copies = [
        [
            pltpu.make_async_copy(weights[3 * e + i], target.at[e], weight_sem.at[3 * e + i])
            for i, target in enumerate((gate_w, up_w, down_w))
        ]
        for e in range(2)
    ]
    start_all(row_copies + cot_copies)
    start_all(weight_copies[0] + weight_copies[1])
    wait_all(row_copies + cot_copies)
    inner = gate_w.shape[2]
    for e in range(2):
        table = held[:, width:].astype(jnp.float32)
        gate = gate_column(table, 1, experts, names_ref[e])
        slot[...] = (gate * cot[...].astype(jnp.float32)).astype(jnp.bfloat16)
        wait_all(weight_copies[e])

        @pl.loop(0, inner // tile)
        def _(f, e=e):
            columns = pl.ds(pl.multiple_of(f * tile, tile), tile)
            rows = held[:, :width]
            first = jnp.dot(rows, gate_w[e, :, columns], preferred_element_type=jnp.float32)
            second = jnp.dot(rows, up_w[e, :, columns], preferred_element_type=jnp.float32)
            back = lax.dot_general(
                slot[...], down_w[e, columns, :], NT, preferred_element_type=jnp.float32
            )
            sigmoid_part = jax.nn.sigmoid(first)
            gate_grad = back * second * sigmoid_part * (1.0 + first * (1.0 - sigmoid_part))
            second_grad = back * (first * sigmoid_part)
            places = pl.ds(pl.multiple_of(f * tile, tile), tile)
            grads[2 * e, :, places] = gate_grad.astype(jnp.bfloat16)
            grads[2 * e + 1, :, places] = second_grad.astype(jnp.bfloat16)

    @pl.loop(0, width // tile)
    def _(n):
        columns = pl.ds(pl.multiple_of(n * tile, tile), tile)
        total = None
        for e in range(2):
            for i, weight in enumerate((gate_w, up_w)):
                term = lax.dot_general(
                    grads[2 * e + i], weight[e, columns, :], NT, preferred_element_type=jnp.float32
                )
                total = term if total is None else total + term
        write_tiles(total, outs, columns)


def expert_call(kind, names, packed, rows, weights, experts):
    parts = len(rows)
    counts = [block.shape[0] for block in rows]
    total = sum(counts)
    width = rows[0].shape[1]
    full = packed[0].shape[1]
    inner = weights[0].shape[1]
    tile = 256
    hbm = pl.BlockSpec(memory_space=pl.ANY)
    weight_scratch = [
        pltpu.VMEM((2, width, inner), jnp.bfloat16),
        pltpu.VMEM((2, width, inner), jnp.bfloat16),
        pltpu.VMEM((2, inner, width), jnp.bfloat16),
    ]
    sems = [pltpu.SemaphoreType.DMA((parts,)), pltpu.SemaphoreType.DMA((parts,))]
    sems += [pltpu.SemaphoreType.DMA((6,))]
    if kind == "forward":
        body = forward_kernel
        scratch = [
            pltpu.VMEM((total, full - width), jnp.bfloat16),
            pltpu.VMEM((total, width), jnp.bfloat16),
            pltpu.VMEM((total, 2 * inner), jnp.bfloat16),
        ]
        products = 6
    else:
        body = backward_kernel
        scratch = [
            pltpu.VMEM((total, full), jnp.bfloat16),
            pltpu.VMEM((total, width), jnp.bfloat16),
            pltpu.VMEM((total, width), jnp.bfloat16),
            pltpu.VMEM((4, total, inner), jnp.bfloat16),
        ]
        products = 10
    out = pl.pallas_call(
        functools.partial(body, parts, experts, width, tile),
        out_shape=[jax.ShapeDtypeStruct((count, width), jnp.bfloat16) for count in counts],
        in_specs=[pl.BlockSpec(memory_space=pltpu.SMEM)] + [hbm] * (2 * parts + 6),
        scratch_shapes=scratch + weight_scratch + sems,
        compiler_params=pltpu.CompilerParams(vmem_limit_bytes=VMEM_LIMIT),
        cost_estimate=pl.CostEstimate(
            flops=2 * products * total * width * inner,
            bytes_accessed=12 * width * inner,
            transcendentals=2 * total * inner,
        ),
    )(names, *packed, *rows, *weights)
    return list(out)


class Ring:
    def __init__(self, sources):
        self.chips = sources // 2
        order = list(range(0, self.chips, 2)) + list(range(1, self.chips, 2))[::-1]
        following = {order[i]: order[(i + 1) % self.chips] for i in range(self.chips)}
        pairs = [(2 * a + core, 2 * b + core) for a, b in following.items() for core in range(2)]
        self.routes = (pairs, [(b, a) for a, b in pairs])
        self.swap = [(i, i ^ 1) for i in range(sources)]

    def pass_on(self, block, way):
        return lax.ppermute(block, "ep", self.routes[way])

    def gather(self, block):
        groups = [[block]]
        behind = ahead = block
        for _ in range(self.chips // 2 - 1):
            behind, ahead = self.pass_on(behind, 0), self.pass_on(ahead, 1)
            groups.append([behind, ahead])
        half = block.shape[0] // 2
        groups.append([self.pass_on(behind[:half], 0), self.pass_on(ahead[half:], 1)])
        return groups

    def scatter_sum(self, groups):
        half = groups[-1][0].shape[0]
        forth, back = self.pass_on(groups[-1][0], 0), self.pass_on(groups[-1][1], 1)
        for distance in range(self.chips // 2 - 1, 0, -1):
            behind, ahead = groups[distance]
            if distance == self.chips // 2 - 1:
                ahead = jnp.concatenate([added(ahead[:half], forth), ahead[half:]])
                behind = jnp.concatenate([behind[:half], added(behind[half:], back)])
            else:
                ahead, behind = added(ahead, forth), added(behind, back)
            forth, back = self.pass_on(ahead, 0), self.pass_on(behind, 1)
        return [piece.astype(jnp.float32) for piece in (groups[0][0], forth, back)]


def added(first, second):
    return (first.astype(jnp.float32) + second.astype(jnp.float32)).astype(jnp.bfloat16)


def run_groups(kind, names, packed, rows, weights, experts):
    first = expert_call(
        kind, names, packed[0] + packed[1], rows[0] + rows[1], weights, experts
    )
    made = [first[:1], first[1:]]
    for near, far in zip(packed[2:], rows[2:]):
        made.append(expert_call(kind, names, near, far, weights, experts))
    return made


def local(
    entering,
    rising_prev,
    falling_cot,
    falling_saved,
    targets,
    norm_gain,
    exit_gain,
    w_gate,
    w_up,
    w_down,
    route_ids,
    route_gates,
    exit_list,
):
    section_index = lax.axis_index("pipe")
    sections = lax.axis_size("pipe")
    sources = lax.axis_size("ep")
    here = lax.axis_index("ep")
    names = jnp.stack([here, here + 1 - 2 * (here % 2)]).astype(jnp.int32)
    norm_row = norm_gain[0]
    exit_row = exit_gain[0]
    ring = Ring(sources)

    packed = packed_rows(falling_saved[0], norm_gain, route_ids[:, 0], route_gates[:, 0], sources)
    all_packed = ring.gather(packed)
    moved_cot, moved_rise = passed_along((falling_cot[0], rising_prev[0]), "pipe", 1)
    own = (w_gate[0, 0], w_up[0, 0], w_down[0, 0])
    weights = own + tuple(lax.ppermute(own, "ep", ring.swap))

    at_start = section_index == 0
    cot_in = jnp.where(at_start, entering[1], moved_cot)
    all_cot = ring.gather(cot_in)
    rise_in = jnp.where(at_start, entering[0], moved_rise)
    rise_wide = rise_in.astype(jnp.float32)
    all_rise = ring.gather(normed(rise_wide, norm_row).astype(jnp.bfloat16))

    cotangent = cot_in.astype(jnp.float32)
    head_rise = jnp.take(exit_list[0], section_index).astype(jnp.float32)
    head_fall = jnp.take(exit_list[1], sections - 1 - section_index).astype(jnp.float32)
    fall_wide = falling_saved[0].astype(jnp.float32)

    made_fall = run_groups("backward", names, all_packed, all_cot, weights, sources)
    grad_parts = ring.scatter_sum(made_fall)
    norm_grad = grad_parts[0] + grad_parts[1] + grad_parts[2]
    made_rise = run_groups("forward", names, all_packed, all_rise, weights, sources)
    rise_parts = ring.scatter_sum(made_rise)
    layer_out = rise_wide + (rise_parts[0] + rise_parts[1] + rise_parts[2])

    rise_diff = normed(rise_wide, exit_row) - targets[0].astype(jnp.float32)
    loss_rise = head_rise * 0.5 * jnp.mean(rise_diff * rise_diff, axis=-1)
    fall_diff = normed(fall_wide, exit_row) - targets[1].astype(jnp.float32)
    fall_total = cotangent + norm_pullback(fall_wide, norm_row, norm_grad)
    fall_total = fall_total + head_fall * norm_pullback(fall_wide, exit_row, fall_diff)
    loss_fall = head_fall * 0.5 * jnp.mean(fall_diff * fall_diff, axis=-1)
    exit_loss = jnp.stack([loss_rise, loss_fall])[:, None, :]
    return (layer_out.astype(jnp.bfloat16)[None], fall_total.astype(jnp.bfloat16)[None], exit_loss)


def solution(mesh):
    placed = (
        P(None, "ep", None),
        P("pipe", "ep", None),
        P("pipe", "ep", None),
        P("pipe", "ep", None),
        P(None, "ep", None),
        P("pipe", None),
        P("pipe", None),
        P("pipe", "ep", None, None),
        P("pipe", "ep", None, None),
        P("pipe", "ep", None, None),
        P(None, "pipe", "ep", None),
        P(None, "pipe", "ep", None),
        P(),
    )
    return jax.shard_map(
        local,
        mesh=mesh,
        in_specs=placed,
        out_specs=(P("pipe", "ep", None), P("pipe", "ep", None), P(None, "pipe", "ep")),
        check_vma=False,
    )
```

```python
import functools
import jax
import jax.numpy as jnp
from jax import lax
from jax.experimental import pallas as pl
from jax.experimental.pallas import tpu as pltpu
from jax.sharding import PartitionSpec as P

EPSILON = 1e-06
VMEM_LIMIT = 56 * 1024 * 1024
NT = (((1,), (1,)), ((), ()))


def passed_along(block, axis, distance):
    devices = range(lax.axis_size(axis))
    route = [(i - distance, i) for i in devices if i - distance in devices]
    return lax.ppermute(block, axis, route)


def normed(values, gain_row):
    return (
        values * lax.rsqrt(jnp.mean(values * values, axis=-1, keepdims=True) + EPSILON) * gain_row
    )


def norm_pullback(values, gain_row, upstream):
    _, pullback = jax.vjp(lambda argument: normed(argument, gain_row), values)
    return pullback(upstream)[0]


def pack_kernel(experts, rows_ref, ids_ref, gates_ref, out_ref):
    width = rows_ref.shape[1]
    out_ref[:, :width] = rows_ref[...]
    count, extra = rows_ref.shape[0], out_ref.shape[1] - width
    lane = lax.broadcasted_iota(jnp.int32, (count, extra), 1)
    table = jnp.zeros((count, extra), jnp.float32)
    for m in range(2):
        for k in range(ids_ref.shape[2]):
            place = ids_ref[m, :, k : k + 1] + 2 * m * experts
            gate = gates_ref[m, :, k : k + 1]
            high = gate.astype(jnp.bfloat16).astype(jnp.float32)
            table = jnp.where(lane == place, high, table)
            table = jnp.where(lane == place + experts, gate - high, table)
    out_ref[:, width:] = table.astype(jnp.bfloat16)


def packed_rows(rows, ids, gates, experts):
    count, width = rows.shape
    extra = -(-4 * experts // 128) * 128
    return pl.pallas_call(
        functools.partial(pack_kernel, experts),
        out_shape=jax.ShapeDtypeStruct((count, width + extra), jnp.bfloat16),
        compiler_params=pltpu.CompilerParams(vmem_limit_bytes=VMEM_LIMIT // 4),
        cost_estimate=pl.CostEstimate(flops=0, bytes_accessed=count * width * 8, transcendentals=0),
    )(rows, ids, gates)


def gate_column(table, micro, experts, expert):
    lane = lax.broadcasted_iota(jnp.int32, table.shape, 1)
    place = 2 * micro * experts + expert
    chosen = (lane == place) | (lane == place + experts)
    return jnp.sum(jnp.where(chosen, table, 0.0), axis=1, keepdims=True)


def start_all(copies):
    for copy in copies:
        copy.start()


def wait_all(copies):
    for copy in copies:
        copy.wait()


def block_copies(sources, target, sems, columns=None):
    copies, start = [], 0
    for i, source in enumerate(sources):
        count = source.shape[0]
        view = source if columns is None else source.at[:, columns]
        copies.append(
            pltpu.make_async_copy(view, target.at[pl.ds(start, count)], sems.at[i])
        )
        start += count
    return copies


def write_tiles(tile, outs, columns):
    start = 0
    for out in outs:
        count = out.shape[0]
        out[:, columns] = tile[start : start + count].astype(out.dtype)
        start += count


def weight_stages(weights, targets, sems, tile, with_down):
    inner = targets[0].shape[2]
    per = inner // tile
    stages, used = [], 0
    for e in range(2):
        for f in range(per):
            part = pl.ds(f * tile, tile)
            views = [(i, (slice(None), part)) for i in range(2)]
            if with_down:
                views.append((2, (part, slice(None))))
            copies = []
            for i, view in views:
                source, target = weights[3 * e + i], targets[i].at[e]
                copies.append(
                    pltpu.make_async_copy(source.at[view], target.at[view], sems.at[used])
                )
                used += 1
            stages.append(copies)
    return stages, used


def forward_kernel(parts, experts, width, tile, names_ref, *refs):
    packed, rows = refs[:parts], refs[parts : 2 * parts]
    weights = refs[2 * parts : 2 * parts + 6]
    outs = refs[2 * parts + 6 : 3 * parts + 6]
    (table, held, hidden, gate_w, up_w, down_w, table_sem, row_sem, weight_sem) = refs[
        3 * parts + 6 :
    ]
    extra = table.shape[1]
    inner = gate_w.shape[2]
    first_copies = block_copies(rows, held, row_sem)
    first_copies += block_copies(packed, table, table_sem, pl.ds(width, extra))
    stages, used = weight_stages(weights, (gate_w, up_w, down_w), weight_sem, tile, False)
    down_copies = [
        pltpu.make_async_copy(weights[3 * e + 2], down_w.at[e], weight_sem.at[used + e])
        for e in range(2)
    ]
    stages.append(down_copies)
    start_all(first_copies + stages[0] + stages[1])
    wait_all(first_copies)
    per = inner // tile
    for stage in range(2 * per):
        e, f = divmod(stage, per)
        wait_all(stages[stage])
        if stage + 2 < len(stages):
            start_all(stages[stage + 2])
        columns = pl.ds(f * tile, tile)
        gate = gate_column(table[...].astype(jnp.float32), 0, experts, names_ref[e])
        first = jnp.dot(held[...], gate_w[e, :, columns], preferred_element_type=jnp.float32)
        second = jnp.dot(held[...], up_w[e, :, columns], preferred_element_type=jnp.float32)
        made = gate * (jax.nn.silu(first) * second)
        hidden[:, pl.ds(stage * tile, tile)] = made.astype(jnp.bfloat16)
    wait_all(down_copies)

    @pl.loop(0, width // tile)
    def _(n):
        columns = pl.ds(pl.multiple_of(n * tile, tile), tile)
        total = jnp.dot(
            hidden[:, :inner], down_w[0, :, columns], preferred_element_type=jnp.float32
        ) + jnp.dot(hidden[:, inner:], down_w[1, :, columns], preferred_element_type=jnp.float32)
        write_tiles(total, outs, columns)


def backward_kernel(parts, experts, width, tile, names_ref, *refs):
    packed, rows = refs[:parts], refs[parts : 2 * parts]
    weights = refs[2 * parts : 2 * parts + 6]
    outs = refs[2 * parts + 6 : 3 * parts + 6]
    (cot, held, slot, grads, gate_w, up_w, down_w, cot_sem, row_sem, weight_sem) = refs[
        3 * parts + 6 :
    ]
    inner = gate_w.shape[2]
    first_copies = block_copies(rows, held, row_sem) + block_copies(packed, cot, cot_sem)
    stages, _ = weight_stages(weights, (gate_w, up_w, down_w), weight_sem, tile, True)
    start_all(first_copies + stages[0] + stages[1])
    wait_all(first_copies)
    per = inner // tile
    for stage in range(2 * per):
        e, f = divmod(stage, per)
        if f == 0:
            table = cot[:, width:].astype(jnp.float32)
            gate = gate_column(table, 1, experts, names_ref[e])
            slot[...] = (gate * cot[:, :width].astype(jnp.float32)).astype(jnp.bfloat16)
        wait_all(stages[stage])
        if stage + 2 < len(stages):
            start_all(stages[stage + 2])
        columns = pl.ds(f * tile, tile)
        first = jnp.dot(held[...], gate_w[e, :, columns], preferred_element_type=jnp.float32)
        second = jnp.dot(held[...], up_w[e, :, columns], preferred_element_type=jnp.float32)
        back = lax.dot_general(
            slot[...], down_w[e, columns, :], NT, preferred_element_type=jnp.float32
        )
        sigmoid_part = jax.nn.sigmoid(first)
        gate_grad = back * second * sigmoid_part * (1.0 + first * (1.0 - sigmoid_part))
        second_grad = back * (first * sigmoid_part)
        grads[2 * e, :, columns] = gate_grad.astype(jnp.bfloat16)
        grads[2 * e + 1, :, columns] = second_grad.astype(jnp.bfloat16)

    @pl.loop(0, width // tile)
    def _(n):
        columns = pl.ds(pl.multiple_of(n * tile, tile), tile)
        total = None
        for e in range(2):
            for i, weight in enumerate((gate_w, up_w)):
                term = lax.dot_general(
                    grads[2 * e + i], weight[e, columns, :], NT, preferred_element_type=jnp.float32
                )
                total = term if total is None else total + term
        write_tiles(total, outs, columns)


def expert_call(kind, names, packed, rows, weights, experts):
    parts = len(rows)
    counts = [block.shape[0] for block in rows]
    total = sum(counts)
    width = rows[0].shape[1]
    full = packed[0].shape[1]
    inner = weights[0].shape[1]
    tile = 256
    hbm = pl.BlockSpec(memory_space=pl.ANY)
    weight_scratch = [
        pltpu.VMEM((2, width, inner), jnp.bfloat16),
        pltpu.VMEM((2, width, inner), jnp.bfloat16),
        pltpu.VMEM((2, inner, width), jnp.bfloat16),
    ]
    sems = [pltpu.SemaphoreType.DMA((parts,)), pltpu.SemaphoreType.DMA((parts,))]
    sems += [pltpu.SemaphoreType.DMA((6 * (inner // tile),))]
    if kind == "forward":
        body = forward_kernel
        scratch = [
            pltpu.VMEM((total, full - width), jnp.bfloat16),
            pltpu.VMEM((total, width), jnp.bfloat16),
            pltpu.VMEM((total, 2 * inner), jnp.bfloat16),
        ]
        products, fixed = 6, 8.5e-6
    else:
        body = backward_kernel
        scratch = [
            pltpu.VMEM((total, full), jnp.bfloat16),
            pltpu.VMEM((total, width), jnp.bfloat16),
            pltpu.VMEM((total, width), jnp.bfloat16),
            pltpu.VMEM((4, total, inner), jnp.bfloat16),
        ]
        products, fixed = 10, 11e-6
    out = pl.pallas_call(
        functools.partial(body, parts, experts, width, tile),
        out_shape=[jax.ShapeDtypeStruct((count, width), jnp.bfloat16) for count in counts],
        in_specs=[pl.BlockSpec(memory_space=pltpu.SMEM)] + [hbm] * (2 * parts + 6),
        scratch_shapes=scratch + weight_scratch + sems,
        compiler_params=pltpu.CompilerParams(vmem_limit_bytes=VMEM_LIMIT),
        cost_estimate=pl.CostEstimate(
            flops=2 * products * total * width * inner + int(fixed * 1.1e15),
            bytes_accessed=12 * width * inner,
            transcendentals=2 * total * inner,
        ),
    )(names, *packed, *rows, *weights)
    return list(out)


def added(first, second):
    return (first.astype(jnp.float32) + second.astype(jnp.float32)).astype(jnp.bfloat16)


class Section:
    def __init__(self, sources, names):
        self.sources = sources
        self.names = names
        self.chips = sources // 2
        self.far = self.chips // 2
        order = list(range(0, self.chips, 2)) + list(range(1, self.chips, 2))[::-1]
        following = {order[i]: order[(i + 1) % self.chips] for i in range(self.chips)}
        pairs = [(2 * a + core, 2 * b + core) for a, b in following.items() for core in range(2)]
        self.routes = (pairs, [(b, a) for a, b in pairs])
        self.swap = [(i, i ^ 1) for i in range(sources)]
        self.held, self.made, self.sums, self.weights = {}, {}, {}, None

    def pass_on(self, block, way):
        return lax.ppermute(block, "ep", self.routes[way])

    def gather(self, name, distance):
        held = self.held[name]
        behind, ahead = held[distance - 1][0], held[distance - 1][-1]
        if distance == self.far:
            half = behind.shape[0] // 2
            behind, ahead = behind[:half], ahead[half:]
        held[distance] = [self.pass_on(behind, 0), self.pass_on(ahead, 1)]

    def work(self, kind, distances):
        rows = self.held["fall" if kind == "backward" else "rise"]
        packed = [block for d in distances for block in self.held["cot"][d]]
        blocks = [block for d in distances for block in rows[d]]
        outs = expert_call(kind, self.names, packed, blocks, self.weights, self.sources)
        made = self.made.setdefault(kind, {})
        for d in distances:
            count = len(rows[d])
            made[d], outs = outs[:count], outs[count:]

    def scatter(self, kind, step):
        distance = self.far + 1 - step
        behind, ahead = self.made[kind][distance]
        if step == 1:
            forth, back = behind, ahead
        else:
            moved_forth, moved_back = self.sums[kind]
            if step == 2:
                half = moved_forth.shape[0]
                forth = jnp.concatenate([added(ahead[:half], moved_forth), ahead[half:]])
                back = jnp.concatenate([behind[:half], added(behind[half:], moved_back)])
            else:
                forth, back = added(ahead, moved_forth), added(behind, moved_back)
        self.sums[kind] = [self.pass_on(forth, 0), self.pass_on(back, 1)]
        del self.made[kind][distance]

    def total(self, kind):
        pieces = self.made[kind][0] + self.sums[kind]
        return sum(piece.astype(jnp.float32) for piece in pieces)

    def fence(self, *others):
        state = (self.held, self.made, self.sums, others)
        state = lax.optimization_barrier(state)
        self.held, self.made, self.sums, others = state
        return others

    def fence_weights(self):
        state = (self.held, self.weights)
        self.held, self.weights = lax.optimization_barrier(state)


def local(
    entering,
    rising_prev,
    falling_cot,
    falling_saved,
    targets,
    norm_gain,
    exit_gain,
    w_gate,
    w_up,
    w_down,
    route_ids,
    route_gates,
    exit_list,
):
    section_index = lax.axis_index("pipe")
    sections = lax.axis_size("pipe")
    sources = lax.axis_size("ep")
    here = lax.axis_index("ep")
    names = jnp.stack([here, here + 1 - 2 * (here % 2)]).astype(jnp.int32)
    norm_row = norm_gain[0]
    exit_row = exit_gain[0]
    ring = Section(sources, names)
    far = ring.far
    planned = far == 4

    fall_wide = falling_saved[0].astype(jnp.float32)
    fall_normal = normed(fall_wide, norm_row).astype(jnp.bfloat16)
    fall_normal, leaving_cot, leaving_rise = lax.optimization_barrier(
        (fall_normal, falling_cot[0], rising_prev[0])
    )
    ring.held["fall"] = {0: [fall_normal]}
    ring.gather("fall", 1)
    moved_cot = passed_along(leaving_cot, "pipe", 1)
    moved_rise = passed_along(leaving_rise, "pipe", 1)
    own = (w_gate[0, 0], w_up[0, 0], w_down[0, 0])
    ring.weights = own + tuple(lax.ppermute(own, "ep", ring.swap))

    at_start = section_index == 0
    cot_in = jnp.where(at_start, entering[1], moved_cot)
    rise_in = jnp.where(at_start, entering[0], moved_rise)
    rise_wide = rise_in.astype(jnp.float32)
    ring.held["cot"] = {0: [packed_rows(cot_in, route_ids[:, 0], route_gates[:, 0], sources)]}
    ring.held["rise"] = {}
    rise_normal = normed(rise_wide, norm_row).astype(jnp.bfloat16)

    def exit_heads(rise_in, cot_in):
        rise_wide = rise_in.astype(jnp.float32)
        head_rise = jnp.take(exit_list[0], section_index).astype(jnp.float32)
        head_fall = jnp.take(exit_list[1], sections - 1 - section_index).astype(jnp.float32)
        rise_diff = normed(rise_wide, exit_row) - targets[0].astype(jnp.float32)
        loss_rise = head_rise * 0.5 * jnp.mean(rise_diff * rise_diff, axis=-1)
        fall_diff = normed(fall_wide, exit_row) - targets[1].astype(jnp.float32)
        loss_fall = head_fall * 0.5 * jnp.mean(fall_diff * fall_diff, axis=-1)
        kept = cot_in.astype(jnp.float32)
        kept = kept + head_fall * norm_pullback(fall_wide, exit_row, fall_diff)
        return kept, jnp.stack([loss_rise, loss_fall])[:, None, :]

    def falling(kept):
        return kept + norm_pullback(fall_wide, norm_row, ring.total("backward"))

    if planned:
        (cot_in,) = ring.fence(cot_in)
        ring.gather("fall", 2)
        ring.gather("cot", 1)
        ring.fence_weights()
        ring.gather("fall", 3)
        ring.gather("cot", 2)
        kept, exit_loss = exit_heads(rise_in, cot_in)
        rise_normal, kept, exit_loss = ring.fence(rise_normal, kept, exit_loss)
        ring.held["rise"] = {0: [rise_normal]}
        ring.gather("fall", 4)
        ring.gather("cot", 3)
        ring.gather("rise", 1)
        ring.work("backward", [0, 1, 2])
        ring.fence()
        ring.gather("cot", 4)
        ring.gather("rise", 2)
        ring.work("forward", [0, 1])
        ring.fence()
        ring.gather("rise", 3)
        ring.work("backward", [3, 4])
        ring.fence()
        ring.gather("rise", 4)
        ring.scatter("backward", 1)
        ring.fence()
        ring.scatter("backward", 2)
        ring.work("forward", [2, 3, 4])
        ring.fence()
        ring.scatter("backward", 3)
        ring.scatter("forward", 1)
        ring.fence()
        ring.scatter("backward", 4)
        ring.scatter("forward", 2)
        ring.fence()
        ring.scatter("forward", 3)
        fall_total = falling(kept).astype(jnp.bfloat16)
        (fall_total,) = ring.fence(fall_total)
        ring.scatter("forward", 4)
    else:
        kept, exit_loss = exit_heads(rise_in, cot_in)
        ring.held["rise"] = {0: [rise_normal]}
        for name in ("fall", "cot", "rise"):
            for distance in range(1 if name != "fall" else 2, far + 1):
                ring.gather(name, distance)
        for kind in ("backward", "forward"):
            ring.work(kind, [0, 1])
            for distance in range(2, far + 1):
                ring.work(kind, [distance])
            for step in range(1, far + 1):
                ring.scatter(kind, step)
        fall_total = falling(kept).astype(jnp.bfloat16)
    layer_out = (rise_wide + ring.total("forward")).astype(jnp.bfloat16)
    return (layer_out[None], fall_total[None], exit_loss)


def solution(mesh):
    placed = (
        P(None, "ep", None),
        P("pipe", "ep", None),
        P("pipe", "ep", None),
        P("pipe", "ep", None),
        P(None, "ep", None),
        P("pipe", None),
        P("pipe", None),
        P("pipe", "ep", None, None),
        P("pipe", "ep", None, None),
        P("pipe", "ep", None, None),
        P(None, "pipe", "ep", None),
        P(None, "pipe", "ep", None),
        P(),
    )
    return jax.shard_map(
        local,
        mesh=mesh,
        in_specs=placed,
        out_specs=(P("pipe", "ep", None), P("pipe", "ep", None), P(None, "pipe", "ep")),
        check_vma=False,
    )
```

```python
import functools
import jax
import jax.numpy as jnp
from jax import lax
from jax.experimental import pallas as pl
from jax.experimental.pallas import tpu as pltpu
from jax.sharding import PartitionSpec as P

EPSILON = 1e-06
VMEM_LIMIT = 56 * 1024 * 1024
NT = (((1,), (1,)), ((), ()))


def passed_along(block, axis, distance):
    devices = range(lax.axis_size(axis))
    route = [(i - distance, i) for i in devices if i - distance in devices]
    return lax.ppermute(block, axis, route)


def normed(values, gain_row):
    return (
        values * lax.rsqrt(jnp.mean(values * values, axis=-1, keepdims=True) + EPSILON) * gain_row
    )


def norm_pullback(values, gain_row, upstream):
    _, pullback = jax.vjp(lambda argument: normed(argument, gain_row), values)
    return pullback(upstream)[0]


def pack_kernel(experts, rows_ref, ids_ref, gates_ref, out_ref):
    width = rows_ref.shape[1]
    out_ref[:, :width] = rows_ref[...]
    count, extra = rows_ref.shape[0], out_ref.shape[1] - width
    lane = lax.broadcasted_iota(jnp.int32, (count, extra), 1)
    table = jnp.zeros((count, extra), jnp.float32)
    for m in range(2):
        for k in range(ids_ref.shape[2]):
            place = ids_ref[m, :, k : k + 1] + 2 * m * experts
            gate = gates_ref[m, :, k : k + 1]
            high = gate.astype(jnp.bfloat16).astype(jnp.float32)
            table = jnp.where(lane == place, high, table)
            table = jnp.where(lane == place + experts, gate - high, table)
    out_ref[:, width:] = table.astype(jnp.bfloat16)


def packed_rows(rows, ids, gates, experts):
    count, width = rows.shape
    extra = -(-4 * experts // 128) * 128
    return pl.pallas_call(
        functools.partial(pack_kernel, experts),
        out_shape=jax.ShapeDtypeStruct((count, width + extra), jnp.bfloat16),
        compiler_params=pltpu.CompilerParams(vmem_limit_bytes=VMEM_LIMIT // 4),
        cost_estimate=pl.CostEstimate(flops=0, bytes_accessed=count * width * 8, transcendentals=0),
    )(rows, ids, gates)


def gate_column(table, micro, experts, expert):
    lane = lax.broadcasted_iota(jnp.int32, table.shape, 1)
    place = 2 * micro * experts + expert
    chosen = (lane == place) | (lane == place + experts)
    return jnp.sum(jnp.where(chosen, table, 0.0), axis=1, keepdims=True)


def start_all(copies):
    for copy in copies:
        copy.start()


def wait_all(copies):
    for copy in copies:
        copy.wait()


def block_copies(sources, target, sems, columns=None):
    copies, start = [], 0
    for i, source in enumerate(sources):
        count = source.shape[0]
        view = source if columns is None else source.at[:, columns]
        copies.append(
            pltpu.make_async_copy(view, target.at[pl.ds(start, count)], sems.at[i])
        )
        start += count
    return copies


def write_tiles(tile, outs, columns):
    start = 0
    for out in outs:
        count = out.shape[0]
        out[:, columns] = tile[start : start + count].astype(out.dtype)
        start += count


def weight_stages(weights, targets, sems, tile, with_down):
    inner = targets[0].shape[2]
    per = inner // tile
    stages, used = [], 0
    for e in range(2):
        for f in range(per):
            part = pl.ds(f * tile, tile)
            views = [(i, (slice(None), part)) for i in range(2)]
            if with_down:
                views.append((2, (part, slice(None))))
            copies = []
            for i, view in views:
                source, target = weights[3 * e + i], targets[i].at[e]
                copies.append(
                    pltpu.make_async_copy(source.at[view], target.at[view], sems.at[used])
                )
                used += 1
            stages.append(copies)
    return stages, used


def forward_kernel(parts, experts, width, tile, names_ref, *refs):
    packed, rows = refs[:parts], refs[parts : 2 * parts]
    weights = refs[2 * parts : 2 * parts + 6]
    outs = refs[2 * parts + 6 : 3 * parts + 6]
    (table, held, hidden, gate_w, up_w, down_w, table_sem, row_sem, weight_sem) = refs[
        3 * parts + 6 :
    ]
    extra = table.shape[1]
    inner = gate_w.shape[2]
    first_copies = block_copies(rows, held, row_sem)
    first_copies += block_copies(packed, table, table_sem, pl.ds(width, extra))
    stages, used = weight_stages(weights, (gate_w, up_w, down_w), weight_sem, tile, False)
    down_copies = [
        pltpu.make_async_copy(weights[3 * e + 2], down_w.at[e], weight_sem.at[used + e])
        for e in range(2)
    ]
    stages.append(down_copies)
    start_all(first_copies + stages[0] + stages[1])
    wait_all(first_copies)
    per = inner // tile
    for stage in range(2 * per):
        e, f = divmod(stage, per)
        wait_all(stages[stage])
        if stage + 2 < len(stages):
            start_all(stages[stage + 2])
        columns = pl.ds(f * tile, tile)
        gate = gate_column(table[...].astype(jnp.float32), 0, experts, names_ref[e])
        first = jnp.dot(held[...], gate_w[e, :, columns], preferred_element_type=jnp.float32)
        second = jnp.dot(held[...], up_w[e, :, columns], preferred_element_type=jnp.float32)
        made = gate * (jax.nn.silu(first) * second)
        hidden[:, pl.ds(stage * tile, tile)] = made.astype(jnp.bfloat16)
    wait_all(down_copies)

    @pl.loop(0, width // tile)
    def _(n):
        columns = pl.ds(pl.multiple_of(n * tile, tile), tile)
        total = jnp.dot(
            hidden[:, :inner], down_w[0, :, columns], preferred_element_type=jnp.float32
        ) + jnp.dot(hidden[:, inner:], down_w[1, :, columns], preferred_element_type=jnp.float32)
        write_tiles(total, outs, columns)


def backward_kernel(parts, experts, width, tile, names_ref, *refs):
    packed, rows = refs[:parts], refs[parts : 2 * parts]
    weights = refs[2 * parts : 2 * parts + 6]
    outs = refs[2 * parts + 6 : 3 * parts + 6]
    (cot, held, slot, grads, gate_w, up_w, down_w, cot_sem, row_sem, weight_sem) = refs[
        3 * parts + 6 :
    ]
    inner = gate_w.shape[2]
    first_copies = block_copies(rows, held, row_sem) + block_copies(packed, cot, cot_sem)
    stages, _ = weight_stages(weights, (gate_w, up_w, down_w), weight_sem, tile, True)
    start_all(first_copies + stages[0] + stages[1])
    wait_all(first_copies)
    per = inner // tile
    for stage in range(2 * per):
        e, f = divmod(stage, per)
        if f == 0:
            table = cot[:, width:].astype(jnp.float32)
            gate = gate_column(table, 1, experts, names_ref[e])
            slot[...] = (gate * cot[:, :width].astype(jnp.float32)).astype(jnp.bfloat16)
        wait_all(stages[stage])
        if stage + 2 < len(stages):
            start_all(stages[stage + 2])
        columns = pl.ds(f * tile, tile)
        first = jnp.dot(held[...], gate_w[e, :, columns], preferred_element_type=jnp.float32)
        second = jnp.dot(held[...], up_w[e, :, columns], preferred_element_type=jnp.float32)
        back = lax.dot_general(
            slot[...], down_w[e, columns, :], NT, preferred_element_type=jnp.float32
        )
        sigmoid_part = jax.nn.sigmoid(first)
        gate_grad = back * second * sigmoid_part * (1.0 + first * (1.0 - sigmoid_part))
        second_grad = back * (first * sigmoid_part)
        grads[2 * e, :, columns] = gate_grad.astype(jnp.bfloat16)
        grads[2 * e + 1, :, columns] = second_grad.astype(jnp.bfloat16)

    @pl.loop(0, width // tile)
    def _(n):
        columns = pl.ds(pl.multiple_of(n * tile, tile), tile)
        total = None
        for e in range(2):
            for i, weight in enumerate((gate_w, up_w)):
                term = lax.dot_general(
                    grads[2 * e + i], weight[e, columns, :], NT, preferred_element_type=jnp.float32
                )
                total = term if total is None else total + term
        write_tiles(total, outs, columns)


def expert_call(kind, names, packed, rows, weights, experts):
    parts = len(rows)
    counts = [block.shape[0] for block in rows]
    total = sum(counts)
    width = rows[0].shape[1]
    full = packed[0].shape[1]
    inner = weights[0].shape[1]
    tile = 256
    hbm = pl.BlockSpec(memory_space=pl.ANY)
    weight_scratch = [
        pltpu.VMEM((2, width, inner), jnp.bfloat16),
        pltpu.VMEM((2, width, inner), jnp.bfloat16),
        pltpu.VMEM((2, inner, width), jnp.bfloat16),
    ]
    sems = [pltpu.SemaphoreType.DMA((parts,)), pltpu.SemaphoreType.DMA((parts,))]
    sems += [pltpu.SemaphoreType.DMA((6 * (inner // tile),))]
    if kind == "forward":
        body = forward_kernel
        scratch = [
            pltpu.VMEM((total, full - width), jnp.bfloat16),
            pltpu.VMEM((total, width), jnp.bfloat16),
            pltpu.VMEM((total, 2 * inner), jnp.bfloat16),
        ]
        products, fixed = 6, 8.5e-6
    else:
        body = backward_kernel
        scratch = [
            pltpu.VMEM((total, full), jnp.bfloat16),
            pltpu.VMEM((total, width), jnp.bfloat16),
            pltpu.VMEM((total, width), jnp.bfloat16),
            pltpu.VMEM((4, total, inner), jnp.bfloat16),
        ]
        products, fixed = 10, 11e-6
    out = pl.pallas_call(
        functools.partial(body, parts, experts, width, tile),
        out_shape=[jax.ShapeDtypeStruct((count, width), jnp.bfloat16) for count in counts],
        in_specs=[pl.BlockSpec(memory_space=pltpu.SMEM)] + [hbm] * (2 * parts + 6),
        scratch_shapes=scratch + weight_scratch + sems,
        compiler_params=pltpu.CompilerParams(vmem_limit_bytes=VMEM_LIMIT),
        cost_estimate=pl.CostEstimate(
            flops=2 * products * total * width * inner + int(fixed * 1.1e15),
            bytes_accessed=12 * width * inner,
            transcendentals=2 * total * inner,
        ),
    )(names, *packed, *rows, *weights)
    return list(out)


def added(first, second):
    return (first.astype(jnp.float32) + second.astype(jnp.float32)).astype(jnp.bfloat16)


def joined(block, moved, way):
    if moved is None:
        return block
    half = moved.shape[0]
    if half == block.shape[0]:
        return added(block, moved)
    if way == 0:
        return jnp.concatenate([added(block[:half], moved), block[half:]])
    return jnp.concatenate([block[:half], added(block[half:], moved)])


class Section:
    def __init__(self, sources, names):
        self.sources = sources
        self.names = names
        self.chips = sources // 2
        self.far = self.chips // 2
        order = list(range(0, self.chips, 2)) + list(range(1, self.chips, 2))[::-1]
        following = {order[i]: order[(i + 1) % self.chips] for i in range(self.chips)}
        pairs = [(2 * a + core, 2 * b + core) for a, b in following.items() for core in range(2)]
        self.routes = (pairs, [(b, a) for a, b in pairs])
        self.swap = [(i, i ^ 1) for i in range(sources)]
        self.held, self.made, self.sums, self.weights = {}, {}, {}, None

    def pass_on(self, block, way):
        return lax.ppermute(block, "ep", self.routes[way])

    def gather(self, name, distance, way=None):
        held = self.held[name]
        behind, ahead = held[distance - 1][0], held[distance - 1][-1]
        if distance == self.far and way is not None:
            held[distance] = [self.pass_on((behind, ahead)[way], way)]
            return
        if distance == self.far:
            half = behind.shape[0] // 2
            behind, ahead = behind[:half], ahead[half:]
        held[distance] = [self.pass_on(behind, 0), self.pass_on(ahead, 1)]

    def work(self, kind, distances):
        rows = self.held["fall" if kind == "backward" else "rise"]
        packed = [block for d in distances for block in self.held["cot"][d]]
        blocks = [block for d in distances for block in rows[d]]
        outs = expert_call(kind, self.names, packed, blocks, self.weights, self.sources)
        made = self.made.setdefault(kind, {})
        for d in distances:
            count = len(rows[d])
            made[d], outs = outs[:count], outs[count:]

    def scatter(self, kind, step, way=None):
        distance = self.far + 1 - step
        pieces = self.made[kind].pop(distance)
        if step == 1 and len(pieces) == 1:
            half = pieces[0].shape[0] // 2
            if way is None:
                pieces = [pieces[0][:half], pieces[0][half:]]
            else:
                pieces = [pieces[0] if way == i else None for i in range(2)]
        elif step > 1:
            moved = self.sums[kind]
            pieces = [joined(pieces[1 - i], moved[i], i) for i in range(2)]
        self.sums[kind] = [
            None if piece is None else self.pass_on(piece, i) for i, piece in enumerate(pieces)
        ]

    def total(self, kind):
        pieces = self.made[kind][0] + self.sums[kind]
        return sum(piece.astype(jnp.float32) for piece in pieces)

    def fence(self, *others):
        state = (self.held, self.made, self.sums, others)
        state = lax.optimization_barrier(state)
        self.held, self.made, self.sums, others = state
        return others


def local(
    entering,
    rising_prev,
    falling_cot,
    falling_saved,
    targets,
    norm_gain,
    exit_gain,
    w_gate,
    w_up,
    w_down,
    route_ids,
    route_gates,
    exit_list,
):
    section_index = lax.axis_index("pipe")
    sections = lax.axis_size("pipe")
    sources = lax.axis_size("ep")
    here = lax.axis_index("ep")
    names = jnp.stack([here, here + 1 - 2 * (here % 2)]).astype(jnp.int32)
    norm_row = norm_gain[0]
    exit_row = exit_gain[0]
    ring = Section(sources, names)
    far = ring.far
    planned = far == 4

    fall_wide = falling_saved[0].astype(jnp.float32)
    fall_normal = normed(fall_wide, norm_row).astype(jnp.bfloat16)
    fall_normal, leaving_cot, leaving_rise = lax.optimization_barrier(
        (fall_normal, falling_cot[0], rising_prev[0])
    )
    ring.held["fall"] = {0: [fall_normal]}
    ring.gather("fall", 1)
    moved_cot = passed_along(leaving_cot, "pipe", 1)
    moved_rise = passed_along(leaving_rise, "pipe", 1)
    own = (w_gate[0, 0], w_up[0, 0], w_down[0, 0])

    def swapped(weight):
        return lax.ppermute(weight, "ep", ring.swap)

    at_start = section_index == 0
    cot_in = jnp.where(at_start, entering[1], moved_cot)
    rise_in = jnp.where(at_start, entering[0], moved_rise)
    ring.held["cot"] = {0: [packed_rows(cot_in, route_ids[:, 0], route_gates[:, 0], sources)]}
    ring.held["rise"] = {}

    head_rise = jnp.take(exit_list[0], section_index).astype(jnp.float32)
    head_fall = jnp.take(exit_list[1], sections - 1 - section_index).astype(jnp.float32)

    def exit_heads(rise_in, cot_in, head_rise, head_fall):
        rise_wide = rise_in.astype(jnp.float32)
        rise_diff = normed(rise_wide, exit_row) - targets[0].astype(jnp.float32)
        loss_rise = head_rise * 0.5 * jnp.mean(rise_diff * rise_diff, axis=-1)
        fall_diff = normed(fall_wide, exit_row) - targets[1].astype(jnp.float32)
        loss_fall = head_fall * 0.5 * jnp.mean(fall_diff * fall_diff, axis=-1)
        kept = cot_in.astype(jnp.float32)
        kept = kept + head_fall * norm_pullback(fall_wide, exit_row, fall_diff)
        return kept, jnp.stack([loss_rise, loss_fall])[:, None, :]

    def falling(kept):
        return kept + norm_pullback(fall_wide, norm_row, ring.total("backward"))

    if planned:
        own_gate, own_up, own_down = own
        other_down = swapped(own_down)
        cot_in, rise_in, own_gate, own_up, other_down = ring.fence(
            cot_in, rise_in, own_gate, own_up, other_down
        )
        heads, ring.names = lax.optimization_barrier(((head_rise, head_fall), names))
        ring.gather("fall", 2)
        ring.gather("cot", 1)
        other_gate = swapped(own_gate)
        rise_normal = normed(rise_in.astype(jnp.float32), norm_row).astype(jnp.bfloat16)
        rise_normal, own_up, other_gate, heads, ring.names = ring.fence(
            rise_normal, own_up, other_gate, heads, ring.names
        )
        ring.gather("fall", 3)
        ring.gather("cot", 2)
        other_up = swapped(own_up)
        kept, exit_loss = exit_heads(rise_in, cot_in, *heads)
        kept, exit_loss, other_up = ring.fence(kept, exit_loss, other_up)
        ring.weights = own + (other_gate, other_up, other_down)
        ring.held["rise"] = {0: [rise_normal]}
        ring.gather("cot", 3)
        ring.gather("rise", 1)
        ring.work("backward", [0, 1])
        ring.fence()
        ring.gather("fall", 4, 0)
        ring.gather("cot", 4, 1)
        ring.gather("rise", 2)
        ring.work("backward", [2, 3])
        ring.fence()
        ring.gather("rise", 3)
        ring.work("backward", [4])
        ring.fence()
        ring.gather("rise", 4, 0)
        ring.scatter("backward", 1, 1)
        ring.work("forward", [0, 1, 2])
        ring.fence()
        ring.scatter("backward", 2)
        ring.work("forward", [3, 4])
        ring.fence()
        ring.scatter("backward", 3)
        ring.scatter("forward", 1)
        ring.fence()
        ring.scatter("backward", 4)
        ring.scatter("forward", 2)
        ring.fence()
        ring.scatter("forward", 3)
        fall_total = falling(kept).astype(jnp.bfloat16)
        (fall_total,) = ring.fence(fall_total)
        ring.scatter("forward", 4)
    else:
        ring.weights = own + tuple(swapped(own))
        kept, exit_loss = exit_heads(rise_in, cot_in, head_rise, head_fall)
        rise_normal = normed(rise_in.astype(jnp.float32), norm_row).astype(jnp.bfloat16)
        ring.held["rise"] = {0: [rise_normal]}
        for name in ("fall", "cot", "rise"):
            for distance in range(1 if name != "fall" else 2, far + 1):
                ring.gather(name, distance)
        for kind in ("backward", "forward"):
            ring.work(kind, [0, 1])
            for distance in range(2, far + 1):
                ring.work(kind, [distance])
            for step in range(1, far + 1):
                ring.scatter(kind, step)
        fall_total = falling(kept).astype(jnp.bfloat16)
    layer_out = (rise_in.astype(jnp.float32) + ring.total("forward")).astype(jnp.bfloat16)
    return (layer_out[None], fall_total[None], exit_loss)


def solution(mesh):
    placed = (
        P(None, "ep", None),
        P("pipe", "ep", None),
        P("pipe", "ep", None),
        P("pipe", "ep", None),
        P(None, "ep", None),
        P("pipe", None),
        P("pipe", None),
        P("pipe", "ep", None, None),
        P("pipe", "ep", None, None),
        P("pipe", "ep", None, None),
        P(None, "pipe", "ep", None),
        P(None, "pipe", "ep", None),
        P(),
    )
    return jax.shard_map(
        local,
        mesh=mesh,
        in_specs=placed,
        out_specs=(P("pipe", "ep", None), P("pipe", "ep", None), P(None, "pipe", "ep")),
        check_vma=False,
    )
```

```python
import functools
import jax
import jax.numpy as jnp
from jax import lax
from jax.experimental import pallas as pl
from jax.experimental.pallas import tpu as pltpu
from jax.sharding import PartitionSpec as P

EPSILON = 1e-06
VMEM_LIMIT = 56 * 1024 * 1024
NT = (((1,), (1,)), ((), ()))


def passed_along(block, axis, distance):
    devices = range(lax.axis_size(axis))
    route = [(i - distance, i) for i in devices if i - distance in devices]
    return lax.ppermute(block, axis, route)


def normed(values, gain_row):
    return (
        values * lax.rsqrt(jnp.mean(values * values, axis=-1, keepdims=True) + EPSILON) * gain_row
    )


def norm_pullback(values, gain_row, upstream):
    _, pullback = jax.vjp(lambda argument: normed(argument, gain_row), values)
    return pullback(upstream)[0]


def pack_kernel(experts, rows_ref, ids_ref, gates_ref, out_ref):
    width = rows_ref.shape[1]
    out_ref[:, :width] = rows_ref[...]
    count, extra = rows_ref.shape[0], out_ref.shape[1] - width
    lane = lax.broadcasted_iota(jnp.int32, (count, extra), 1)
    table = jnp.zeros((count, extra), jnp.float32)
    for m in range(2):
        for k in range(ids_ref.shape[2]):
            place = ids_ref[m, :, k : k + 1] + 2 * m * experts
            gate = gates_ref[m, :, k : k + 1]
            high = gate.astype(jnp.bfloat16).astype(jnp.float32)
            table = jnp.where(lane == place, high, table)
            table = jnp.where(lane == place + experts, gate - high, table)
    out_ref[:, width:] = table.astype(jnp.bfloat16)


def packed_rows(rows, ids, gates, experts):
    count, width = rows.shape
    extra = -(-4 * experts // 128) * 128
    return pl.pallas_call(
        functools.partial(pack_kernel, experts),
        out_shape=jax.ShapeDtypeStruct((count, width + extra), jnp.bfloat16),
        compiler_params=pltpu.CompilerParams(vmem_limit_bytes=VMEM_LIMIT // 4),
        cost_estimate=pl.CostEstimate(flops=0, bytes_accessed=count * width * 8, transcendentals=0),
    )(rows, ids, gates)


def gate_column(table, micro, experts, expert):
    lane = lax.broadcasted_iota(jnp.int32, table.shape, 1)
    place = 2 * micro * experts + expert
    chosen = (lane == place) | (lane == place + experts)
    return jnp.sum(jnp.where(chosen, table, 0.0), axis=1, keepdims=True)


def start_all(copies):
    for copy in copies:
        copy.start()


def wait_all(copies):
    for copy in copies:
        copy.wait()


def block_copies(sources, target, sems, columns=None):
    copies, start = [], 0
    for i, source in enumerate(sources):
        count = source.shape[0]
        view = source if columns is None else source.at[:, columns]
        copies.append(
            pltpu.make_async_copy(view, target.at[pl.ds(start, count)], sems.at[i])
        )
        start += count
    return copies


def write_tiles(tile, outs, columns):
    start = 0
    for out in outs:
        count = out.shape[0]
        out[:, columns] = tile[start : start + count].astype(out.dtype)
        start += count


def in_order(copies):
    start_all(copies[:2])

    def arrived(i):
        copies[i].wait()
        if i + 2 < len(copies):
            copies[i + 2].start()

    return arrived


def matrix_copies(weights, targets, sems):
    return [
        pltpu.make_async_copy(weight, target, sems.at[i])
        for i, (weight, target) in enumerate(zip(weights, targets))
    ]


def dot(first, second):
    return jnp.dot(first, second, preferred_element_type=jnp.float32)


def dot_nt(first, second):
    return lax.dot_general(first, second, NT, preferred_element_type=jnp.float32)


def forward_kernel(parts, experts, width, tile, names_ref, *refs):
    packed, rows = refs[:parts], refs[parts : 2 * parts]
    weights = refs[2 * parts : 2 * parts + 6]
    outs = refs[2 * parts + 6 : 3 * parts + 6]
    (table, held, hidden, gate_w, up_w, down_w, table_sem, row_sem, weight_sem) = refs[
        3 * parts + 6 :
    ]
    extra = table.shape[1]
    inner = gate_w.shape[2]
    first_copies = block_copies(rows, held, row_sem)
    first_copies += block_copies(packed, table, table_sem, pl.ds(width, extra))
    start_all(first_copies)
    order = [(0, gate_w, 0), (1, up_w, 0), (3, gate_w, 1), (4, up_w, 1), (2, down_w, 0)]
    order += [(5, down_w, 1)]
    arrived = in_order(
        matrix_copies(
            [weights[i] for i, _, _ in order], [ref.at[e] for _, ref, e in order], weight_sem
        )
    )
    wait_all(first_copies)
    for e in range(2):
        gate = gate_column(table[...].astype(jnp.float32), 0, experts, names_ref[e])
        arrived(2 * e)
        first = dot(held[...], gate_w[e])
        arrived(2 * e + 1)
        second = dot(held[...], up_w[e])
        made = gate * (jax.nn.silu(first) * second)
        hidden[:, pl.ds(e * inner, inner)] = made.astype(jnp.bfloat16)
    arrived(4)
    arrived(5)

    @pl.loop(0, width // tile)
    def _(n):
        columns = pl.ds(pl.multiple_of(n * tile, tile), tile)
        total = dot(hidden[:, :inner], down_w[0, :, columns])
        total = total + dot(hidden[:, inner:], down_w[1, :, columns])
        write_tiles(total, outs, columns)


def factor_kernel(parts, *refs):
    rows, weights, out = refs[:parts], refs[parts : parts + 4], refs[parts + 4]
    held, gate_w, up_w, row_sem, weight_sem = refs[parts + 5 :]
    first_copies = block_copies(rows, held, row_sem)
    start_all(first_copies)
    targets = [gate_w.at[0], up_w.at[0], gate_w.at[1], up_w.at[1]]
    arrived = in_order(matrix_copies(weights, targets, weight_sem))
    wait_all(first_copies)
    for e in range(2):
        arrived(2 * e)
        first = dot(held[...], gate_w[e])
        arrived(2 * e + 1)
        second = dot(held[...], up_w[e])
        sigmoid_part = jax.nn.sigmoid(first)
        out[2 * e] = (
            second * sigmoid_part * (1.0 + first * (1.0 - sigmoid_part))
        ).astype(jnp.bfloat16)
        out[2 * e + 1] = (first * sigmoid_part).astype(jnp.bfloat16)


def backward_kernel(parts, experts, width, tile, start, names_ref, *refs):
    packed, factors = refs[:parts], refs[parts]
    weights = refs[parts + 1 : parts + 7]
    outs = refs[parts + 7 : 2 * parts + 7]
    (cot, slot, grads, gate_w, up_w, down_w, cot_sem, factor_sem, weight_sem) = refs[
        2 * parts + 7 :
    ]
    total_rows = slot.shape[0]
    first_copies = block_copies(packed, cot, cot_sem)
    start_all(first_copies)
    order = [(2, down_w, 0), (5, down_w, 1), (0, gate_w, 0), (1, up_w, 0), (3, gate_w, 1)]
    order += [(4, up_w, 1)]
    arrived = in_order(
        matrix_copies(
            [weights[i] for i, _, _ in order], [ref.at[e] for _, ref, e in order], weight_sem
        )
    )
    factor_copy = pltpu.make_async_copy(
        factors.at[:, pl.ds(start, total_rows)], grads, factor_sem
    )
    factor_copy.start()
    wait_all(first_copies)
    for e in range(2):
        table = cot[:, width:].astype(jnp.float32)
        gate = gate_column(table, 1, experts, names_ref[e])
        slot[...] = (gate * cot[:, :width].astype(jnp.float32)).astype(jnp.bfloat16)
        arrived(e)
        back = dot_nt(slot[...], down_w[e])
        if e == 0:
            factor_copy.wait()
        for i in range(2):
            made = back * grads[2 * e + i].astype(jnp.float32)
            grads[2 * e + i] = made.astype(jnp.bfloat16)
    for i in range(2, 6):
        arrived(i)

    @pl.loop(0, width // tile)
    def _(n):
        columns = pl.ds(pl.multiple_of(n * tile, tile), tile)
        total = None
        for e in range(2):
            for i, weight in enumerate((gate_w, up_w)):
                term = dot_nt(grads[2 * e + i], weight[e, columns, :])
                total = term if total is None else total + term
        write_tiles(total, outs, columns)


HBM = pl.BlockSpec(memory_space=pl.ANY)
TILE = 512


def weight_scratch(width, inner, with_down=True):
    shapes = [(2, width, inner), (2, width, inner), (2, inner, width)]
    return [pltpu.VMEM(shape, jnp.bfloat16) for shape in shapes[: 3 if with_down else 2]]


def cost(units, rows, width, inner, fixed):
    return pl.CostEstimate(
        flops=2 * units * rows * width * inner + int(fixed * 1.1e15),
        bytes_accessed=12 * width * inner,
        transcendentals=2 * rows * inner,
    )


PARAMS = pltpu.CompilerParams(vmem_limit_bytes=VMEM_LIMIT)


def forward_call(names, packed, rows, weights, experts):
    parts = len(rows)
    counts = [block.shape[0] for block in rows]
    total, width = sum(counts), rows[0].shape[1]
    full, inner = packed[0].shape[1], weights[0].shape[1]
    out = pl.pallas_call(
        functools.partial(forward_kernel, parts, experts, width, TILE),
        out_shape=[jax.ShapeDtypeStruct((count, width), jnp.bfloat16) for count in counts],
        in_specs=[pl.BlockSpec(memory_space=pltpu.SMEM)] + [HBM] * (2 * parts + 6),
        scratch_shapes=[
            pltpu.VMEM((total, full - width), jnp.bfloat16),
            pltpu.VMEM((total, width), jnp.bfloat16),
            pltpu.VMEM((total, 2 * inner), jnp.bfloat16),
        ]
        + weight_scratch(width, inner)
        + [pltpu.SemaphoreType.DMA((count,)) for count in (parts, parts, 6)],
        compiler_params=PARAMS,
        cost_estimate=cost(6, total, width, inner, 6e-6),
    )(names, *packed, *rows, *weights)
    return list(out)


def factor_call(rows, weights):
    parts = len(rows)
    total, width = sum(block.shape[0] for block in rows), rows[0].shape[1]
    inner = weights[0].shape[1]
    return pl.pallas_call(
        functools.partial(factor_kernel, parts),
        out_shape=jax.ShapeDtypeStruct((4, total, inner), jnp.bfloat16),
        in_specs=[HBM] * (parts + 4),
        scratch_shapes=[pltpu.VMEM((total, width), jnp.bfloat16)]
        + weight_scratch(width, inner, False)
        + [pltpu.SemaphoreType.DMA((count,)) for count in (parts, 4)],
        compiler_params=PARAMS,
        cost_estimate=cost(4, total, width, inner, 5e-6),
    )(*rows, weights[0], weights[1], weights[3], weights[4])


def backward_call(names, packed, factors, start, weights, experts):
    parts = len(packed)
    counts = [block.shape[0] for block in packed]
    total, full = sum(counts), packed[0].shape[1]
    width, inner = weights[0].shape
    out = pl.pallas_call(
        functools.partial(backward_kernel, parts, experts, width, TILE, start),
        out_shape=[jax.ShapeDtypeStruct((count, width), jnp.bfloat16) for count in counts],
        in_specs=[pl.BlockSpec(memory_space=pltpu.SMEM)] + [HBM] * (parts + 7),
        scratch_shapes=[
            pltpu.VMEM((total, full), jnp.bfloat16),
            pltpu.VMEM((total, width), jnp.bfloat16),
            pltpu.VMEM((4, total, inner), jnp.bfloat16),
        ]
        + weight_scratch(width, inner)
        + [
            pltpu.SemaphoreType.DMA((parts,)),
            pltpu.SemaphoreType.DMA(()),
            pltpu.SemaphoreType.DMA((6,)),
        ],
        compiler_params=PARAMS,
        cost_estimate=cost(6, total, width, inner, 6e-6),
    )(names, *packed, factors, *weights)
    return list(out)


def added(first, second):
    return (first.astype(jnp.float32) + second.astype(jnp.float32)).astype(jnp.bfloat16)


def joined(block, moved, way):
    if moved is None:
        return block
    half = moved.shape[0]
    if half == block.shape[0]:
        return added(block, moved)
    if way == 0:
        return jnp.concatenate([added(block[:half], moved), block[half:]])
    return jnp.concatenate([block[:half], added(block[half:], moved)])


class Section:
    def __init__(self, sources, names):
        self.sources = sources
        self.names = names
        self.chips = sources // 2
        self.far = self.chips // 2
        order = list(range(0, self.chips, 2)) + list(range(1, self.chips, 2))[::-1]
        following = {order[i]: order[(i + 1) % self.chips] for i in range(self.chips)}
        pairs = [(2 * a + core, 2 * b + core) for a, b in following.items() for core in range(2)]
        self.routes = (pairs, [(b, a) for a, b in pairs])
        self.swap = [(i, i ^ 1) for i in range(sources)]
        self.held, self.made, self.sums, self.starts = {}, {}, {}, {}
        self.weights = None

    def pass_on(self, block, way):
        return lax.ppermute(block, "ep", self.routes[way])

    def gather(self, name, distance, way=None):
        held = self.held[name]
        behind, ahead = held[distance - 1][0], held[distance - 1][-1]
        if distance == self.far and way is not None:
            held[distance] = [self.pass_on((behind, ahead)[way], way)]
            return
        if distance == self.far:
            half = behind.shape[0] // 2
            behind, ahead = behind[:half], ahead[half:]
        held[distance] = [self.pass_on(behind, 0), self.pass_on(ahead, 1)]

    def prepare(self, distances):
        blocks = [block for d in distances for block in self.held["fall"][d]]
        factors, start = factor_call(blocks, self.weights), 0
        for d in distances:
            self.held[f"factors{d}"] = {0: [factors]}
            self.starts[d] = start
            start += sum(block.shape[0] for block in self.held["fall"][d])

    def work(self, kind, distances):
        packed = [block for d in distances for block in self.held["cot"][d]]
        if kind == "backward":
            factors = self.held[f"factors{distances[0]}"][0][0]
            start = self.starts[distances[0]]
            outs = backward_call(
                self.names, packed, factors, start, self.weights, self.sources
            )
        else:
            blocks = [block for d in distances for block in self.held["rise"][d]]
            outs = forward_call(self.names, packed, blocks, self.weights, self.sources)
        made = self.made.setdefault(kind, {})
        for d in distances:
            count = len(self.held["cot"][d])
            made[d], outs = outs[:count], outs[count:]

    def scatter(self, kind, step, way=None):
        distance = self.far + 1 - step
        pieces = self.made[kind].pop(distance)
        if step == 1 and len(pieces) == 1:
            half = pieces[0].shape[0] // 2
            if way is None:
                pieces = [pieces[0][:half], pieces[0][half:]]
            else:
                pieces = [pieces[0] if way == i else None for i in range(2)]
        elif step > 1:
            moved = self.sums[kind]
            pieces = [joined(pieces[1 - i], moved[i], i) for i in range(2)]
        self.sums[kind] = [
            None if piece is None else self.pass_on(piece, i) for i, piece in enumerate(pieces)
        ]

    def total(self, kind):
        pieces = self.made[kind][0] + self.sums[kind]
        return sum(piece.astype(jnp.float32) for piece in pieces)

    def fence(self, *others):
        state = (self.held, self.made, self.sums, others)
        state = lax.optimization_barrier(state)
        self.held, self.made, self.sums, others = state
        return others


def local(
    entering,
    rising_prev,
    falling_cot,
    falling_saved,
    targets,
    norm_gain,
    exit_gain,
    w_gate,
    w_up,
    w_down,
    route_ids,
    route_gates,
    exit_list,
):
    section_index = lax.axis_index("pipe")
    sections = lax.axis_size("pipe")
    sources = lax.axis_size("ep")
    here = lax.axis_index("ep")
    names = jnp.stack([here, here + 1 - 2 * (here % 2)]).astype(jnp.int32)
    norm_row = norm_gain[0]
    exit_row = exit_gain[0]
    ring = Section(sources, names)
    far = ring.far
    planned = far == 4

    fall_wide = falling_saved[0].astype(jnp.float32)
    fall_normal = normed(fall_wide, norm_row).astype(jnp.bfloat16)
    fall_normal, leaving_cot, leaving_rise = lax.optimization_barrier(
        (fall_normal, falling_cot[0], rising_prev[0])
    )
    ring.held["fall"] = {0: [fall_normal]}
    ring.gather("fall", 1)
    moved_cot = passed_along(leaving_cot, "pipe", 1)
    own = (w_gate[0, 0], w_up[0, 0], w_down[0, 0])

    def swapped(weight):
        return lax.ppermute(weight, "ep", ring.swap)

    at_start = section_index == 0
    cot_in = jnp.where(at_start, entering[1], moved_cot)

    def entered(leaving_rise):
        moved_rise = passed_along(leaving_rise, "pipe", 1)
        return jnp.where(at_start, entering[0], moved_rise)

    ring.held["cot"] = {0: [packed_rows(cot_in, route_ids[:, 0], route_gates[:, 0], sources)]}
    ring.held["rise"] = {}

    head_rise = jnp.take(exit_list[0], section_index).astype(jnp.float32)
    head_fall = jnp.take(exit_list[1], sections - 1 - section_index).astype(jnp.float32)

    def exit_heads(rise_in, cot_in, head_rise, head_fall):
        rise_wide = rise_in.astype(jnp.float32)
        rise_diff = normed(rise_wide, exit_row) - targets[0].astype(jnp.float32)
        loss_rise = head_rise * 0.5 * jnp.mean(rise_diff * rise_diff, axis=-1)
        fall_diff = normed(fall_wide, exit_row) - targets[1].astype(jnp.float32)
        loss_fall = head_fall * 0.5 * jnp.mean(fall_diff * fall_diff, axis=-1)
        kept = cot_in.astype(jnp.float32)
        kept = kept + head_fall * norm_pullback(fall_wide, exit_row, fall_diff)
        return kept, jnp.stack([loss_rise, loss_fall])[:, None, :]

    def falling(kept):
        return kept + norm_pullback(fall_wide, norm_row, ring.total("backward"))

    if planned:
        ring.gather("fall", 2)
        own_gate, own_up, own_down = own
        other_gate = swapped(own_gate)
        heads = (head_rise, head_fall)
        cot_in, leaving_rise, own_up, own_down, other_gate, heads, ring.names = ring.fence(
            cot_in, leaving_rise, own_up, own_down, other_gate, heads, names
        )
        ring.gather("fall", 3)
        ring.gather("cot", 1)
        rise_in = entered(leaving_rise)
        rise_in, own_up, own_down = ring.fence(rise_in, own_up, own_down)
        ring.gather("fall", 4)
        ring.gather("cot", 2)
        other_up = swapped(own_up)
        rise_normal = normed(rise_in.astype(jnp.float32), norm_row).astype(jnp.bfloat16)
        kept, exit_loss = exit_heads(rise_in, cot_in, *heads)
        rise_normal, kept, exit_loss, other_up, own_down = ring.fence(
            rise_normal, kept, exit_loss, other_up, own_down
        )
        ring.held["rise"] = {0: [rise_normal]}
        ring.gather("cot", 3)
        ring.gather("rise", 1)
        other_down = swapped(own_down)
        ring.weights = own + (other_gate, other_up, other_down)
        ring.prepare([0, 1, 2, 3, 4])
        (other_down,) = ring.fence(other_down)
        ring.weights = own + (other_gate, other_up, other_down)
        ring.gather("cot", 4, 1)
        ring.gather("rise", 2)
        ring.work("backward", [0, 1, 2])
        ring.fence()
        ring.gather("rise", 3)
        ring.work("backward", [3, 4])
        ring.fence()
        ring.gather("rise", 4, 0)
        ring.scatter("backward", 1, 1)
        ring.work("forward", [0, 1, 2])
        ring.fence()
        ring.scatter("backward", 2)
        ring.work("forward", [3, 4])
        ring.fence()
        ring.scatter("backward", 3)
        ring.scatter("forward", 1)
        ring.fence()
        ring.scatter("backward", 4)
        ring.scatter("forward", 2)
        ring.fence()
        ring.scatter("forward", 3)
        fall_total = falling(kept).astype(jnp.bfloat16)
        (fall_total,) = ring.fence(fall_total)
        ring.scatter("forward", 4)
    else:
        rise_in = entered(leaving_rise)
        ring.weights = own + tuple(swapped(own))
        kept, exit_loss = exit_heads(rise_in, cot_in, head_rise, head_fall)
        rise_normal = normed(rise_in.astype(jnp.float32), norm_row).astype(jnp.bfloat16)
        ring.held["rise"] = {0: [rise_normal]}
        for name in ("fall", "cot", "rise"):
            for distance in range(1 if name != "fall" else 2, far + 1):
                ring.gather(name, distance)
        groups = [[0, 1]] + [[distance] for distance in range(2, far + 1)]
        for group in groups:
            ring.prepare(group)
            ring.work("backward", group)
        for group in groups:
            ring.work("forward", group)
        for kind in ("backward", "forward"):
            for step in range(1, far + 1):
                ring.scatter(kind, step)
        fall_total = falling(kept).astype(jnp.bfloat16)
    layer_out = (rise_in.astype(jnp.float32) + ring.total("forward")).astype(jnp.bfloat16)
    return (layer_out[None], fall_total[None], exit_loss)


def solution(mesh):
    placed = (
        P(None, "ep", None),
        P("pipe", "ep", None),
        P("pipe", "ep", None),
        P("pipe", "ep", None),
        P(None, "ep", None),
        P("pipe", None),
        P("pipe", None),
        P("pipe", "ep", None, None),
        P("pipe", "ep", None, None),
        P("pipe", "ep", None, None),
        P(None, "pipe", "ep", None),
        P(None, "pipe", "ep", None),
        P(),
    )
    return jax.shard_map(
        local,
        mesh=mesh,
        in_specs=placed,
        out_specs=(P("pipe", "ep", None), P("pipe", "ep", None), P(None, "pipe", "ep")),
        check_vma=False,
    )
```

```python
import functools
import jax
import jax.numpy as jnp
from jax import lax
from jax.experimental import pallas as pl
from jax.experimental.pallas import tpu as pltpu
from jax.sharding import PartitionSpec as P

EPSILON = 1e-06
VMEM_LIMIT = 24 * 1024 * 1024
NT = (((1,), (1,)), ((), ()))


def passed_along(block, axis, distance):
    devices = range(lax.axis_size(axis))
    route = [(i - distance, i) for i in devices if i - distance in devices]
    return lax.ppermute(block, axis, route)


def normed(values, gain_row):
    return (
        values * lax.rsqrt(jnp.mean(values * values, axis=-1, keepdims=True) + EPSILON) * gain_row
    )


def norm_pullback(values, gain_row, upstream):
    _, pullback = jax.vjp(lambda argument: normed(argument, gain_row), values)
    return pullback(upstream)[0]


def pack_kernel(experts, rows_ref, ids_ref, gates_ref, out_ref):
    width = rows_ref.shape[1]
    out_ref[:, :width] = rows_ref[...]
    count, extra = rows_ref.shape[0], out_ref.shape[1] - width
    lane = lax.broadcasted_iota(jnp.int32, (count, extra), 1)
    table = jnp.zeros((count, extra), jnp.float32)
    for m in range(2):
        for k in range(ids_ref.shape[2]):
            place = ids_ref[m, :, k : k + 1] + 2 * m * experts
            gate = gates_ref[m, :, k : k + 1]
            high = gate.astype(jnp.bfloat16).astype(jnp.float32)
            table = jnp.where(lane == place, high, table)
            table = jnp.where(lane == place + experts, gate - high, table)
    out_ref[:, width:] = table.astype(jnp.bfloat16)


def packed_rows(rows, ids, gates, experts):
    count, width = rows.shape
    extra = -(-4 * experts // 128) * 128
    return pl.pallas_call(
        functools.partial(pack_kernel, experts),
        out_shape=jax.ShapeDtypeStruct((count, width + extra), jnp.bfloat16),
        compiler_params=pltpu.CompilerParams(vmem_limit_bytes=VMEM_LIMIT),
        cost_estimate=pl.CostEstimate(flops=0, bytes_accessed=count * width * 8, transcendentals=0),
    )(rows, ids, gates)


def gate_column(table, micro, experts, expert):
    lane = lax.broadcasted_iota(jnp.int32, table.shape, 1)
    place = 2 * micro * experts + expert
    chosen = (lane == place) | (lane == place + experts)
    return jnp.sum(jnp.where(chosen, table, 0.0), axis=1, keepdims=True)


def start_all(copies):
    for copy in copies:
        copy.start()


def wait_all(copies):
    for copy in copies:
        copy.wait()


def block_copies(sources, target, sems, columns=None):
    copies, start = [], 0
    for i, source in enumerate(sources):
        count = source.shape[0]
        view = source if columns is None else source.at[:, columns]
        copies.append(
            pltpu.make_async_copy(view, target.at[pl.ds(start, count)], sems.at[i])
        )
        start += count
    return copies


def write_tiles(tile, outs, columns):
    start = 0
    for out in outs:
        count = out.shape[0]
        out[:, columns] = tile[start : start + count].astype(out.dtype)
        start += count


def dot(first, second):
    return jnp.dot(first, second, preferred_element_type=jnp.float32)


def dot_nt(first, second):
    return lax.dot_general(first, second, NT, preferred_element_type=jnp.float32)


def forward_kernel(parts, experts, width, tile, names_ref, *refs):
    packed, rows = refs[:parts], refs[parts : 2 * parts]
    weights = refs[2 * parts : 2 * parts + 6]
    outs = refs[2 * parts + 6 : 3 * parts + 6]
    table, held, hidden, table_sem, row_sem = refs[3 * parts + 6 :]
    extra = table.shape[1]
    inner = weights[0].shape[1]
    copies = block_copies(rows, held, row_sem)
    copies += block_copies(packed, table, table_sem, pl.ds(width, extra))
    start_all(copies)
    wait_all(copies)
    for e in range(2):
        gate = gate_column(table[...].astype(jnp.float32), 0, experts, names_ref[e])
        first = dot(held[...], weights[3 * e][...])
        second = dot(held[...], weights[3 * e + 1][...])
        made = gate * (jax.nn.silu(first) * second)
        hidden[:, pl.ds(e * inner, inner)] = made.astype(jnp.bfloat16)

    @pl.loop(0, width // tile)
    def _(n):
        columns = pl.ds(pl.multiple_of(n * tile, tile), tile)
        total = dot(hidden[:, :inner], weights[2][:, columns])
        total = total + dot(hidden[:, inner:], weights[5][:, columns])
        write_tiles(total, outs, columns)


def factor_kernel(parts, *refs):
    rows, weights, out = refs[:parts], refs[parts : parts + 4], refs[parts + 4]
    held, row_sem = refs[parts + 5 :]
    copies = block_copies(rows, held, row_sem)
    start_all(copies)
    wait_all(copies)
    for e in range(2):
        first = dot(held[...], weights[2 * e][...])
        second = dot(held[...], weights[2 * e + 1][...])
        sigmoid_part = jax.nn.sigmoid(first)
        out[2 * e] = (
            second * sigmoid_part * (1.0 + first * (1.0 - sigmoid_part))
        ).astype(jnp.bfloat16)
        out[2 * e + 1] = (first * sigmoid_part).astype(jnp.bfloat16)


def backward_kernel(parts, experts, width, tile, start, names_ref, *refs):
    packed, factors = refs[:parts], refs[parts]
    weights = refs[parts + 1 : parts + 7]
    outs = refs[parts + 7 : 2 * parts + 7]
    cot, slot, grads, cot_sem, factor_sem = refs[2 * parts + 7 :]
    copies = block_copies(packed, cot, cot_sem)
    factor_copy = pltpu.make_async_copy(
        factors.at[:, pl.ds(start, slot.shape[0])], grads, factor_sem
    )
    start_all(copies)
    factor_copy.start()
    wait_all(copies)
    for e in range(2):
        table = cot[:, width:].astype(jnp.float32)
        gate = gate_column(table, 1, experts, names_ref[e])
        slot[...] = (gate * cot[:, :width].astype(jnp.float32)).astype(jnp.bfloat16)
        back = dot_nt(slot[...], weights[3 * e + 2][...])
        if e == 0:
            factor_copy.wait()
        for i in range(2):
            made = back * grads[2 * e + i].astype(jnp.float32)
            grads[2 * e + i] = made.astype(jnp.bfloat16)

    @pl.loop(0, width // tile)
    def _(n):
        columns = pl.ds(pl.multiple_of(n * tile, tile), tile)
        total = None
        for e in range(2):
            for i in range(2):
                term = dot_nt(grads[2 * e + i], weights[3 * e + i][columns, :])
                total = term if total is None else total + term
        write_tiles(total, outs, columns)


HBM = pl.BlockSpec(memory_space=pl.ANY)
TILE = 512


WHOLE = pl.BlockSpec(memory_space=pltpu.VMEM)


def in_vmem(weights):
    return [pltpu.with_memory_space_constraint(weight, pltpu.VMEM) for weight in weights]


def cost(units, rows, width, inner, fixed):
    return pl.CostEstimate(
        flops=2 * units * rows * width * inner + int(fixed * 1.1e15),
        bytes_accessed=12 * width * inner,
        transcendentals=2 * rows * inner,
    )


PARAMS = pltpu.CompilerParams(vmem_limit_bytes=VMEM_LIMIT)


def forward_call(names, packed, rows, weights, experts):
    parts = len(rows)
    counts = [block.shape[0] for block in rows]
    total, width = sum(counts), rows[0].shape[1]
    full, inner = packed[0].shape[1], weights[0].shape[1]
    out = pl.pallas_call(
        functools.partial(forward_kernel, parts, experts, width, TILE),
        out_shape=[jax.ShapeDtypeStruct((count, width), jnp.bfloat16) for count in counts],
        in_specs=[pl.BlockSpec(memory_space=pltpu.SMEM)] + [HBM] * (2 * parts) + [WHOLE] * 6,
        scratch_shapes=[
            pltpu.VMEM((total, full - width), jnp.bfloat16),
            pltpu.VMEM((total, width), jnp.bfloat16),
            pltpu.VMEM((total, 2 * inner), jnp.bfloat16),
        ]
        + [pltpu.SemaphoreType.DMA((parts,)) for _ in range(2)],
        compiler_params=PARAMS,
        cost_estimate=cost(6, total, width, inner, 6e-6),
    )(names, *packed, *rows, *in_vmem(weights))
    return list(out)


def factor_call(rows, weights):
    parts = len(rows)
    total, width = sum(block.shape[0] for block in rows), rows[0].shape[1]
    inner = weights[0].shape[1]
    return pl.pallas_call(
        functools.partial(factor_kernel, parts),
        out_shape=jax.ShapeDtypeStruct((4, total, inner), jnp.bfloat16),
        in_specs=[HBM] * parts + [WHOLE] * 4,
        scratch_shapes=[
            pltpu.VMEM((total, width), jnp.bfloat16),
            pltpu.SemaphoreType.DMA((parts,)),
        ],
        compiler_params=PARAMS,
        cost_estimate=cost(4, total, width, inner, 5e-6),
    )(*rows, *in_vmem([weights[i] for i in (0, 1, 3, 4)]))


def backward_call(names, packed, factors, start, weights, experts):
    parts = len(packed)
    counts = [block.shape[0] for block in packed]
    total, full = sum(counts), packed[0].shape[1]
    width, inner = weights[0].shape
    out = pl.pallas_call(
        functools.partial(backward_kernel, parts, experts, width, TILE, start),
        out_shape=[jax.ShapeDtypeStruct((count, width), jnp.bfloat16) for count in counts],
        in_specs=[pl.BlockSpec(memory_space=pltpu.SMEM)] + [HBM] * (parts + 1) + [WHOLE] * 6,
        scratch_shapes=[
            pltpu.VMEM((total, full), jnp.bfloat16),
            pltpu.VMEM((total, width), jnp.bfloat16),
            pltpu.VMEM((4, total, inner), jnp.bfloat16),
            pltpu.SemaphoreType.DMA((parts,)),
            pltpu.SemaphoreType.DMA(()),
        ],
        compiler_params=PARAMS,
        cost_estimate=cost(6, total, width, inner, 6e-6),
    )(names, *packed, factors, *in_vmem(weights))
    return list(out)


def added(first, second):
    return (first.astype(jnp.float32) + second.astype(jnp.float32)).astype(jnp.bfloat16)


def joined(block, moved, way):
    if moved is None:
        return block
    half = moved.shape[0]
    if half == block.shape[0]:
        return added(block, moved)
    if way == 0:
        return jnp.concatenate([added(block[:half], moved), block[half:]])
    return jnp.concatenate([block[:half], added(block[half:], moved)])


class Section:
    def __init__(self, sources, names):
        self.sources = sources
        self.names = names
        self.chips = sources // 2
        self.far = self.chips // 2
        order = list(range(0, self.chips, 2)) + list(range(1, self.chips, 2))[::-1]
        following = {order[i]: order[(i + 1) % self.chips] for i in range(self.chips)}
        pairs = [(2 * a + core, 2 * b + core) for a, b in following.items() for core in range(2)]
        self.routes = (pairs, [(b, a) for a, b in pairs])
        self.swap = [(i, i ^ 1) for i in range(sources)]
        self.held, self.made, self.sums, self.starts = {}, {}, {}, {}
        self.weights = None

    def pass_on(self, block, way):
        return lax.ppermute(block, "ep", self.routes[way])

    def gather(self, name, distance, way=None):
        held = self.held[name]
        behind, ahead = held[distance - 1][0], held[distance - 1][-1]
        if distance == self.far and way is not None:
            held[distance] = [self.pass_on((behind, ahead)[way], way)]
            return
        if distance == self.far:
            half = behind.shape[0] // 2
            behind, ahead = behind[:half], ahead[half:]
        held[distance] = [self.pass_on(behind, 0), self.pass_on(ahead, 1)]

    def prepare(self, distances):
        blocks = [block for d in distances for block in self.held["fall"][d]]
        factors, start = factor_call(blocks, self.weights), 0
        for d in distances:
            self.held[f"factors{d}"] = {0: [factors]}
            self.starts[d] = start
            start += sum(block.shape[0] for block in self.held["fall"][d])

    def work(self, kind, distances):
        packed = [block for d in distances for block in self.held["cot"][d]]
        if kind == "backward":
            factors = self.held[f"factors{distances[0]}"][0][0]
            start = self.starts[distances[0]]
            outs = backward_call(
                self.names, packed, factors, start, self.weights, self.sources
            )
        else:
            blocks = [block for d in distances for block in self.held["rise"][d]]
            outs = forward_call(self.names, packed, blocks, self.weights, self.sources)
        made = self.made.setdefault(kind, {})
        for d in distances:
            count = len(self.held["cot"][d])
            made[d], outs = outs[:count], outs[count:]

    def scatter(self, kind, step, way=None):
        distance = self.far + 1 - step
        pieces = self.made[kind].pop(distance)
        if step == 1 and len(pieces) == 1:
            half = pieces[0].shape[0] // 2
            if way is None:
                pieces = [pieces[0][:half], pieces[0][half:]]
            else:
                pieces = [pieces[0] if way == i else None for i in range(2)]
        elif step > 1:
            moved = self.sums[kind]
            pieces = [joined(pieces[1 - i], moved[i], i) for i in range(2)]
        self.sums[kind] = [
            None if piece is None else self.pass_on(piece, i) for i, piece in enumerate(pieces)
        ]

    def total(self, kind):
        pieces = self.made[kind][0] + self.sums[kind]
        return sum(piece.astype(jnp.float32) for piece in pieces)

    def fence(self, *others):
        state = (self.held, self.made, self.sums, others)
        state = lax.optimization_barrier(state)
        self.held, self.made, self.sums, others = state
        return others


def local(
    entering,
    rising_prev,
    falling_cot,
    falling_saved,
    targets,
    norm_gain,
    exit_gain,
    w_gate,
    w_up,
    w_down,
    route_ids,
    route_gates,
    exit_list,
):
    section_index = lax.axis_index("pipe")
    sections = lax.axis_size("pipe")
    sources = lax.axis_size("ep")
    here = lax.axis_index("ep")
    names = jnp.stack([here, here + 1 - 2 * (here % 2)]).astype(jnp.int32)
    norm_row = norm_gain[0]
    exit_row = exit_gain[0]
    ring = Section(sources, names)
    far = ring.far
    planned = far == 4

    fall_wide = falling_saved[0].astype(jnp.float32)
    fall_normal = normed(fall_wide, norm_row).astype(jnp.bfloat16)
    fall_normal, leaving_cot, leaving_rise = lax.optimization_barrier(
        (fall_normal, falling_cot[0], rising_prev[0])
    )
    ring.held["fall"] = {0: [fall_normal]}
    ring.gather("fall", 1)
    moved_cot = passed_along(leaving_cot, "pipe", 1)
    moved_cot, leaving_rise = lax.optimization_barrier((moved_cot, leaving_rise))
    own = (w_gate[0, 0], w_up[0, 0], w_down[0, 0])

    def swapped(weight):
        return lax.ppermute(weight, "ep", ring.swap)

    at_start = section_index == 0
    cot_in = jnp.where(at_start, entering[1], moved_cot)

    def entered(leaving_rise):
        moved_rise = passed_along(leaving_rise, "pipe", 1)
        return jnp.where(at_start, entering[0], moved_rise)

    ring.held["cot"] = {0: [packed_rows(cot_in, route_ids[:, 0], route_gates[:, 0], sources)]}
    ring.held["rise"] = {}

    head_rise = jnp.take(exit_list[0], section_index).astype(jnp.float32)
    head_fall = jnp.take(exit_list[1], sections - 1 - section_index).astype(jnp.float32)

    def exit_heads(rise_in, cot_in, head_rise, head_fall):
        rise_wide = rise_in.astype(jnp.float32)
        rise_diff = normed(rise_wide, exit_row) - targets[0].astype(jnp.float32)
        loss_rise = head_rise * 0.5 * jnp.mean(rise_diff * rise_diff, axis=-1)
        fall_diff = normed(fall_wide, exit_row) - targets[1].astype(jnp.float32)
        loss_fall = head_fall * 0.5 * jnp.mean(fall_diff * fall_diff, axis=-1)
        kept = cot_in.astype(jnp.float32)
        kept = kept + head_fall * norm_pullback(fall_wide, exit_row, fall_diff)
        return kept, jnp.stack([loss_rise, loss_fall])[:, None, :]

    def falling(kept):
        return kept + norm_pullback(fall_wide, norm_row, ring.total("backward"))

    if planned:
        ring.gather("fall", 2)
        own_gate, own_up, own_down = own
        other_gate = swapped(own_gate)
        heads = (head_rise, head_fall)
        rise_in = entered(leaving_rise)
        cot_in, rise_in, own_up, own_down, other_gate, heads, ring.names = ring.fence(
            cot_in, rise_in, own_up, own_down, other_gate, heads, names
        )
        ring.gather("fall", 3)
        ring.gather("cot", 1)
        rise_normal = normed(rise_in.astype(jnp.float32), norm_row).astype(jnp.bfloat16)
        rise_normal, own_up, own_down = ring.fence(rise_normal, own_up, own_down)
        ring.gather("fall", 4)
        ring.gather("cot", 2)
        other_up = swapped(own_up)
        kept, exit_loss = exit_heads(rise_in, cot_in, *heads)
        rise_normal, kept, exit_loss, other_up, own_down = ring.fence(
            rise_normal, kept, exit_loss, other_up, own_down
        )
        ring.held["rise"] = {0: [rise_normal]}
        ring.gather("cot", 3)
        ring.gather("rise", 1)
        other_down = swapped(own_down)
        ring.weights = own + (other_gate, other_up, other_down)
        ring.prepare([0, 1, 2, 3, 4])
        (other_down,) = ring.fence(other_down)
        ring.weights = own + (other_gate, other_up, other_down)
        ring.gather("cot", 4, 1)
        ring.gather("rise", 2)
        ring.work("backward", [0, 1, 2])
        ring.fence()
        ring.gather("rise", 3)
        ring.work("backward", [3, 4])
        ring.fence()
        ring.gather("rise", 4, 0)
        ring.scatter("backward", 1, 1)
        ring.work("forward", [0, 1, 2])
        ring.fence()
        ring.scatter("backward", 2)
        ring.work("forward", [3, 4])
        ring.fence()
        ring.scatter("backward", 3)
        ring.scatter("forward", 1)
        ring.fence()
        ring.scatter("backward", 4)
        ring.scatter("forward", 2)
        ring.fence()
        ring.scatter("forward", 3)
        fall_total = falling(kept).astype(jnp.bfloat16)
        (fall_total,) = ring.fence(fall_total)
        ring.scatter("forward", 4)
    else:
        rise_in = entered(leaving_rise)
        ring.weights = own + tuple(swapped(own))
        kept, exit_loss = exit_heads(rise_in, cot_in, head_rise, head_fall)
        rise_normal = normed(rise_in.astype(jnp.float32), norm_row).astype(jnp.bfloat16)
        ring.held["rise"] = {0: [rise_normal]}
        for name in ("fall", "cot", "rise"):
            for distance in range(1 if name != "fall" else 2, far + 1):
                ring.gather(name, distance)
        groups = [[0, 1]] + [[distance] for distance in range(2, far + 1)]
        for group in groups:
            ring.prepare(group)
            ring.work("backward", group)
        for group in groups:
            ring.work("forward", group)
        for kind in ("backward", "forward"):
            for step in range(1, far + 1):
                ring.scatter(kind, step)
        fall_total = falling(kept).astype(jnp.bfloat16)
    layer_out = (rise_in.astype(jnp.float32) + ring.total("forward")).astype(jnp.bfloat16)
    return (layer_out[None], fall_total[None], exit_loss)


def solution(mesh):
    placed = (
        P(None, "ep", None),
        P("pipe", "ep", None),
        P("pipe", "ep", None),
        P("pipe", "ep", None),
        P(None, "ep", None),
        P("pipe", None),
        P("pipe", None),
        P("pipe", "ep", None, None),
        P("pipe", "ep", None, None),
        P("pipe", "ep", None, None),
        P(None, "pipe", "ep", None),
        P(None, "pipe", "ep", None),
        P(),
    )
    return jax.shard_map(
        local,
        mesh=mesh,
        in_specs=placed,
        out_specs=(P("pipe", "ep", None), P("pipe", "ep", None), P(None, "pipe", "ep")),
        check_vma=False,
    )
```

```python
import functools
import jax
import jax.numpy as jnp
from jax import lax
from jax.experimental import pallas as pl
from jax.experimental.pallas import tpu as pltpu
from jax.sharding import PartitionSpec as P

EPSILON = 1e-06
VMEM_LIMIT = 24 * 1024 * 1024
NT = (((1,), (1,)), ((), ()))


def passed_along(block, axis, distance):
    devices = range(lax.axis_size(axis))
    route = [(i - distance, i) for i in devices if i - distance in devices]
    return lax.ppermute(block, axis, route)


def normed(values, gain_row):
    return (
        values * lax.rsqrt(jnp.mean(values * values, axis=-1, keepdims=True) + EPSILON) * gain_row
    )


def norm_pullback(values, gain_row, upstream):
    _, pullback = jax.vjp(lambda argument: normed(argument, gain_row), values)
    return pullback(upstream)[0]


def pack_kernel(experts, rows_ref, ids_ref, gates_ref, out_ref):
    width = rows_ref.shape[1]
    out_ref[:, :width] = rows_ref[...]
    count, extra = rows_ref.shape[0], out_ref.shape[1] - width
    lane = lax.broadcasted_iota(jnp.int32, (count, extra), 1)
    table = jnp.zeros((count, extra), jnp.float32)
    for m in range(2):
        for k in range(ids_ref.shape[2]):
            place = ids_ref[m, :, k : k + 1] + 2 * m * experts
            gate = gates_ref[m, :, k : k + 1]
            high = gate.astype(jnp.bfloat16).astype(jnp.float32)
            table = jnp.where(lane == place, high, table)
            table = jnp.where(lane == place + experts, gate - high, table)
    out_ref[:, width:] = table.astype(jnp.bfloat16)


def packed_rows(rows, ids, gates, experts):
    count, width = rows.shape
    extra = -(-4 * experts // 128) * 128
    return pl.pallas_call(
        functools.partial(pack_kernel, experts),
        out_shape=jax.ShapeDtypeStruct((count, width + extra), jnp.bfloat16),
        compiler_params=pltpu.CompilerParams(vmem_limit_bytes=VMEM_LIMIT),
        cost_estimate=pl.CostEstimate(flops=0, bytes_accessed=count * width * 8, transcendentals=0),
    )(rows, ids, gates)


def gate_column(table, micro, experts, expert):
    lane = lax.broadcasted_iota(jnp.int32, table.shape, 1)
    place = 2 * micro * experts + expert
    chosen = (lane == place) | (lane == place + experts)
    return jnp.sum(jnp.where(chosen, table, 0.0), axis=1, keepdims=True)


def start_all(copies):
    for copy in copies:
        copy.start()


def wait_all(copies):
    for copy in copies:
        copy.wait()


def block_copies(sources, target, sems, columns=None):
    copies, start = [], 0
    for i, source in enumerate(sources):
        count = source.shape[0]
        view = source if columns is None else source.at[:, columns]
        copies.append(
            pltpu.make_async_copy(view, target.at[pl.ds(start, count)], sems.at[i])
        )
        start += count
    return copies


def write_tiles(tile, outs, columns):
    start = 0
    for out in outs:
        count = out.shape[0]
        out[:, columns] = tile[start : start + count].astype(out.dtype)
        start += count


def dot(first, second):
    return jnp.dot(first, second, preferred_element_type=jnp.float32)


def dot_nt(first, second):
    return lax.dot_general(first, second, NT, preferred_element_type=jnp.float32)


def forward_kernel(parts, experts, width, tile, names_ref, *refs):
    packed, rows = refs[:parts], refs[parts : 2 * parts]
    weights = refs[2 * parts : 2 * parts + 6]
    outs = refs[2 * parts + 6 : 3 * parts + 6]
    table, held, hidden, table_sem, row_sem = refs[3 * parts + 6 :]
    extra = table.shape[1]
    inner = weights[0].shape[1]
    copies = block_copies(rows, held, row_sem)
    copies += block_copies(packed, table, table_sem, pl.ds(width, extra))
    start_all(copies)
    wait_all(copies)
    for e in range(2):
        gate = gate_column(table[...].astype(jnp.float32), 0, experts, names_ref[e])
        first = dot(held[...], weights[3 * e][...])
        second = dot(held[...], weights[3 * e + 1][...])
        made = gate * (jax.nn.silu(first) * second)
        hidden[:, pl.ds(e * inner, inner)] = made.astype(jnp.bfloat16)

    @pl.loop(0, width // tile)
    def _(n):
        columns = pl.ds(pl.multiple_of(n * tile, tile), tile)
        total = dot(hidden[:, :inner], weights[2][:, columns])
        total = total + dot(hidden[:, inner:], weights[5][:, columns])
        write_tiles(total, outs, columns)


def factor_kernel(parts, *refs):
    rows, weights, out = refs[:parts], refs[parts : parts + 4], refs[parts + 4]
    held, row_sem = refs[parts + 5 :]
    copies = block_copies(rows, held, row_sem)
    start_all(copies)
    wait_all(copies)
    for e in range(2):
        first = dot(held[...], weights[2 * e][...])
        second = dot(held[...], weights[2 * e + 1][...])
        sigmoid_part = jax.nn.sigmoid(first)
        out[2 * e] = (
            second * sigmoid_part * (1.0 + first * (1.0 - sigmoid_part))
        ).astype(jnp.bfloat16)
        out[2 * e + 1] = (first * sigmoid_part).astype(jnp.bfloat16)


def backward_kernel(parts, experts, width, tile, pieces, names_ref, *refs):
    packed, factors = refs[:parts], refs[parts : parts + len(pieces)]
    weights = refs[parts + len(pieces) :][:6]
    outs = refs[parts + len(pieces) + 6 :][:parts]
    cot, slot, grads, cot_sem, factor_sem = refs[2 * parts + len(pieces) + 6 :]
    copies = block_copies(packed, cot, cot_sem)
    factor_copies, place = [], 0
    for i, (start, count) in enumerate(pieces):
        factor_copies.append(
            pltpu.make_async_copy(
                factors[i].at[:, pl.ds(start, count)],
                grads.at[:, pl.ds(place, count)],
                factor_sem.at[i],
            )
        )
        place += count
    start_all(copies + factor_copies)
    wait_all(copies)
    for e in range(2):
        table = cot[:, width:].astype(jnp.float32)
        gate = gate_column(table, 1, experts, names_ref[e])
        slot[...] = (gate * cot[:, :width].astype(jnp.float32)).astype(jnp.bfloat16)
        back = dot_nt(slot[...], weights[3 * e + 2][...])
        if e == 0:
            wait_all(factor_copies)
        for i in range(2):
            made = back * grads[2 * e + i].astype(jnp.float32)
            grads[2 * e + i] = made.astype(jnp.bfloat16)

    @pl.loop(0, width // tile)
    def _(n):
        columns = pl.ds(pl.multiple_of(n * tile, tile), tile)
        total = None
        for e in range(2):
            for i in range(2):
                term = dot_nt(grads[2 * e + i], weights[3 * e + i][columns, :])
                total = term if total is None else total + term
        write_tiles(total, outs, columns)


HBM = pl.BlockSpec(memory_space=pl.ANY)
TILE = 512


WHOLE = pl.BlockSpec(memory_space=pltpu.VMEM)


def in_vmem(weights):
    return [pltpu.with_memory_space_constraint(weight, pltpu.VMEM) for weight in weights]


def in_hbm(blocks):
    return [pltpu.with_memory_space_constraint(block, pltpu.HBM) for block in blocks]


def fetch_kernel(count, *refs):
    sems = refs[2 * count]
    copies = [
        pltpu.make_async_copy(refs[i], refs[count + i], sems.at[i]) for i in range(count)
    ]
    start_all(copies)
    wait_all(copies)


def fetched(weights):
    count = len(weights)
    return tuple(
        pl.pallas_call(
            functools.partial(fetch_kernel, count),
            out_shape=[pltpu.VMEM(weight.shape, weight.dtype) for weight in weights],
            in_specs=[HBM] * count,
            out_specs=[WHOLE] * count,
            scratch_shapes=[pltpu.SemaphoreType.DMA((count,))],
            compiler_params=PARAMS,
            cost_estimate=pl.CostEstimate(
                flops=0, bytes_accessed=8 * 2**20, transcendentals=0
            ),
        )(*weights)
    )


def cost(units, rows, width, inner, fixed):
    return pl.CostEstimate(
        flops=2 * units * rows * width * inner + int(fixed * 1.1e15),
        bytes_accessed=12 * width * inner,
        transcendentals=2 * rows * inner,
    )


PARAMS = pltpu.CompilerParams(vmem_limit_bytes=VMEM_LIMIT)


def forward_call(names, packed, rows, weights, experts):
    parts = len(rows)
    counts = [block.shape[0] for block in rows]
    total, width = sum(counts), rows[0].shape[1]
    full, inner = packed[0].shape[1], weights[0].shape[1]
    out = pl.pallas_call(
        functools.partial(forward_kernel, parts, experts, width, TILE),
        out_shape=[jax.ShapeDtypeStruct((count, width), jnp.bfloat16) for count in counts],
        in_specs=[pl.BlockSpec(memory_space=pltpu.SMEM)] + [HBM] * (2 * parts) + [WHOLE] * 6,
        scratch_shapes=[
            pltpu.VMEM((total, full - width), jnp.bfloat16),
            pltpu.VMEM((total, width), jnp.bfloat16),
            pltpu.VMEM((total, 2 * inner), jnp.bfloat16),
        ]
        + [pltpu.SemaphoreType.DMA((parts,)) for _ in range(2)],
        compiler_params=PARAMS,
        cost_estimate=cost(6, total, width, inner, 6e-6),
    )(names, *packed, *rows, *in_vmem(weights))
    return list(out)


def factor_call(rows, weights):
    parts = len(rows)
    total, width = sum(block.shape[0] for block in rows), rows[0].shape[1]
    inner = weights[0].shape[1]
    return pl.pallas_call(
        functools.partial(factor_kernel, parts),
        out_shape=jax.ShapeDtypeStruct((4, total, inner), jnp.bfloat16),
        in_specs=[HBM] * parts + [WHOLE] * 4,
        scratch_shapes=[
            pltpu.VMEM((total, width), jnp.bfloat16),
            pltpu.SemaphoreType.DMA((parts,)),
        ],
        compiler_params=PARAMS,
        cost_estimate=cost(4, total, width, inner, 5e-6),
    )(*in_hbm(rows), *in_vmem([weights[i] for i in (0, 1, 3, 4)]))


def backward_call(names, packed, factors, pieces, weights, experts):
    parts = len(packed)
    counts = [block.shape[0] for block in packed]
    total, full = sum(counts), packed[0].shape[1]
    width, inner = weights[0].shape
    out = pl.pallas_call(
        functools.partial(backward_kernel, parts, experts, width, TILE, pieces),
        out_shape=[jax.ShapeDtypeStruct((count, width), jnp.bfloat16) for count in counts],
        in_specs=[pl.BlockSpec(memory_space=pltpu.SMEM)] + [HBM] * (parts + len(pieces)) + [WHOLE] * 6,
        scratch_shapes=[
            pltpu.VMEM((total, full), jnp.bfloat16),
            pltpu.VMEM((total, width), jnp.bfloat16),
            pltpu.VMEM((4, total, inner), jnp.bfloat16),
            pltpu.SemaphoreType.DMA((parts,)),
            pltpu.SemaphoreType.DMA((len(pieces),)),
        ],
        compiler_params=PARAMS,
        cost_estimate=cost(6, total, width, inner, 6e-6),
    )(names, *packed, *factors, *in_vmem(weights))
    return list(out)


def added(first, second):
    return (first.astype(jnp.float32) + second.astype(jnp.float32)).astype(jnp.bfloat16)


def joined(block, moved, way):
    if moved is None:
        return block
    half = moved.shape[0]
    if half == block.shape[0]:
        return added(block, moved)
    if way == 0:
        return jnp.concatenate([added(block[:half], moved), block[half:]])
    return jnp.concatenate([block[:half], added(block[half:], moved)])


class Section:
    def __init__(self, sources, names):
        self.sources = sources
        self.names = names
        self.chips = sources // 2
        self.far = self.chips // 2
        order = list(range(0, self.chips, 2)) + list(range(1, self.chips, 2))[::-1]
        following = {order[i]: order[(i + 1) % self.chips] for i in range(self.chips)}
        pairs = [(2 * a + core, 2 * b + core) for a, b in following.items() for core in range(2)]
        self.routes = (pairs, [(b, a) for a, b in pairs])
        self.swap = [(i, i ^ 1) for i in range(sources)]
        self.held, self.made, self.sums, self.starts = {}, {}, {}, {}
        self.weights = None

    def pass_on(self, block, way):
        return lax.ppermute(block, "ep", self.routes[way])

    def gather(self, name, distance, way=None):
        held = self.held[name]
        behind, ahead = held[distance - 1][0], held[distance - 1][-1]
        if distance == self.far and way is not None:
            held[distance] = [self.pass_on((behind, ahead)[way], way)]
            return
        if distance == self.far:
            half = behind.shape[0] // 2
            behind, ahead = behind[:half], ahead[half:]
        held[distance] = [self.pass_on(behind, 0), self.pass_on(ahead, 1)]

    def prepare(self, distances):
        blocks = [block for d in distances for block in self.held["fall"][d]]
        key, start = f"factors{distances[0]}", 0
        self.held[key] = {0: [factor_call(blocks, self.weights)]}
        for d in distances:
            count = sum(block.shape[0] for block in self.held["fall"][d])
            self.starts[d] = (key, start, count)
            start += count

    def work(self, kind, distances):
        packed = [block for d in distances for block in self.held["cot"][d]]
        if kind == "backward":
            runs = []
            for key, start, count in [self.starts[d] for d in distances]:
                if runs and runs[-1][0] == key and sum(runs[-1][1:]) == start:
                    runs[-1][2] += count
                else:
                    runs.append([key, start, count])
            factors = [self.held[key][0][0] for key, _, _ in runs]
            pieces = tuple((start, count) for _, start, count in runs)
            outs = backward_call(
                self.names, packed, factors, pieces, self.weights, self.sources
            )
        else:
            blocks = [block for d in distances for block in self.held["rise"][d]]
            outs = forward_call(self.names, packed, blocks, self.weights, self.sources)
        made = self.made.setdefault(kind, {})
        for d in distances:
            count = len(self.held["cot"][d])
            made[d], outs = outs[:count], outs[count:]

    def scatter(self, kind, step, way=None):
        distance = self.far + 1 - step
        pieces = self.made[kind].pop(distance)
        if step == 1 and len(pieces) == 1:
            half = pieces[0].shape[0] // 2
            if way is None:
                pieces = [pieces[0][:half], pieces[0][half:]]
            else:
                pieces = [pieces[0] if way == i else None for i in range(2)]
        elif step > 1:
            moved = self.sums[kind]
            pieces = [joined(pieces[1 - i], moved[i], i) for i in range(2)]
        self.sums[kind] = [
            None if piece is None else self.pass_on(piece, i) for i, piece in enumerate(pieces)
        ]

    def total(self, kind):
        pieces = self.made[kind][0] + self.sums[kind]
        return sum(piece.astype(jnp.float32) for piece in pieces)

    def fence(self, *others):
        state = (self.held, self.made, self.sums, others)
        state = lax.optimization_barrier(state)
        self.held, self.made, self.sums, others = state
        return others


def local(
    entering,
    rising_prev,
    falling_cot,
    falling_saved,
    targets,
    norm_gain,
    exit_gain,
    w_gate,
    w_up,
    w_down,
    route_ids,
    route_gates,
    exit_list,
):
    section_index = lax.axis_index("pipe")
    sections = lax.axis_size("pipe")
    sources = lax.axis_size("ep")
    here = lax.axis_index("ep")
    names = jnp.stack([here, here + 1 - 2 * (here % 2)]).astype(jnp.int32)
    norm_row = norm_gain[0]
    exit_row = exit_gain[0]
    ring = Section(sources, names)
    far = ring.far
    planned = far == 4

    fall_wide = falling_saved[0].astype(jnp.float32)
    fall_normal = normed(fall_wide, norm_row).astype(jnp.bfloat16)
    fall_normal, leaving_cot, leaving_rise = lax.optimization_barrier(
        (fall_normal, falling_cot[0], rising_prev[0])
    )
    ring.held["fall"] = {0: [fall_normal]}
    ring.gather("fall", 1)
    moved_cot = passed_along(leaving_cot, "pipe", 1)
    own = (w_gate[0, 0], w_up[0, 0], w_down[0, 0])

    def swapped(weight):
        return lax.ppermute(weight, "ep", ring.swap)

    at_start = section_index == 0
    cot_in = jnp.where(at_start, entering[1], moved_cot)

    def entered(moved_rise):
        return jnp.where(at_start, entering[0], moved_rise)

    ring.held["cot"] = {0: [packed_rows(cot_in, route_ids[:, 0], route_gates[:, 0], sources)]}
    ring.held["rise"] = {}

    head_rise = jnp.take(exit_list[0], section_index).astype(jnp.float32)
    head_fall = jnp.take(exit_list[1], sections - 1 - section_index).astype(jnp.float32)

    def exit_heads(rise_in, cot_in, head_rise, head_fall):
        rise_wide = rise_in.astype(jnp.float32)
        rise_diff = normed(rise_wide, exit_row) - targets[0].astype(jnp.float32)
        loss_rise = head_rise * 0.5 * jnp.mean(rise_diff * rise_diff, axis=-1)
        fall_diff = normed(fall_wide, exit_row) - targets[1].astype(jnp.float32)
        loss_fall = head_fall * 0.5 * jnp.mean(fall_diff * fall_diff, axis=-1)
        kept = cot_in.astype(jnp.float32)
        kept = kept + head_fall * norm_pullback(fall_wide, exit_row, fall_diff)
        return kept, jnp.stack([loss_rise, loss_fall])[:, None, :]

    def falling(kept):
        return kept + norm_pullback(fall_wide, norm_row, ring.total("backward"))

    if planned:
        ring.gather("fall", 2)
        own_gate, own_up, own_down = own
        other_gate, other_up = swapped(own_gate), swapped(own_up)
        heads = (head_rise, head_fall)
        cot_in, leaving_rise, own, other_gate, other_up, heads, ring.names = ring.fence(
            cot_in, leaving_rise, own, other_gate, other_up, heads, names
        )
        ring.gather("fall", 3)
        ring.gather("cot", 1)
        moved_rise = passed_along(leaving_rise, "pipe", 1)
        own_down = own[2]
        own = fetched(own)
        moved_rise, own, own_down = ring.fence(moved_rise, own, own_down)
        ring.gather("fall", 4)
        ring.gather("cot", 2)
        other_down = swapped(own_down)
        rise_in = entered(moved_rise)
        rise_normal = normed(rise_in.astype(jnp.float32), norm_row).astype(jnp.bfloat16)
        kept, exit_loss = exit_heads(rise_in, cot_in, *heads)
        ring.weights = own + (other_gate, other_up, None)
        ring.prepare([0, 1, 2, 3])
        rise_normal, kept, exit_loss, other_down = ring.fence(
            rise_normal, kept, exit_loss, other_down
        )
        ring.weights = own + (other_gate, other_up, other_down)
        ring.held["rise"] = {0: [rise_normal]}
        ring.gather("cot", 3)
        ring.gather("rise", 1)
        ring.work("backward", [0, 1, 2])
        ring.fence()
        ring.gather("cot", 4)
        ring.gather("rise", 2)
        ring.prepare([4])
        ring.work("forward", [0, 1])
        ring.fence()
        ring.gather("rise", 3)
        ring.work("backward", [3, 4])
        ring.fence()
        ring.gather("rise", 4)
        ring.scatter("backward", 1)
        ring.work("forward", [2])
        ring.fence()
        ring.scatter("backward", 2)
        ring.work("forward", [3, 4])
        ring.fence()
        ring.scatter("backward", 3)
        ring.scatter("forward", 1)
        ring.fence()
        ring.scatter("backward", 4)
        ring.scatter("forward", 2)
        ring.fence()
        ring.scatter("forward", 3)
        fall_total = falling(kept).astype(jnp.bfloat16)
        (fall_total,) = ring.fence(fall_total)
        ring.scatter("forward", 4)
    else:
        rise_in = entered(passed_along(leaving_rise, "pipe", 1))
        ring.weights = own + tuple(swapped(own))
        kept, exit_loss = exit_heads(rise_in, cot_in, head_rise, head_fall)
        rise_normal = normed(rise_in.astype(jnp.float32), norm_row).astype(jnp.bfloat16)
        ring.held["rise"] = {0: [rise_normal]}
        for name in ("fall", "cot", "rise"):
            for distance in range(1 if name != "fall" else 2, far + 1):
                ring.gather(name, distance)
        groups = [[0, 1]] + [[distance] for distance in range(2, far + 1)]
        for group in groups:
            ring.prepare(group)
            ring.work("backward", group)
        for group in groups:
            ring.work("forward", group)
        for kind in ("backward", "forward"):
            for step in range(1, far + 1):
                ring.scatter(kind, step)
        fall_total = falling(kept).astype(jnp.bfloat16)
    layer_out = (rise_in.astype(jnp.float32) + ring.total("forward")).astype(jnp.bfloat16)
    return (layer_out[None], fall_total[None], exit_loss)


def solution(mesh):
    placed = (
        P(None, "ep", None),
        P("pipe", "ep", None),
        P("pipe", "ep", None),
        P("pipe", "ep", None),
        P(None, "ep", None),
        P("pipe", None),
        P("pipe", None),
        P("pipe", "ep", None, None),
        P("pipe", "ep", None, None),
        P("pipe", "ep", None, None),
        P(None, "pipe", "ep", None),
        P(None, "pipe", "ep", None),
        P(),
    )
    return jax.shard_map(
        local,
        mesh=mesh,
        in_specs=placed,
        out_specs=(P("pipe", "ep", None), P("pipe", "ep", None), P(None, "pipe", "ep")),
        check_vma=False,
    )
```

```python
import functools
import jax
import jax.numpy as jnp
from jax import lax
from jax.experimental import pallas as pl
from jax.experimental.pallas import tpu as pltpu
from jax.sharding import PartitionSpec as P

EPSILON = 1e-06
VMEM_LIMIT = 24 * 1024 * 1024
NT = (((1,), (1,)), ((), ()))


def passed_along(block, axis, distance):
    devices = range(lax.axis_size(axis))
    route = [(i - distance, i) for i in devices if i - distance in devices]
    return lax.ppermute(block, axis, route)


def normed(values, gain_row):
    return (
        values * lax.rsqrt(jnp.mean(values * values, axis=-1, keepdims=True) + EPSILON) * gain_row
    )


def norm_pullback(values, gain_row, upstream):
    _, pullback = jax.vjp(lambda argument: normed(argument, gain_row), values)
    return pullback(upstream)[0]


def norm_kernel(rows_ref, gain_ref, out_ref):
    out_ref[...] = normed(rows_ref[...].astype(jnp.float32), gain_ref[...]).astype(jnp.bfloat16)


def normed_rows(rows, gain_row):
    count, width = rows.shape
    return pl.pallas_call(
        norm_kernel,
        out_shape=jax.ShapeDtypeStruct((count, width), jnp.bfloat16),
        compiler_params=pltpu.CompilerParams(vmem_limit_bytes=VMEM_LIMIT),
        cost_estimate=pl.CostEstimate(flops=0, bytes_accessed=count * width * 4, transcendentals=0),
    )(rows, gain_row)


def pack_kernel(experts, rows_ref, ids_ref, gates_ref, out_ref):
    width = rows_ref.shape[1]
    out_ref[:, :width] = rows_ref[...]
    count, extra = rows_ref.shape[0], out_ref.shape[1] - width
    lane = lax.broadcasted_iota(jnp.int32, (count, extra), 1)
    table = jnp.zeros((count, extra), jnp.float32)
    for m in range(2):
        for k in range(ids_ref.shape[2]):
            place = ids_ref[m, :, k : k + 1] + 2 * m * experts
            gate = gates_ref[m, :, k : k + 1]
            high = gate.astype(jnp.bfloat16).astype(jnp.float32)
            table = jnp.where(lane == place, high, table)
            table = jnp.where(lane == place + experts, gate - high, table)
    out_ref[:, width:] = table.astype(jnp.bfloat16)


def packed_rows(rows, ids, gates, experts):
    count, width = rows.shape
    extra = -(-4 * experts // 128) * 128
    return pl.pallas_call(
        functools.partial(pack_kernel, experts),
        out_shape=jax.ShapeDtypeStruct((count, width + extra), jnp.bfloat16),
        compiler_params=pltpu.CompilerParams(vmem_limit_bytes=VMEM_LIMIT),
        cost_estimate=pl.CostEstimate(flops=0, bytes_accessed=count * width * 8, transcendentals=0),
    )(rows, ids, gates)


def gate_column(table, micro, experts, expert):
    lane = lax.broadcasted_iota(jnp.int32, table.shape, 1)
    place = 2 * micro * experts + expert
    chosen = (lane == place) | (lane == place + experts)
    return jnp.sum(jnp.where(chosen, table, 0.0), axis=1, keepdims=True)


def start_all(copies):
    for copy in copies:
        copy.start()


def wait_all(copies):
    for copy in copies:
        copy.wait()


def block_copies(sources, target, sems, columns=None):
    copies, start = [], 0
    for i, source in enumerate(sources):
        count = source.shape[0]
        view = source if columns is None else source.at[:, columns]
        copies.append(
            pltpu.make_async_copy(view, target.at[pl.ds(start, count)], sems.at[i])
        )
        start += count
    return copies


def write_tiles(tile, outs, columns):
    start = 0
    for out in outs:
        count = out.shape[0]
        out[:, columns] = tile[start : start + count].astype(out.dtype)
        start += count


def dot(first, second):
    return jnp.dot(first, second, preferred_element_type=jnp.float32)


def dot_nt(first, second):
    return lax.dot_general(first, second, NT, preferred_element_type=jnp.float32)


def forward_kernel(parts, experts, width, tile, names_ref, *refs):
    packed, rows = refs[:parts], refs[parts : 2 * parts]
    weights = refs[2 * parts : 2 * parts + 6]
    outs = refs[2 * parts + 6 : 3 * parts + 6]
    table, held, hidden, table_sem, row_sem = refs[3 * parts + 6 :]
    extra = table.shape[1]
    inner = weights[0].shape[1]
    copies = block_copies(rows, held, row_sem)
    copies += block_copies(packed, table, table_sem, pl.ds(width, extra))
    start_all(copies)
    wait_all(copies)
    for e in range(2):
        gate = gate_column(table[...].astype(jnp.float32), 0, experts, names_ref[e])
        first = dot(held[...], weights[3 * e][...])
        second = dot(held[...], weights[3 * e + 1][...])
        made = gate * (jax.nn.silu(first) * second)
        hidden[:, pl.ds(e * inner, inner)] = made.astype(jnp.bfloat16)

    @pl.loop(0, width // tile)
    def _(n):
        columns = pl.ds(pl.multiple_of(n * tile, tile), tile)
        total = dot(hidden[:, :inner], weights[2][:, columns])
        total = total + dot(hidden[:, inner:], weights[5][:, columns])
        write_tiles(total, outs, columns)


def factor_kernel(parts, *refs):
    rows, weights, out = refs[:parts], refs[parts : parts + 4], refs[parts + 4]
    held, row_sem = refs[parts + 5 :]
    copies = block_copies(rows, held, row_sem)
    start_all(copies)
    wait_all(copies)
    for e in range(2):
        first = dot(held[...], weights[2 * e][...])
        second = dot(held[...], weights[2 * e + 1][...])
        sigmoid_part = jax.nn.sigmoid(first)
        out[2 * e] = (
            second * sigmoid_part * (1.0 + first * (1.0 - sigmoid_part))
        ).astype(jnp.bfloat16)
        out[2 * e + 1] = (first * sigmoid_part).astype(jnp.bfloat16)


def backward_kernel(parts, experts, width, tile, pieces, names_ref, *refs):
    packed, factors = refs[:parts], refs[parts : parts + len(pieces)]
    weights = refs[parts + len(pieces) :][:6]
    outs = refs[parts + len(pieces) + 6 :][:parts]
    cot, slot, grads, cot_sem, factor_sem = refs[2 * parts + len(pieces) + 6 :]
    copies = block_copies(packed, cot, cot_sem)
    factor_copies, place = [], 0
    for i, (start, count) in enumerate(pieces):
        factor_copies.append(
            pltpu.make_async_copy(
                factors[i].at[:, pl.ds(start, count)],
                grads.at[:, pl.ds(place, count)],
                factor_sem.at[i],
            )
        )
        place += count
    start_all(copies + factor_copies)
    wait_all(copies)
    for e in range(2):
        table = cot[:, width:].astype(jnp.float32)
        gate = gate_column(table, 1, experts, names_ref[e])
        slot[...] = (gate * cot[:, :width].astype(jnp.float32)).astype(jnp.bfloat16)
        back = dot_nt(slot[...], weights[3 * e + 2][...])
        if e == 0:
            wait_all(factor_copies)
        for i in range(2):
            made = back * grads[2 * e + i].astype(jnp.float32)
            grads[2 * e + i] = made.astype(jnp.bfloat16)

    @pl.loop(0, width // tile)
    def _(n):
        columns = pl.ds(pl.multiple_of(n * tile, tile), tile)
        total = None
        for e in range(2):
            for i in range(2):
                term = dot_nt(grads[2 * e + i], weights[3 * e + i][columns, :])
                total = term if total is None else total + term
        write_tiles(total, outs, columns)


HBM = pl.BlockSpec(memory_space=pl.ANY)
TILE = 512


WHOLE = pl.BlockSpec(memory_space=pltpu.VMEM)


def in_vmem(weights):
    return [pltpu.with_memory_space_constraint(weight, pltpu.VMEM) for weight in weights]


def in_hbm(blocks):
    return [pltpu.with_memory_space_constraint(block, pltpu.HBM) for block in blocks]


def fetch_kernel(count, *refs):
    sems = refs[2 * count]
    copies = [
        pltpu.make_async_copy(refs[i], refs[count + i], sems.at[i]) for i in range(count)
    ]
    start_all(copies)
    wait_all(copies)


def fetched(weights):
    count = len(weights)
    return tuple(
        pl.pallas_call(
            functools.partial(fetch_kernel, count),
            out_shape=[pltpu.VMEM(weight.shape, weight.dtype) for weight in weights],
            in_specs=[HBM] * count,
            out_specs=[WHOLE] * count,
            scratch_shapes=[pltpu.SemaphoreType.DMA((count,))],
            compiler_params=PARAMS,
            cost_estimate=pl.CostEstimate(
                flops=0, bytes_accessed=8 * 2**20, transcendentals=0
            ),
        )(*in_hbm(weights))
    )


def cost(units, rows, width, inner, fixed):
    return pl.CostEstimate(
        flops=2 * units * rows * width * inner + int(fixed * 1.1e15),
        bytes_accessed=12 * width * inner,
        transcendentals=2 * rows * inner,
    )


PARAMS = pltpu.CompilerParams(vmem_limit_bytes=VMEM_LIMIT)


def forward_call(names, packed, rows, weights, experts):
    parts = len(rows)
    counts = [block.shape[0] for block in rows]
    total, width = sum(counts), rows[0].shape[1]
    full, inner = packed[0].shape[1], weights[0].shape[1]
    out = pl.pallas_call(
        functools.partial(forward_kernel, parts, experts, width, TILE),
        out_shape=[jax.ShapeDtypeStruct((count, width), jnp.bfloat16) for count in counts],
        in_specs=[pl.BlockSpec(memory_space=pltpu.SMEM)] + [HBM] * (2 * parts) + [WHOLE] * 6,
        scratch_shapes=[
            pltpu.VMEM((total, full - width), jnp.bfloat16),
            pltpu.VMEM((total, width), jnp.bfloat16),
            pltpu.VMEM((total, 2 * inner), jnp.bfloat16),
        ]
        + [pltpu.SemaphoreType.DMA((parts,)) for _ in range(2)],
        compiler_params=PARAMS,
        cost_estimate=cost(6, total, width, inner, 6e-6),
    )(names, *packed, *rows, *in_vmem(weights))
    return list(out)


def factor_call(rows, weights):
    parts = len(rows)
    total, width = sum(block.shape[0] for block in rows), rows[0].shape[1]
    inner = weights[0].shape[1]
    return pl.pallas_call(
        functools.partial(factor_kernel, parts),
        out_shape=jax.ShapeDtypeStruct((4, total, inner), jnp.bfloat16),
        in_specs=[HBM] * parts + [WHOLE] * 4,
        scratch_shapes=[
            pltpu.VMEM((total, width), jnp.bfloat16),
            pltpu.SemaphoreType.DMA((parts,)),
        ],
        compiler_params=PARAMS,
        cost_estimate=cost(4, total, width, inner, 5e-6),
    )(*in_hbm(rows), *in_vmem([weights[i] for i in (0, 1, 3, 4)]))


def backward_call(names, packed, factors, pieces, weights, experts):
    parts = len(packed)
    counts = [block.shape[0] for block in packed]
    total, full = sum(counts), packed[0].shape[1]
    width, inner = weights[0].shape
    out = pl.pallas_call(
        functools.partial(backward_kernel, parts, experts, width, TILE, pieces),
        out_shape=[jax.ShapeDtypeStruct((count, width), jnp.bfloat16) for count in counts],
        in_specs=[pl.BlockSpec(memory_space=pltpu.SMEM)] + [HBM] * (parts + len(pieces)) + [WHOLE] * 6,
        scratch_shapes=[
            pltpu.VMEM((total, full), jnp.bfloat16),
            pltpu.VMEM((total, width), jnp.bfloat16),
            pltpu.VMEM((4, total, inner), jnp.bfloat16),
            pltpu.SemaphoreType.DMA((parts,)),
            pltpu.SemaphoreType.DMA((len(pieces),)),
        ],
        compiler_params=PARAMS,
        cost_estimate=cost(6, total, width, inner, 6e-6),
    )(names, *packed, *factors, *in_vmem(weights))
    return list(out)


def added(first, second):
    return (first.astype(jnp.float32) + second.astype(jnp.float32)).astype(jnp.bfloat16)


def joined(block, moved, way):
    if moved is None:
        return block
    half = moved.shape[0]
    if half == block.shape[0]:
        return added(block, moved)
    if way == 0:
        return jnp.concatenate([added(block[:half], moved), block[half:]])
    return jnp.concatenate([block[:half], added(block[half:], moved)])


class Section:
    def __init__(self, sources, names):
        self.sources = sources
        self.names = names
        self.chips = sources // 2
        self.far = self.chips // 2
        order = list(range(0, self.chips, 2)) + list(range(1, self.chips, 2))[::-1]
        following = {order[i]: order[(i + 1) % self.chips] for i in range(self.chips)}
        pairs = [(2 * a + core, 2 * b + core) for a, b in following.items() for core in range(2)]
        self.routes = (pairs, [(b, a) for a, b in pairs])
        self.swap = [(i, i ^ 1) for i in range(sources)]
        self.held, self.made, self.sums, self.starts = {}, {}, {}, {}
        self.weights = None

    def pass_on(self, block, way):
        return lax.ppermute(block, "ep", self.routes[way])

    def gather(self, name, distance, way=None):
        held = self.held[name]
        behind, ahead = held[distance - 1][0], held[distance - 1][-1]
        if distance == self.far and way is not None:
            held[distance] = [self.pass_on((behind, ahead)[way], way)]
            return
        if distance == self.far:
            half = behind.shape[0] // 2
            behind, ahead = behind[:half], ahead[half:]
        held[distance] = [self.pass_on(behind, 0), self.pass_on(ahead, 1)]

    def prepare(self, distances):
        blocks = [block for d in distances for block in self.held["fall"][d]]
        key, start = f"factors{distances[0]}", 0
        self.held[key] = {0: [factor_call(blocks, self.weights)]}
        for d in distances:
            count = sum(block.shape[0] for block in self.held["fall"][d])
            self.starts[d] = (key, start, count)
            start += count

    def work(self, kind, distances):
        packed = [block for d in distances for block in self.held["cot"][d]]
        if kind == "backward":
            runs = []
            for key, start, count in [self.starts[d] for d in distances]:
                if runs and runs[-1][0] == key and sum(runs[-1][1:]) == start:
                    runs[-1][2] += count
                else:
                    runs.append([key, start, count])
            factors = [self.held[key][0][0] for key, _, _ in runs]
            pieces = tuple((start, count) for _, start, count in runs)
            outs = backward_call(
                self.names, packed, factors, pieces, self.weights, self.sources
            )
        else:
            blocks = [block for d in distances for block in self.held["rise"][d]]
            outs = forward_call(self.names, packed, blocks, self.weights, self.sources)
        made = self.made.setdefault(kind, {})
        for d in distances:
            count = len(self.held["cot"][d])
            made[d], outs = outs[:count], outs[count:]

    def scatter(self, kind, step, way=None):
        distance = self.far + 1 - step
        pieces = self.made[kind].pop(distance)
        if step == 1 and len(pieces) == 1:
            half = pieces[0].shape[0] // 2
            if way is None:
                pieces = [pieces[0][:half], pieces[0][half:]]
            else:
                pieces = [pieces[0] if way == i else None for i in range(2)]
        elif step > 1:
            moved = self.sums[kind]
            pieces = [joined(pieces[1 - i], moved[i], i) for i in range(2)]
        self.sums[kind] = [
            None if piece is None else self.pass_on(piece, i) for i, piece in enumerate(pieces)
        ]

    def total(self, kind):
        pieces = self.made[kind][0] + self.sums[kind]
        return sum(piece.astype(jnp.float32) for piece in pieces)

    def fence(self, *others):
        state = (self.held, self.made, self.sums, others)
        state = lax.optimization_barrier(state)
        self.held, self.made, self.sums, others = state
        return others


def local(
    entering,
    rising_prev,
    falling_cot,
    falling_saved,
    targets,
    norm_gain,
    exit_gain,
    w_gate,
    w_up,
    w_down,
    route_ids,
    route_gates,
    exit_list,
):
    section_index = lax.axis_index("pipe")
    sections = lax.axis_size("pipe")
    sources = lax.axis_size("ep")
    here = lax.axis_index("ep")
    names = jnp.stack([here, here + 1 - 2 * (here % 2)]).astype(jnp.int32)
    norm_row = norm_gain[0]
    exit_row = exit_gain[0]
    ring = Section(sources, names)
    far = ring.far
    planned = far == 4

    fall_wide = falling_saved[0].astype(jnp.float32)
    fall_normal = normed_rows(falling_saved[0], norm_gain)
    fall_normal, leaving_cot, leaving_rise = lax.optimization_barrier(
        (fall_normal, falling_cot[0], rising_prev[0])
    )
    ring.held["fall"] = {0: [fall_normal]}
    ring.gather("fall", 1)
    moved_cot = passed_along(leaving_cot, "pipe", 1)
    own = (w_gate[0, 0], w_up[0, 0], w_down[0, 0])

    def swapped(weight):
        return lax.ppermute(weight, "ep", ring.swap)

    at_start = section_index == 0
    cot_in = jnp.where(at_start, entering[1], moved_cot)

    def entered(moved_rise):
        return jnp.where(at_start, entering[0], moved_rise)

    ring.held["cot"] = {0: [packed_rows(cot_in, route_ids[:, 0], route_gates[:, 0], sources)]}
    ring.held["rise"] = {}

    head_rise = jnp.take(exit_list[0], section_index).astype(jnp.float32)
    head_fall = jnp.take(exit_list[1], sections - 1 - section_index).astype(jnp.float32)

    def exit_heads(rise_in, cot_in, head_rise, head_fall):
        rise_wide = rise_in.astype(jnp.float32)
        rise_diff = normed(rise_wide, exit_row) - targets[0].astype(jnp.float32)
        loss_rise = head_rise * 0.5 * jnp.mean(rise_diff * rise_diff, axis=-1)
        fall_diff = normed(fall_wide, exit_row) - targets[1].astype(jnp.float32)
        loss_fall = head_fall * 0.5 * jnp.mean(fall_diff * fall_diff, axis=-1)
        kept = cot_in.astype(jnp.float32)
        kept = kept + head_fall * norm_pullback(fall_wide, exit_row, fall_diff)
        return kept, jnp.stack([loss_rise, loss_fall])[:, None, :]

    def falling(kept):
        return kept + norm_pullback(fall_wide, norm_row, ring.total("backward"))

    if planned:
        ring.gather("fall", 2)
        own_gate, own_up, own_down = own
        other_gate, other_up = swapped(own_gate), swapped(own_up)
        packed, leaving_rise = lax.optimization_barrier((ring.held["cot"][0][0], leaving_rise))
        ring.held["cot"][0] = [packed]
        moved_rise = passed_along(leaving_rise, "pipe", 1)
        own = fetched(own)
        heads = (head_rise, head_fall)
        cot_in, own, own_down, other_gate, other_up, heads, ring.names = ring.fence(
            cot_in, own, own_down, other_gate, other_up, heads, names
        )
        ring.gather("fall", 3)
        ring.gather("cot", 1)
        ring.weights = own + (other_gate, other_up, None)
        ring.prepare([0, 1, 2])
        moved_rise, own_down = ring.fence(moved_rise, own_down)
        ring.gather("fall", 4)
        ring.gather("cot", 2)
        other_down = swapped(own_down)
        rise_in = entered(moved_rise)
        rise_normal = normed(rise_in.astype(jnp.float32), norm_row).astype(jnp.bfloat16)
        kept, exit_loss = exit_heads(rise_in, cot_in, *heads)
        rise_normal, kept, exit_loss, other_down = ring.fence(
            rise_normal, kept, exit_loss, other_down
        )
        ring.weights = own + (other_gate, other_up, other_down)
        ring.held["rise"] = {0: [rise_normal]}
        ring.gather("cot", 3)
        ring.gather("rise", 1)
        ring.work("backward", [0, 1, 2])
        ring.prepare([3, 4])
        ring.fence()
        ring.gather("cot", 4)
        ring.gather("rise", 2)
        ring.work("forward", [0, 1])
        ring.fence()
        ring.gather("rise", 3)
        ring.work("backward", [3, 4])
        ring.fence()
        ring.gather("rise", 4)
        ring.scatter("backward", 1)
        ring.work("forward", [2])
        ring.fence()
        ring.scatter("backward", 2)
        ring.work("forward", [3, 4])
        ring.fence()
        ring.scatter("backward", 3)
        ring.scatter("forward", 1)
        ring.fence()
        ring.scatter("backward", 4)
        ring.scatter("forward", 2)
        ring.fence()
        ring.scatter("forward", 3)
        fall_total = falling(kept).astype(jnp.bfloat16)
        (fall_total,) = ring.fence(fall_total)
        ring.scatter("forward", 4)
    else:
        rise_in = entered(passed_along(leaving_rise, "pipe", 1))
        ring.weights = own + tuple(swapped(own))
        kept, exit_loss = exit_heads(rise_in, cot_in, head_rise, head_fall)
        rise_normal = normed(rise_in.astype(jnp.float32), norm_row).astype(jnp.bfloat16)
        ring.held["rise"] = {0: [rise_normal]}
        for name in ("fall", "cot", "rise"):
            for distance in range(1 if name != "fall" else 2, far + 1):
                ring.gather(name, distance)
        groups = [[0, 1]] + [[distance] for distance in range(2, far + 1)]
        for group in groups:
            ring.prepare(group)
            ring.work("backward", group)
        for group in groups:
            ring.work("forward", group)
        for kind in ("backward", "forward"):
            for step in range(1, far + 1):
                ring.scatter(kind, step)
        fall_total = falling(kept).astype(jnp.bfloat16)
    layer_out = (rise_in.astype(jnp.float32) + ring.total("forward")).astype(jnp.bfloat16)
    return (layer_out[None], fall_total[None], exit_loss)


def solution(mesh):
    placed = (
        P(None, "ep", None),
        P("pipe", "ep", None),
        P("pipe", "ep", None),
        P("pipe", "ep", None),
        P(None, "ep", None),
        P("pipe", None),
        P("pipe", None),
        P("pipe", "ep", None, None),
        P("pipe", "ep", None, None),
        P("pipe", "ep", None, None),
        P(None, "pipe", "ep", None),
        P(None, "pipe", "ep", None),
        P(),
    )
    return jax.shard_map(
        local,
        mesh=mesh,
        in_specs=placed,
        out_specs=(P("pipe", "ep", None), P("pipe", "ep", None), P(None, "pipe", "ep")),
        check_vma=False,
    )
```

```python
import functools
import jax
import jax.numpy as jnp
from jax import lax
from jax.experimental import pallas as pl
from jax.experimental.pallas import tpu as pltpu
from jax.sharding import PartitionSpec as P

EPSILON = 1e-06
VMEM_LIMIT = 16 * 1024 * 1024
NT = (((1,), (1,)), ((), ()))


def passed_along(block, axis, distance):
    devices = range(lax.axis_size(axis))
    route = [(i - distance, i) for i in devices if i - distance in devices]
    return lax.ppermute(block, axis, route)


def normed(values, gain_row):
    return (
        values * lax.rsqrt(jnp.mean(values * values, axis=-1, keepdims=True) + EPSILON) * gain_row
    )


def norm_pullback(values, gain_row, upstream):
    _, pullback = jax.vjp(lambda argument: normed(argument, gain_row), values)
    return pullback(upstream)[0]


def norm_kernel(rows_ref, gain_ref, out_ref):
    out_ref[...] = normed(rows_ref[...].astype(jnp.float32), gain_ref[...]).astype(jnp.bfloat16)


def normed_rows(rows, gain_row):
    count, width = rows.shape
    return pl.pallas_call(
        norm_kernel,
        out_shape=jax.ShapeDtypeStruct((count, width), jnp.bfloat16),
        compiler_params=pltpu.CompilerParams(vmem_limit_bytes=VMEM_LIMIT),
        cost_estimate=pl.CostEstimate(flops=0, bytes_accessed=count * width * 4, transcendentals=0),
    )(rows, gain_row)


def pack_kernel(experts, rows_ref, ids_ref, gates_ref, out_ref):
    width = rows_ref.shape[1]
    out_ref[:, :width] = rows_ref[...]
    count, extra = rows_ref.shape[0], out_ref.shape[1] - width
    lane = lax.broadcasted_iota(jnp.int32, (count, extra), 1)
    table = jnp.zeros((count, extra), jnp.float32)
    for m in range(2):
        for k in range(ids_ref.shape[2]):
            place = ids_ref[m, :, k : k + 1] + 2 * m * experts
            gate = gates_ref[m, :, k : k + 1]
            high = gate.astype(jnp.bfloat16).astype(jnp.float32)
            table = jnp.where(lane == place, high, table)
            table = jnp.where(lane == place + experts, gate - high, table)
    out_ref[:, width:] = table.astype(jnp.bfloat16)


def packed_rows(rows, ids, gates, experts):
    count, width = rows.shape
    extra = -(-4 * experts // 128) * 128
    return pl.pallas_call(
        functools.partial(pack_kernel, experts),
        out_shape=jax.ShapeDtypeStruct((count, width + extra), jnp.bfloat16),
        compiler_params=pltpu.CompilerParams(vmem_limit_bytes=VMEM_LIMIT),
        cost_estimate=pl.CostEstimate(flops=0, bytes_accessed=count * width * 8, transcendentals=0),
    )(rows, ids, gates)


def gate_column(table, micro, experts, expert):
    lane = lax.broadcasted_iota(jnp.int32, table.shape, 1)
    place = 2 * micro * experts + expert
    chosen = (lane == place) | (lane == place + experts)
    return jnp.sum(jnp.where(chosen, table, 0.0), axis=1, keepdims=True)


def start_all(copies):
    for copy in copies:
        copy.start()


def wait_all(copies):
    for copy in copies:
        copy.wait()


def block_copies(sources, target, sems, columns=None):
    copies, start = [], 0
    for i, source in enumerate(sources):
        count = source.shape[0]
        view = source if columns is None else source.at[:, columns]
        copies.append(
            pltpu.make_async_copy(view, target.at[pl.ds(start, count)], sems.at[i])
        )
        start += count
    return copies


def write_tiles(tile, outs, columns):
    start = 0
    for out in outs:
        count = out.shape[0]
        out[:, columns] = tile[start : start + count].astype(out.dtype)
        start += count


def dot(first, second):
    return jnp.dot(first, second, preferred_element_type=jnp.float32)


def dot_nt(first, second):
    return lax.dot_general(first, second, NT, preferred_element_type=jnp.float32)


def forward_kernel(parts, experts, width, tile, names_ref, *refs):
    packed, rows = refs[:parts], refs[parts : 2 * parts]
    weights = refs[2 * parts : 2 * parts + 6]
    outs = refs[2 * parts + 6 : 3 * parts + 6]
    table, held, hidden, table_sem, row_sem = refs[3 * parts + 6 :]
    extra = table.shape[1]
    inner = weights[0].shape[1]
    copies = block_copies(rows, held, row_sem)
    copies += block_copies(packed, table, table_sem, pl.ds(width, extra))
    start_all(copies)
    wait_all(copies)
    for e in range(2):
        gate = gate_column(table[...].astype(jnp.float32), 0, experts, names_ref[e])
        first = dot(held[...], weights[3 * e][...])
        second = dot(held[...], weights[3 * e + 1][...])
        made = gate * (jax.nn.silu(first) * second)
        hidden[:, pl.ds(e * inner, inner)] = made.astype(jnp.bfloat16)

    @pl.loop(0, width // tile)
    def _(n):
        columns = pl.ds(pl.multiple_of(n * tile, tile), tile)
        total = dot(hidden[:, :inner], weights[2][:, columns])
        total = total + dot(hidden[:, inner:], weights[5][:, columns])
        write_tiles(total, outs, columns)


def factor_kernel(parts, *refs):
    rows, weights, out = refs[:parts], refs[parts : parts + 4], refs[parts + 4]
    held, row_sem = refs[parts + 5 :]
    copies = block_copies(rows, held, row_sem)
    start_all(copies)
    wait_all(copies)
    for e in range(2):
        first = dot(held[...], weights[2 * e][...])
        second = dot(held[...], weights[2 * e + 1][...])
        sigmoid_part = jax.nn.sigmoid(first)
        out[2 * e] = (
            second * sigmoid_part * (1.0 + first * (1.0 - sigmoid_part))
        ).astype(jnp.bfloat16)
        out[2 * e + 1] = (first * sigmoid_part).astype(jnp.bfloat16)


def backward_kernel(parts, experts, width, tile, pieces, names_ref, *refs):
    packed, factors = refs[:parts], refs[parts : parts + len(pieces)]
    weights = refs[parts + len(pieces) :][:6]
    outs = refs[parts + len(pieces) + 6 :][:parts]
    cot, slot, grads, cot_sem, factor_sem = refs[2 * parts + len(pieces) + 6 :]
    copies = block_copies(packed, cot, cot_sem)
    factor_copies, place = [], 0
    for i, (start, count) in enumerate(pieces):
        factor_copies.append(
            pltpu.make_async_copy(
                factors[i].at[:, pl.ds(start, count)],
                grads.at[:, pl.ds(place, count)],
                factor_sem.at[i],
            )
        )
        place += count
    start_all(copies + factor_copies)
    wait_all(copies)
    for e in range(2):
        table = cot[:, width:].astype(jnp.float32)
        gate = gate_column(table, 1, experts, names_ref[e])
        slot[...] = (gate * cot[:, :width].astype(jnp.float32)).astype(jnp.bfloat16)
        back = dot_nt(slot[...], weights[3 * e + 2][...])
        if e == 0:
            wait_all(factor_copies)
        for i in range(2):
            made = back * grads[2 * e + i].astype(jnp.float32)
            grads[2 * e + i] = made.astype(jnp.bfloat16)

    @pl.loop(0, width // tile)
    def _(n):
        columns = pl.ds(pl.multiple_of(n * tile, tile), tile)
        total = None
        for e in range(2):
            for i in range(2):
                term = dot_nt(grads[2 * e + i], weights[3 * e + i][columns, :])
                total = term if total is None else total + term
        write_tiles(total, outs, columns)


HBM = pl.BlockSpec(memory_space=pl.ANY)
TILE = 512


WHOLE = pl.BlockSpec(memory_space=pltpu.VMEM)


def in_vmem(weights):
    return [pltpu.with_memory_space_constraint(weight, pltpu.VMEM) for weight in weights]


def in_hbm(blocks):
    return [pltpu.with_memory_space_constraint(block, pltpu.HBM) for block in blocks]


def fetch_kernel(count, *refs):
    sems = refs[2 * count]
    copies = [
        pltpu.make_async_copy(refs[i], refs[count + i], sems.at[i]) for i in range(count)
    ]
    start_all(copies)
    wait_all(copies)


def fetched(weights):
    count = len(weights)
    return tuple(
        pl.pallas_call(
            functools.partial(fetch_kernel, count),
            out_shape=[pltpu.VMEM(weight.shape, weight.dtype) for weight in weights],
            in_specs=[HBM] * count,
            out_specs=[WHOLE] * count,
            scratch_shapes=[pltpu.SemaphoreType.DMA((count,))],
            compiler_params=PARAMS,
            cost_estimate=pl.CostEstimate(
                flops=0, bytes_accessed=8 * 2**20, transcendentals=0
            ),
        )(*in_hbm(weights))
    )


def cost(units, rows, width, inner, fixed):
    return pl.CostEstimate(
        flops=2 * units * rows * width * inner + int(fixed * 1.1e15),
        bytes_accessed=12 * width * inner,
        transcendentals=2 * rows * inner,
    )


PARAMS = pltpu.CompilerParams(vmem_limit_bytes=VMEM_LIMIT)


def forward_call(names, packed, rows, weights, experts):
    parts = len(rows)
    counts = [block.shape[0] for block in rows]
    total, width = sum(counts), rows[0].shape[1]
    full, inner = packed[0].shape[1], weights[0].shape[1]
    out = pl.pallas_call(
        functools.partial(forward_kernel, parts, experts, width, TILE),
        out_shape=[jax.ShapeDtypeStruct((count, width), jnp.bfloat16) for count in counts],
        in_specs=[pl.BlockSpec(memory_space=pltpu.SMEM)] + [HBM] * (2 * parts) + [WHOLE] * 6,
        scratch_shapes=[
            pltpu.VMEM((total, full - width), jnp.bfloat16),
            pltpu.VMEM((total, width), jnp.bfloat16),
            pltpu.VMEM((total, 2 * inner), jnp.bfloat16),
        ]
        + [pltpu.SemaphoreType.DMA((parts,)) for _ in range(2)],
        compiler_params=PARAMS,
        cost_estimate=cost(6, total, width, inner, 6e-6),
    )(names, *packed, *rows, *in_vmem(weights))
    return list(out)


def factor_call(rows, weights):
    parts = len(rows)
    total, width = sum(block.shape[0] for block in rows), rows[0].shape[1]
    inner = weights[0].shape[1]
    return pl.pallas_call(
        functools.partial(factor_kernel, parts),
        out_shape=jax.ShapeDtypeStruct((4, total, inner), jnp.bfloat16),
        in_specs=[HBM] * parts + [WHOLE] * 4,
        scratch_shapes=[
            pltpu.VMEM((total, width), jnp.bfloat16),
            pltpu.SemaphoreType.DMA((parts,)),
        ],
        compiler_params=PARAMS,
        cost_estimate=cost(4, total, width, inner, 5e-6),
    )(*in_hbm(rows), *in_vmem([weights[i] for i in (0, 1, 3, 4)]))


def backward_call(names, packed, factors, pieces, weights, experts):
    parts = len(packed)
    counts = [block.shape[0] for block in packed]
    total, full = sum(counts), packed[0].shape[1]
    width, inner = weights[0].shape
    out = pl.pallas_call(
        functools.partial(backward_kernel, parts, experts, width, TILE, pieces),
        out_shape=[jax.ShapeDtypeStruct((count, width), jnp.bfloat16) for count in counts],
        in_specs=[pl.BlockSpec(memory_space=pltpu.SMEM)] + [HBM] * (parts + len(pieces)) + [WHOLE] * 6,
        scratch_shapes=[
            pltpu.VMEM((total, full), jnp.bfloat16),
            pltpu.VMEM((total, width), jnp.bfloat16),
            pltpu.VMEM((4, total, inner), jnp.bfloat16),
            pltpu.SemaphoreType.DMA((parts,)),
            pltpu.SemaphoreType.DMA((len(pieces),)),
        ],
        compiler_params=PARAMS,
        cost_estimate=cost(6, total, width, inner, 6e-6),
    )(names, *packed, *factors, *in_vmem(weights))
    return list(out)


def added(first, second):
    return (first.astype(jnp.float32) + second.astype(jnp.float32)).astype(jnp.bfloat16)


def joined(block, moved, way):
    if moved is None:
        return block
    half = moved.shape[0]
    if half == block.shape[0]:
        return added(block, moved)
    if way == 0:
        return jnp.concatenate([added(block[:half], moved), block[half:]])
    return jnp.concatenate([block[:half], added(block[half:], moved)])


class Section:
    def __init__(self, sources, names):
        self.sources = sources
        self.names = names
        self.chips = sources // 2
        self.far = self.chips // 2
        order = list(range(0, self.chips, 2)) + list(range(1, self.chips, 2))[::-1]
        following = {order[i]: order[(i + 1) % self.chips] for i in range(self.chips)}
        pairs = [(2 * a + core, 2 * b + core) for a, b in following.items() for core in range(2)]
        self.routes = (pairs, [(b, a) for a, b in pairs])
        self.swap = [(i, i ^ 1) for i in range(sources)]
        self.held, self.made, self.sums, self.starts = {}, {}, {}, {}
        self.weights = None

    def pass_on(self, block, way):
        return lax.ppermute(block, "ep", self.routes[way])

    def gather(self, name, distance, way=None):
        held = self.held[name]
        behind, ahead = held[distance - 1][0], held[distance - 1][-1]
        if distance == self.far and way is not None:
            held[distance] = [self.pass_on((behind, ahead)[way], way)]
            return
        if distance == self.far:
            half = behind.shape[0] // 2
            behind, ahead = behind[:half], ahead[half:]
        held[distance] = [self.pass_on(behind, 0), self.pass_on(ahead, 1)]

    def prepare(self, distances):
        blocks = [block for d in distances for block in self.held["fall"][d]]
        key, start = f"factors{distances[0]}", 0
        self.held[key] = {0: [factor_call(blocks, self.weights)]}
        for d in distances:
            count = sum(block.shape[0] for block in self.held["fall"][d])
            self.starts[d] = (key, start, count)
            start += count

    def work(self, kind, distances):
        packed = [block for d in distances for block in self.held["cot"][d]]
        if kind == "backward":
            runs = []
            for key, start, count in [self.starts[d] for d in distances]:
                if runs and runs[-1][0] == key and sum(runs[-1][1:]) == start:
                    runs[-1][2] += count
                else:
                    runs.append([key, start, count])
            factors = [self.held[key][0][0] for key, _, _ in runs]
            pieces = tuple((start, count) for _, start, count in runs)
            outs = backward_call(
                self.names, packed, factors, pieces, self.weights, self.sources
            )
        else:
            blocks = [block for d in distances for block in self.held["rise"][d]]
            outs = forward_call(self.names, packed, blocks, self.weights, self.sources)
        made = self.made.setdefault(kind, {})
        for d in distances:
            count = len(self.held["cot"][d])
            made[d], outs = outs[:count], outs[count:]

    def scatter(self, kind, step, way=None):
        distance = self.far + 1 - step
        pieces = self.made[kind].pop(distance)
        if step == 1 and len(pieces) == 1:
            half = pieces[0].shape[0] // 2
            if way is None:
                pieces = [pieces[0][:half], pieces[0][half:]]
            else:
                pieces = [pieces[0] if way == i else None for i in range(2)]
        elif step > 1:
            moved = self.sums[kind]
            pieces = [joined(pieces[1 - i], moved[i], i) for i in range(2)]
        self.sums[kind] = [
            None if piece is None else self.pass_on(piece, i) for i, piece in enumerate(pieces)
        ]

    def total(self, kind):
        pieces = self.made[kind][0] + self.sums[kind]
        return sum(piece.astype(jnp.float32) for piece in pieces)

    def fence(self, *others):
        state = (self.held, self.made, self.sums, others)
        state = lax.optimization_barrier(state)
        self.held, self.made, self.sums, others = state
        return others


def local(
    entering,
    rising_prev,
    falling_cot,
    falling_saved,
    targets,
    norm_gain,
    exit_gain,
    w_gate,
    w_up,
    w_down,
    route_ids,
    route_gates,
    exit_list,
):
    section_index = lax.axis_index("pipe")
    sections = lax.axis_size("pipe")
    sources = lax.axis_size("ep")
    here = lax.axis_index("ep")
    names = jnp.stack([here, here + 1 - 2 * (here % 2)]).astype(jnp.int32)
    norm_row = norm_gain[0]
    exit_row = exit_gain[0]
    ring = Section(sources, names)
    far = ring.far
    planned = far == 4

    fall_wide = falling_saved[0].astype(jnp.float32)
    fall_normal = normed_rows(falling_saved[0], norm_gain)
    fall_normal, leaving_cot, leaving_rise = lax.optimization_barrier(
        (fall_normal, falling_cot[0], rising_prev[0])
    )
    ring.held["fall"] = {0: [fall_normal]}
    ring.gather("fall", 1)
    moved_cot = passed_along(leaving_cot, "pipe", 1)
    own = (w_gate[0, 0], w_up[0, 0], w_down[0, 0])

    def swapped(weight):
        return lax.ppermute(weight, "ep", ring.swap)

    at_start = section_index == 0
    cot_in = jnp.where(at_start, entering[1], moved_cot)

    def entered(moved_rise):
        return jnp.where(at_start, entering[0], moved_rise)

    ring.held["cot"] = {0: [packed_rows(cot_in, route_ids[:, 0], route_gates[:, 0], sources)]}
    ring.held["rise"] = {}

    head_rise = jnp.take(exit_list[0], section_index).astype(jnp.float32)
    head_fall = jnp.take(exit_list[1], sections - 1 - section_index).astype(jnp.float32)

    def exit_heads(rise_in, cot_in, head_rise, head_fall):
        rise_wide = rise_in.astype(jnp.float32)
        rise_diff = normed(rise_wide, exit_row) - targets[0].astype(jnp.float32)
        loss_rise = head_rise * 0.5 * jnp.mean(rise_diff * rise_diff, axis=-1)
        fall_diff = normed(fall_wide, exit_row) - targets[1].astype(jnp.float32)
        loss_fall = head_fall * 0.5 * jnp.mean(fall_diff * fall_diff, axis=-1)
        kept = cot_in.astype(jnp.float32)
        kept = kept + head_fall * norm_pullback(fall_wide, exit_row, fall_diff)
        return kept, jnp.stack([loss_rise, loss_fall])[:, None, :]

    def falling(kept):
        return kept + norm_pullback(fall_wide, norm_row, ring.total("backward"))

    if planned:
        ring.gather("fall", 2)
        own_gate, own_up, own_down = own
        other_gate, other_up = swapped(own_gate), swapped(own_up)
        packed, leaving_rise = lax.optimization_barrier((ring.held["cot"][0][0], leaving_rise))
        ring.held["cot"][0] = [packed]
        moved_rise = passed_along(leaving_rise, "pipe", 1)
        heads = (head_rise, head_fall)
        cot_in, own, own_down, other_gate, other_up, heads, ring.names = ring.fence(
            cot_in, own, own_down, other_gate, other_up, heads, names
        )
        ring.gather("fall", 3)
        ring.gather("cot", 1)
        own = fetched(own)
        moved_rise, own, own_down = ring.fence(moved_rise, own, own_down)
        ring.gather("fall", 4)
        ring.gather("cot", 2)
        ring.weights = own + (other_gate, other_up, None)
        ring.prepare([0, 1, 2, 3])
        other_down = swapped(own_down)
        rise_in = entered(moved_rise)
        rise_normal = normed(rise_in.astype(jnp.float32), norm_row).astype(jnp.bfloat16)
        kept, exit_loss = exit_heads(rise_in, cot_in, *heads)
        rise_normal, kept, exit_loss, other_down = ring.fence(
            rise_normal, kept, exit_loss, other_down
        )
        ring.weights = own + (other_gate, other_up, other_down)
        ring.held["rise"] = {0: [rise_normal]}
        ring.gather("cot", 3)
        ring.gather("rise", 1)
        ring.work("backward", [0, 1, 2])
        ring.prepare([4])
        ring.fence()
        ring.gather("cot", 4)
        ring.gather("rise", 2)
        ring.work("forward", [0, 1])
        ring.fence()
        ring.gather("rise", 3)
        ring.work("backward", [3, 4])
        ring.fence()
        ring.gather("rise", 4)
        ring.scatter("backward", 1)
        ring.work("forward", [2])
        ring.fence()
        ring.scatter("backward", 2)
        ring.work("forward", [3, 4])
        ring.fence()
        ring.scatter("backward", 3)
        ring.scatter("forward", 1)
        ring.fence()
        ring.scatter("backward", 4)
        ring.scatter("forward", 2)
        ring.fence()
        ring.scatter("forward", 3)
        fall_total = falling(kept).astype(jnp.bfloat16)
        (fall_total,) = ring.fence(fall_total)
        ring.scatter("forward", 4)
    else:
        rise_in = entered(passed_along(leaving_rise, "pipe", 1))
        ring.weights = own + tuple(swapped(own))
        kept, exit_loss = exit_heads(rise_in, cot_in, head_rise, head_fall)
        rise_normal = normed(rise_in.astype(jnp.float32), norm_row).astype(jnp.bfloat16)
        ring.held["rise"] = {0: [rise_normal]}
        for name in ("fall", "cot", "rise"):
            for distance in range(1 if name != "fall" else 2, far + 1):
                ring.gather(name, distance)
        groups = [[0, 1]] + [[distance] for distance in range(2, far + 1)]
        for group in groups:
            ring.prepare(group)
            ring.work("backward", group)
        for group in groups:
            ring.work("forward", group)
        for kind in ("backward", "forward"):
            for step in range(1, far + 1):
                ring.scatter(kind, step)
        fall_total = falling(kept).astype(jnp.bfloat16)
    layer_out = (rise_in.astype(jnp.float32) + ring.total("forward")).astype(jnp.bfloat16)
    return (layer_out[None], fall_total[None], exit_loss)


def solution(mesh):
    placed = (
        P(None, "ep", None),
        P("pipe", "ep", None),
        P("pipe", "ep", None),
        P("pipe", "ep", None),
        P(None, "ep", None),
        P("pipe", None),
        P("pipe", None),
        P("pipe", "ep", None, None),
        P("pipe", "ep", None, None),
        P("pipe", "ep", None, None),
        P(None, "pipe", "ep", None),
        P(None, "pipe", "ep", None),
        P(),
    )
    return jax.shard_map(
        local,
        mesh=mesh,
        in_specs=placed,
        out_specs=(P("pipe", "ep", None), P("pipe", "ep", None), P(None, "pipe", "ep")),
        check_vma=False,
    )
```

```python
import functools
import jax
import jax.numpy as jnp
from jax import lax
from jax.experimental import pallas as pl
from jax.experimental.pallas import tpu as pltpu
from jax.sharding import PartitionSpec as P

EPSILON = 1e-06
VMEM_LIMIT = 16 * 1024 * 1024
NT = (((1,), (1,)), ((), ()))


def passed_along(block, axis, distance):
    devices = range(lax.axis_size(axis))
    route = [(i - distance, i) for i in devices if i - distance in devices]
    return lax.ppermute(block, axis, route)


def normed(values, gain_row):
    return (
        values * lax.rsqrt(jnp.mean(values * values, axis=-1, keepdims=True) + EPSILON) * gain_row
    )


def norm_pullback(values, gain_row, upstream):
    _, pullback = jax.vjp(lambda argument: normed(argument, gain_row), values)
    return pullback(upstream)[0]


def norm_kernel(rows_ref, gain_ref, out_ref):
    out_ref[...] = normed(rows_ref[...].astype(jnp.float32), gain_ref[...]).astype(jnp.bfloat16)


def normed_rows(rows, gain_row):
    count, width = rows.shape
    return pl.pallas_call(
        norm_kernel,
        out_shape=jax.ShapeDtypeStruct((count, width), jnp.bfloat16),
        compiler_params=pltpu.CompilerParams(vmem_limit_bytes=VMEM_LIMIT),
        cost_estimate=pl.CostEstimate(flops=0, bytes_accessed=count * width * 4, transcendentals=0),
    )(*in_hbm([rows, gain_row]))


def pack_kernel(experts, rows_ref, ids_ref, gates_ref, out_ref):
    width = rows_ref.shape[1]
    out_ref[:, :width] = rows_ref[...]
    count, extra = rows_ref.shape[0], out_ref.shape[1] - width
    lane = lax.broadcasted_iota(jnp.int32, (count, extra), 1)
    table = jnp.zeros((count, extra), jnp.float32)
    for m in range(2):
        for k in range(ids_ref.shape[2]):
            place = ids_ref[m, :, k : k + 1] + 2 * m * experts
            gate = gates_ref[m, :, k : k + 1]
            high = gate.astype(jnp.bfloat16).astype(jnp.float32)
            table = jnp.where(lane == place, high, table)
            table = jnp.where(lane == place + experts, gate - high, table)
    out_ref[:, width:] = table.astype(jnp.bfloat16)


def packed_rows(rows, ids, gates, experts):
    count, width = rows.shape
    extra = -(-4 * experts // 128) * 128
    return pl.pallas_call(
        functools.partial(pack_kernel, experts),
        out_shape=jax.ShapeDtypeStruct((count, width + extra), jnp.bfloat16),
        compiler_params=pltpu.CompilerParams(vmem_limit_bytes=VMEM_LIMIT),
        cost_estimate=pl.CostEstimate(flops=0, bytes_accessed=count * width * 8, transcendentals=0),
    )(rows, ids, gates)


def gate_column(table, micro, experts, expert):
    lane = lax.broadcasted_iota(jnp.int32, table.shape, 1)
    place = 2 * micro * experts + expert
    chosen = (lane == place) | (lane == place + experts)
    return jnp.sum(jnp.where(chosen, table, 0.0), axis=1, keepdims=True)


def start_all(copies):
    for copy in copies:
        copy.start()


def wait_all(copies):
    for copy in copies:
        copy.wait()


def block_copies(sources, target, sems, columns=None):
    copies, start = [], 0
    for i, source in enumerate(sources):
        count = source.shape[0]
        view = source if columns is None else source.at[:, columns]
        copies.append(
            pltpu.make_async_copy(view, target.at[pl.ds(start, count)], sems.at[i])
        )
        start += count
    return copies


def write_tiles(tile, outs, columns):
    start = 0
    for out in outs:
        count = out.shape[0]
        out[:, columns] = tile[start : start + count].astype(out.dtype)
        start += count


def dot(first, second):
    return jnp.dot(first, second, preferred_element_type=jnp.float32)


def dot_nt(first, second):
    return lax.dot_general(first, second, NT, preferred_element_type=jnp.float32)


def forward_kernel(parts, experts, width, tile, names_ref, *refs):
    packed, rows = refs[:parts], refs[parts : 2 * parts]
    weights = refs[2 * parts : 2 * parts + 6]
    outs = refs[2 * parts + 6 : 3 * parts + 6]
    table, held, hidden, table_sem, row_sem = refs[3 * parts + 6 :]
    extra = table.shape[1]
    inner = weights[0].shape[1]
    copies = block_copies(rows, held, row_sem)
    copies += block_copies(packed, table, table_sem, pl.ds(width, extra))
    start_all(copies)
    wait_all(copies)
    for e in range(2):
        gate = gate_column(table[...].astype(jnp.float32), 0, experts, names_ref[e])
        first = dot(held[...], weights[3 * e][...])
        second = dot(held[...], weights[3 * e + 1][...])
        made = gate * (jax.nn.silu(first) * second)
        hidden[:, pl.ds(e * inner, inner)] = made.astype(jnp.bfloat16)

    @pl.loop(0, width // tile)
    def _(n):
        columns = pl.ds(pl.multiple_of(n * tile, tile), tile)
        total = dot(hidden[:, :inner], weights[2][:, columns])
        total = total + dot(hidden[:, inner:], weights[5][:, columns])
        write_tiles(total, outs, columns)


def factor_kernel(parts, *refs):
    rows, weights, out = refs[:parts], refs[parts : parts + 4], refs[parts + 4]
    held, row_sem = refs[parts + 5 :]
    copies = block_copies(rows, held, row_sem)
    start_all(copies)
    wait_all(copies)
    for e in range(2):
        first = dot(held[...], weights[2 * e][...])
        second = dot(held[...], weights[2 * e + 1][...])
        sigmoid_part = jax.nn.sigmoid(first)
        out[2 * e] = (
            second * sigmoid_part * (1.0 + first * (1.0 - sigmoid_part))
        ).astype(jnp.bfloat16)
        out[2 * e + 1] = (first * sigmoid_part).astype(jnp.bfloat16)


def backward_kernel(parts, experts, width, tile, pieces, names_ref, *refs):
    packed, factors = refs[:parts], refs[parts : parts + len(pieces)]
    weights = refs[parts + len(pieces) :][:6]
    outs = refs[parts + len(pieces) + 6 :][:parts]
    slot, grads = refs[2 * parts + len(pieces) + 6 :]
    for e in range(2):
        row = 0
        for block in packed:
            count = block.shape[0]
            table = block[:, width:].astype(jnp.float32)
            gate = gate_column(table, 1, experts, names_ref[e])
            made = gate * block[:, :width].astype(jnp.float32)
            slot[row : row + count] = made.astype(jnp.bfloat16)
            row += count
        back = dot_nt(slot[...], weights[3 * e + 2][...])
        row = 0
        for factor, (start, count) in zip(factors, pieces):
            part = back[row : row + count]
            for i in range(2):
                made = part * factor[2 * e + i, start : start + count].astype(jnp.float32)
                grads[2 * e + i, row : row + count] = made.astype(jnp.bfloat16)
            row += count

    @pl.loop(0, width // tile)
    def _(n):
        columns = pl.ds(pl.multiple_of(n * tile, tile), tile)
        total = None
        for e in range(2):
            for i in range(2):
                term = dot_nt(grads[2 * e + i], weights[3 * e + i][columns, :])
                total = term if total is None else total + term
        write_tiles(total, outs, columns)


HBM = pl.BlockSpec(memory_space=pl.ANY)
TILE = 512


WHOLE = pl.BlockSpec(memory_space=pltpu.VMEM)


def in_vmem(weights):
    return [pltpu.with_memory_space_constraint(weight, pltpu.VMEM) for weight in weights]


def in_hbm(blocks):
    return [pltpu.with_memory_space_constraint(block, pltpu.HBM) for block in blocks]


def fetch_kernel(count, *refs):
    sems = refs[2 * count]
    copies = [
        pltpu.make_async_copy(refs[i], refs[count + i], sems.at[i]) for i in range(count)
    ]
    start_all(copies)
    wait_all(copies)


def fetched(weights):
    count = len(weights)
    return tuple(
        pl.pallas_call(
            functools.partial(fetch_kernel, count),
            out_shape=[pltpu.VMEM(weight.shape, weight.dtype) for weight in weights],
            in_specs=[HBM] * count,
            out_specs=[WHOLE] * count,
            scratch_shapes=[pltpu.SemaphoreType.DMA((count,))],
            compiler_params=PARAMS,
            cost_estimate=pl.CostEstimate(
                flops=0, bytes_accessed=8 * 2**20, transcendentals=0
            ),
        )(*in_hbm(weights))
    )


def cost(units, rows, width, inner, fixed):
    return pl.CostEstimate(
        flops=2 * units * rows * width * inner + int(fixed * 1.1e15),
        bytes_accessed=12 * width * inner,
        transcendentals=2 * rows * inner,
    )


PARAMS = pltpu.CompilerParams(vmem_limit_bytes=VMEM_LIMIT)


def forward_call(names, packed, rows, weights, experts):
    parts = len(rows)
    counts = [block.shape[0] for block in rows]
    total, width = sum(counts), rows[0].shape[1]
    full, inner = packed[0].shape[1], weights[0].shape[1]
    out = pl.pallas_call(
        functools.partial(forward_kernel, parts, experts, width, TILE),
        out_shape=[jax.ShapeDtypeStruct((count, width), jnp.bfloat16) for count in counts],
        in_specs=[pl.BlockSpec(memory_space=pltpu.SMEM)] + [HBM] * (2 * parts) + [WHOLE] * 6,
        scratch_shapes=[
            pltpu.VMEM((total, full - width), jnp.bfloat16),
            pltpu.VMEM((total, width), jnp.bfloat16),
            pltpu.VMEM((total, 2 * inner), jnp.bfloat16),
        ]
        + [pltpu.SemaphoreType.DMA((parts,)) for _ in range(2)],
        compiler_params=PARAMS,
        cost_estimate=cost(6, total, width, inner, 6e-6),
    )(names, *packed, *rows, *in_vmem(weights))
    return list(out)


def factor_call(rows, weights):
    parts = len(rows)
    total, width = sum(block.shape[0] for block in rows), rows[0].shape[1]
    inner = weights[0].shape[1]
    return pl.pallas_call(
        functools.partial(factor_kernel, parts),
        out_shape=jax.ShapeDtypeStruct((4, total, inner), jnp.bfloat16),
        in_specs=[HBM] * parts + [WHOLE] * 4,
        scratch_shapes=[
            pltpu.VMEM((total, width), jnp.bfloat16),
            pltpu.SemaphoreType.DMA((parts,)),
        ],
        compiler_params=PARAMS,
        cost_estimate=cost(4, total, width, inner, 5e-6),
    )(*in_hbm(rows), *in_vmem([weights[i] for i in (0, 1, 3, 4)]))


def backward_call(names, packed, factors, pieces, weights, experts):
    parts = len(packed)
    counts = [block.shape[0] for block in packed]
    total = sum(counts)
    width, inner = weights[0].shape
    out = pl.pallas_call(
        functools.partial(backward_kernel, parts, experts, width, TILE, pieces),
        out_shape=[jax.ShapeDtypeStruct((count, width), jnp.bfloat16) for count in counts],
        in_specs=[pl.BlockSpec(memory_space=pltpu.SMEM)] + [WHOLE] * (parts + len(pieces) + 6),
        scratch_shapes=[
            pltpu.VMEM((total, width), jnp.bfloat16),
            pltpu.VMEM((4, total, inner), jnp.bfloat16),
        ],
        compiler_params=PARAMS,
        cost_estimate=cost(6, total, width, inner, 6e-6),
    )(names, *in_vmem(packed), *in_vmem(factors), *in_vmem(weights))
    return list(out)


def added(first, second):
    return (first.astype(jnp.float32) + second.astype(jnp.float32)).astype(jnp.bfloat16)


def joined(block, moved, way):
    if moved is None:
        return block
    half = moved.shape[0]
    if half == block.shape[0]:
        return added(block, moved)
    if way == 0:
        return jnp.concatenate([added(block[:half], moved), block[half:]])
    return jnp.concatenate([block[:half], added(block[half:], moved)])


class Section:
    def __init__(self, sources, names):
        self.sources = sources
        self.names = names
        self.chips = sources // 2
        self.far = self.chips // 2
        order = list(range(0, self.chips, 2)) + list(range(1, self.chips, 2))[::-1]
        following = {order[i]: order[(i + 1) % self.chips] for i in range(self.chips)}
        pairs = [(2 * a + core, 2 * b + core) for a, b in following.items() for core in range(2)]
        self.routes = (pairs, [(b, a) for a, b in pairs])
        self.swap = [(i, i ^ 1) for i in range(sources)]
        self.held, self.made, self.sums, self.starts = {}, {}, {}, {}
        self.weights = None

    def pass_on(self, block, way):
        return lax.ppermute(block, "ep", self.routes[way])

    def gather(self, name, distance, way=None):
        held = self.held[name]
        behind, ahead = held[distance - 1][0], held[distance - 1][-1]
        if distance == self.far and way is not None:
            held[distance] = [self.pass_on((behind, ahead)[way], way)]
            return
        if distance == self.far:
            half = behind.shape[0] // 2
            behind, ahead = behind[:half], ahead[half:]
        held[distance] = [self.pass_on(behind, 0), self.pass_on(ahead, 1)]

    def prepare(self, distances):
        blocks = [block for d in distances for block in self.held["fall"][d]]
        key, start = f"factors{distances[0]}", 0
        self.held[key] = {0: [factor_call(blocks, self.weights)]}
        for d in distances:
            count = sum(block.shape[0] for block in self.held["fall"][d])
            self.starts[d] = (key, start, count)
            start += count

    def work(self, kind, distances):
        packed = [block for d in distances for block in self.held["cot"][d]]
        if kind == "backward":
            runs = []
            for key, start, count in [self.starts[d] for d in distances]:
                if runs and runs[-1][0] == key and sum(runs[-1][1:]) == start:
                    runs[-1][2] += count
                else:
                    runs.append([key, start, count])
            factors = [self.held[key][0][0] for key, _, _ in runs]
            pieces = tuple((start, count) for _, start, count in runs)
            outs = backward_call(
                self.names, packed, factors, pieces, self.weights, self.sources
            )
        else:
            blocks = [block for d in distances for block in self.held["rise"][d]]
            outs = forward_call(self.names, packed, blocks, self.weights, self.sources)
        made = self.made.setdefault(kind, {})
        for d in distances:
            count = len(self.held["cot"][d])
            made[d], outs = outs[:count], outs[count:]

    def scatter(self, kind, step, way=None):
        distance = self.far + 1 - step
        pieces = self.made[kind].pop(distance)
        if step == 1 and len(pieces) == 1:
            half = pieces[0].shape[0] // 2
            if way is None:
                pieces = [pieces[0][:half], pieces[0][half:]]
            else:
                pieces = [pieces[0] if way == i else None for i in range(2)]
        elif step > 1:
            moved = self.sums[kind]
            pieces = [joined(pieces[1 - i], moved[i], i) for i in range(2)]
        self.sums[kind] = [
            None if piece is None else self.pass_on(piece, i) for i, piece in enumerate(pieces)
        ]

    def total(self, kind):
        pieces = self.made[kind][0] + self.sums[kind]
        return sum(piece.astype(jnp.float32) for piece in pieces)

    def fence(self, *others):
        state = (self.held, self.made, self.sums, others)
        state = lax.optimization_barrier(state)
        self.held, self.made, self.sums, others = state
        return others


def local(
    entering,
    rising_prev,
    falling_cot,
    falling_saved,
    targets,
    norm_gain,
    exit_gain,
    w_gate,
    w_up,
    w_down,
    route_ids,
    route_gates,
    exit_list,
):
    section_index = lax.axis_index("pipe")
    sections = lax.axis_size("pipe")
    sources = lax.axis_size("ep")
    here = lax.axis_index("ep")
    names = jnp.stack([here, here + 1 - 2 * (here % 2)]).astype(jnp.int32)
    norm_row = norm_gain[0]
    exit_row = exit_gain[0]
    ring = Section(sources, names)
    far = ring.far
    planned = far == 4

    fall_wide = falling_saved[0].astype(jnp.float32)
    fall_normal = normed_rows(falling_saved[0], norm_gain)
    fall_normal, leaving_cot, leaving_rise = lax.optimization_barrier(
        (fall_normal, falling_cot[0], rising_prev[0])
    )
    ring.held["fall"] = {0: [fall_normal]}
    ring.gather("fall", 1)
    moved_cot = passed_along(leaving_cot, "pipe", 1)
    own = (w_gate[0, 0], w_up[0, 0], w_down[0, 0])

    def swapped(weight):
        return lax.ppermute(weight, "ep", ring.swap)

    at_start = section_index == 0
    cot_in = jnp.where(at_start, entering[1], moved_cot)

    def entered(moved_rise):
        return jnp.where(at_start, entering[0], moved_rise)

    ring.held["cot"] = {0: [packed_rows(cot_in, route_ids[:, 0], route_gates[:, 0], sources)]}
    ring.held["rise"] = {}

    head_rise = jnp.take(exit_list[0], section_index).astype(jnp.float32)
    head_fall = jnp.take(exit_list[1], sections - 1 - section_index).astype(jnp.float32)

    def exit_heads(rise_in, cot_in, head_rise, head_fall):
        rise_wide = rise_in.astype(jnp.float32)
        rise_diff = normed(rise_wide, exit_row) - targets[0].astype(jnp.float32)
        loss_rise = head_rise * 0.5 * jnp.mean(rise_diff * rise_diff, axis=-1)
        fall_diff = normed(fall_wide, exit_row) - targets[1].astype(jnp.float32)
        loss_fall = head_fall * 0.5 * jnp.mean(fall_diff * fall_diff, axis=-1)
        kept = cot_in.astype(jnp.float32)
        kept = kept + head_fall * norm_pullback(fall_wide, exit_row, fall_diff)
        return kept, jnp.stack([loss_rise, loss_fall])[:, None, :]

    def falling(kept):
        return kept + norm_pullback(fall_wide, norm_row, ring.total("backward"))

    if planned:
        first_hop, leaving_rise = lax.optimization_barrier((ring.held["fall"][1], leaving_rise))
        ring.held["fall"][1] = first_hop
        ring.gather("fall", 2)
        moved_rise = passed_along(leaving_rise, "pipe", 1)
        own_gate, own_up, own_down = own
        other_gate, other_up = swapped(own_gate), swapped(own_up)
        heads = (head_rise, head_fall)
        cot_in, moved_rise, own, own_down, other_gate, other_up, heads, ring.names = ring.fence(
            cot_in, moved_rise, own, own_down, other_gate, other_up, heads, names
        )
        ring.gather("fall", 3)
        ring.gather("cot", 1)
        own = fetched(own)
        moved_rise, cot_in, own, own_down = ring.fence(moved_rise, cot_in, own, own_down)
        ring.gather("fall", 4)
        ring.gather("cot", 2)
        ring.weights = own + (other_gate, other_up, None)
        ring.prepare([0, 1, 2, 3])
        other_down = swapped(own_down)
        rise_in = entered(moved_rise)
        rise_normal = normed(rise_in.astype(jnp.float32), norm_row).astype(jnp.bfloat16)
        kept, exit_loss = exit_heads(rise_in, cot_in, *heads)
        rise_normal, kept, exit_loss, other_down = ring.fence(
            rise_normal, kept, exit_loss, other_down
        )
        ring.weights = own + (other_gate, other_up, other_down)
        ring.held["rise"] = {0: [rise_normal]}
        ring.gather("cot", 3)
        ring.gather("rise", 1)
        ring.work("backward", [0, 1, 2])
        ring.prepare([4])
        ring.fence()
        ring.gather("cot", 4)
        ring.gather("rise", 2)
        ring.work("forward", [0, 1])
        ring.fence()
        ring.gather("rise", 3)
        ring.work("backward", [3, 4])
        ring.fence()
        ring.gather("rise", 4)
        ring.scatter("backward", 1)
        ring.work("forward", [2])
        ring.fence()
        ring.scatter("backward", 2)
        ring.work("forward", [3, 4])
        ring.fence()
        ring.scatter("backward", 3)
        ring.scatter("forward", 1)
        ring.fence()
        ring.scatter("backward", 4)
        ring.scatter("forward", 2)
        ring.fence()
        ring.scatter("forward", 3)
        fall_total = falling(kept).astype(jnp.bfloat16)
        (fall_total,) = ring.fence(fall_total)
        ring.scatter("forward", 4)
    else:
        rise_in = entered(passed_along(leaving_rise, "pipe", 1))
        ring.weights = own + tuple(swapped(own))
        kept, exit_loss = exit_heads(rise_in, cot_in, head_rise, head_fall)
        rise_normal = normed(rise_in.astype(jnp.float32), norm_row).astype(jnp.bfloat16)
        ring.held["rise"] = {0: [rise_normal]}
        for name in ("fall", "cot", "rise"):
            for distance in range(1 if name != "fall" else 2, far + 1):
                ring.gather(name, distance)
        groups = [[0, 1]] + [[distance] for distance in range(2, far + 1)]
        for group in groups:
            ring.prepare(group)
            ring.work("backward", group)
        for group in groups:
            ring.work("forward", group)
        for kind in ("backward", "forward"):
            for step in range(1, far + 1):
                ring.scatter(kind, step)
        fall_total = falling(kept).astype(jnp.bfloat16)
    layer_out = (rise_in.astype(jnp.float32) + ring.total("forward")).astype(jnp.bfloat16)
    return (layer_out[None], fall_total[None], exit_loss)


def solution(mesh):
    placed = (
        P(None, "ep", None),
        P("pipe", "ep", None),
        P("pipe", "ep", None),
        P("pipe", "ep", None),
        P(None, "ep", None),
        P("pipe", None),
        P("pipe", None),
        P("pipe", "ep", None, None),
        P("pipe", "ep", None, None),
        P("pipe", "ep", None, None),
        P(None, "pipe", "ep", None),
        P(None, "pipe", "ep", None),
        P(),
    )
    return jax.shard_map(
        local,
        mesh=mesh,
        in_specs=placed,
        out_specs=(P("pipe", "ep", None), P("pipe", "ep", None), P(None, "pipe", "ep")),
        check_vma=False,
    )
```

```python
import functools
import jax
import jax.numpy as jnp
from jax import lax
from jax.experimental import pallas as pl
from jax.experimental.pallas import tpu as pltpu
from jax.sharding import PartitionSpec as P

EPSILON = 1e-06
VMEM_LIMIT = 16 * 1024 * 1024
NT = (((1,), (1,)), ((), ()))


def passed_along(block, axis, distance):
    devices = range(lax.axis_size(axis))
    route = [(i - distance, i) for i in devices if i - distance in devices]
    return lax.ppermute(block, axis, route)


def normed(values, gain_row):
    return (
        values * lax.rsqrt(jnp.mean(values * values, axis=-1, keepdims=True) + EPSILON) * gain_row
    )


def norm_pullback(values, gain_row, upstream):
    _, pullback = jax.vjp(lambda argument: normed(argument, gain_row), values)
    return pullback(upstream)[0]


def norm_kernel(rows_ref, gain_ref, out_ref):
    out_ref[...] = normed(rows_ref[...].astype(jnp.float32), gain_ref[...]).astype(jnp.bfloat16)


def normed_rows(rows, gain_row):
    count, width = rows.shape
    return pl.pallas_call(
        norm_kernel,
        out_shape=jax.ShapeDtypeStruct((count, width), jnp.bfloat16),
        compiler_params=pltpu.CompilerParams(vmem_limit_bytes=VMEM_LIMIT),
        cost_estimate=pl.CostEstimate(flops=0, bytes_accessed=count * width * 4, transcendentals=0),
    )(*in_hbm([rows, gain_row]))


def pack_kernel(experts, rows_ref, ids_ref, gates_ref, out_ref):
    width = rows_ref.shape[1]
    out_ref[:, :width] = rows_ref[...]
    count, extra = rows_ref.shape[0], out_ref.shape[1] - width
    lane = lax.broadcasted_iota(jnp.int32, (count, extra), 1)
    table = jnp.zeros((count, extra), jnp.float32)
    for m in range(2):
        for k in range(ids_ref.shape[2]):
            place = ids_ref[m, :, k : k + 1] + 2 * m * experts
            gate = gates_ref[m, :, k : k + 1]
            high = gate.astype(jnp.bfloat16).astype(jnp.float32)
            table = jnp.where(lane == place, high, table)
            table = jnp.where(lane == place + experts, gate - high, table)
    out_ref[:, width:] = table.astype(jnp.bfloat16)


def packed_rows(rows, ids, gates, experts):
    count, width = rows.shape
    extra = -(-4 * experts // 128) * 128
    return pl.pallas_call(
        functools.partial(pack_kernel, experts),
        out_shape=jax.ShapeDtypeStruct((count, width + extra), jnp.bfloat16),
        compiler_params=pltpu.CompilerParams(vmem_limit_bytes=VMEM_LIMIT),
        cost_estimate=pl.CostEstimate(flops=0, bytes_accessed=count * width * 8, transcendentals=0),
    )(rows, ids, gates)


def gate_column(table, micro, experts, expert):
    lane = lax.broadcasted_iota(jnp.int32, table.shape, 1)
    place = 2 * micro * experts + expert
    chosen = (lane == place) | (lane == place + experts)
    return jnp.sum(jnp.where(chosen, table, 0.0), axis=1, keepdims=True)


def start_all(copies):
    for copy in copies:
        copy.start()


def wait_all(copies):
    for copy in copies:
        copy.wait()


def block_copies(sources, target, sems, columns=None):
    copies, start = [], 0
    for i, source in enumerate(sources):
        count = source.shape[0]
        view = source if columns is None else source.at[:, columns]
        copies.append(
            pltpu.make_async_copy(view, target.at[pl.ds(start, count)], sems.at[i])
        )
        start += count
    return copies


def write_tiles(tile, outs, columns):
    start = 0
    for out in outs:
        count = out.shape[0]
        out[:, columns] = tile[start : start + count].astype(out.dtype)
        start += count


def dot(first, second):
    return jnp.dot(first, second, preferred_element_type=jnp.float32)


def dot_nt(first, second):
    return lax.dot_general(first, second, NT, preferred_element_type=jnp.float32)


def forward_kernel(parts, experts, width, tile, names_ref, *refs):
    packed, rows = refs[:parts], refs[parts : 2 * parts]
    weights = refs[2 * parts : 2 * parts + 6]
    outs = refs[2 * parts + 6 : 3 * parts + 6]
    table, held, hidden, table_sem, row_sem = refs[3 * parts + 6 :]
    extra = table.shape[1]
    inner = weights[0].shape[1]
    copies = block_copies(rows, held, row_sem)
    copies += block_copies(packed, table, table_sem, pl.ds(width, extra))
    start_all(copies)
    wait_all(copies)
    for e in range(2):
        gate = gate_column(table[...].astype(jnp.float32), 0, experts, names_ref[e])
        first = dot(held[...], weights[3 * e][...])
        second = dot(held[...], weights[3 * e + 1][...])
        made = gate * (jax.nn.silu(first) * second)
        hidden[:, pl.ds(e * inner, inner)] = made.astype(jnp.bfloat16)

    @pl.loop(0, width // tile)
    def _(n):
        columns = pl.ds(pl.multiple_of(n * tile, tile), tile)
        total = dot(hidden[:, :inner], weights[2][:, columns])
        total = total + dot(hidden[:, inner:], weights[5][:, columns])
        write_tiles(total, outs, columns)


def factor_kernel(parts, *refs):
    rows, weights, out = refs[:parts], refs[parts : parts + 4], refs[parts + 4]
    held, row_sem = refs[parts + 5 :]
    copies = block_copies(rows, held, row_sem)
    start_all(copies)
    wait_all(copies)
    for e in range(2):
        first = dot(held[...], weights[2 * e][...])
        second = dot(held[...], weights[2 * e + 1][...])
        sigmoid_part = jax.nn.sigmoid(first)
        out[2 * e] = (
            second * sigmoid_part * (1.0 + first * (1.0 - sigmoid_part))
        ).astype(jnp.bfloat16)
        out[2 * e + 1] = (first * sigmoid_part).astype(jnp.bfloat16)


def backward_kernel(parts, experts, width, tile, pieces, names_ref, *refs):
    packed, factors = refs[:parts], refs[parts : parts + len(pieces)]
    weights = refs[parts + len(pieces) :][:6]
    outs = refs[parts + len(pieces) + 6 :][:parts]
    slot, grads = refs[2 * parts + len(pieces) + 6 :]
    for e in range(2):
        row = 0
        for block in packed:
            count = block.shape[0]
            table = block[:, width:].astype(jnp.float32)
            gate = gate_column(table, 1, experts, names_ref[e])
            made = gate * block[:, :width].astype(jnp.float32)
            slot[row : row + count] = made.astype(jnp.bfloat16)
            row += count
        back = dot_nt(slot[...], weights[3 * e + 2][...])
        row = 0
        for factor, (start, count) in zip(factors, pieces):
            part = back[row : row + count]
            for i in range(2):
                made = part * factor[2 * e + i, start : start + count].astype(jnp.float32)
                grads[2 * e + i, row : row + count] = made.astype(jnp.bfloat16)
            row += count

    @pl.loop(0, width // tile)
    def _(n):
        columns = pl.ds(pl.multiple_of(n * tile, tile), tile)
        total = None
        for e in range(2):
            for i in range(2):
                term = dot_nt(grads[2 * e + i], weights[3 * e + i][columns, :])
                total = term if total is None else total + term
        write_tiles(total, outs, columns)


HBM = pl.BlockSpec(memory_space=pl.ANY)
TILE = 512


WHOLE = pl.BlockSpec(memory_space=pltpu.VMEM)


def in_vmem(weights):
    return [pltpu.with_memory_space_constraint(weight, pltpu.VMEM) for weight in weights]


def in_hbm(blocks):
    return [pltpu.with_memory_space_constraint(block, pltpu.HBM) for block in blocks]


def fetch_kernel(count, *refs):
    sems = refs[2 * count]
    copies = [
        pltpu.make_async_copy(refs[i], refs[count + i], sems.at[i]) for i in range(count)
    ]
    start_all(copies)
    wait_all(copies)


def fetched(weights):
    count = len(weights)
    return tuple(
        pl.pallas_call(
            functools.partial(fetch_kernel, count),
            out_shape=[pltpu.VMEM(weight.shape, weight.dtype) for weight in weights],
            in_specs=[HBM] * count,
            out_specs=[WHOLE] * count,
            scratch_shapes=[pltpu.SemaphoreType.DMA((count,))],
            compiler_params=PARAMS,
            cost_estimate=pl.CostEstimate(
                flops=0, bytes_accessed=8 * 2**20, transcendentals=0
            ),
        )(*in_hbm(weights))
    )


def cost(units, rows, width, inner, fixed):
    return pl.CostEstimate(
        flops=2 * units * rows * width * inner + int(fixed * 1.1e15),
        bytes_accessed=12 * width * inner,
        transcendentals=2 * rows * inner,
    )


PARAMS = pltpu.CompilerParams(vmem_limit_bytes=VMEM_LIMIT)


def forward_call(names, packed, rows, weights, experts):
    parts = len(rows)
    counts = [block.shape[0] for block in rows]
    total, width = sum(counts), rows[0].shape[1]
    full, inner = packed[0].shape[1], weights[0].shape[1]
    out = pl.pallas_call(
        functools.partial(forward_kernel, parts, experts, width, TILE),
        out_shape=[jax.ShapeDtypeStruct((count, width), jnp.bfloat16) for count in counts],
        in_specs=[pl.BlockSpec(memory_space=pltpu.SMEM)] + [HBM] * (2 * parts) + [WHOLE] * 6,
        scratch_shapes=[
            pltpu.VMEM((total, full - width), jnp.bfloat16),
            pltpu.VMEM((total, width), jnp.bfloat16),
            pltpu.VMEM((total, 2 * inner), jnp.bfloat16),
        ]
        + [pltpu.SemaphoreType.DMA((parts,)) for _ in range(2)],
        compiler_params=PARAMS,
        cost_estimate=cost(6, total, width, inner, 6e-6),
    )(names, *packed, *rows, *in_vmem(weights))
    return list(out)


def factor_call(rows, weights):
    parts = len(rows)
    total, width = sum(block.shape[0] for block in rows), rows[0].shape[1]
    inner = weights[0].shape[1]
    return pl.pallas_call(
        functools.partial(factor_kernel, parts),
        out_shape=jax.ShapeDtypeStruct((4, total, inner), jnp.bfloat16),
        in_specs=[HBM] * parts + [WHOLE] * 4,
        scratch_shapes=[
            pltpu.VMEM((total, width), jnp.bfloat16),
            pltpu.SemaphoreType.DMA((parts,)),
        ],
        compiler_params=PARAMS,
        cost_estimate=cost(4, total, width, inner, 5e-6),
    )(*in_hbm(rows), *in_vmem([weights[i] for i in (0, 1, 3, 4)]))


def backward_call(names, packed, factors, pieces, weights, experts):
    parts = len(packed)
    counts = [block.shape[0] for block in packed]
    total = sum(counts)
    width, inner = weights[0].shape
    out = pl.pallas_call(
        functools.partial(backward_kernel, parts, experts, width, TILE, pieces),
        out_shape=[jax.ShapeDtypeStruct((count, width), jnp.bfloat16) for count in counts],
        in_specs=[pl.BlockSpec(memory_space=pltpu.SMEM)] + [WHOLE] * (parts + len(pieces) + 6),
        scratch_shapes=[
            pltpu.VMEM((total, width), jnp.bfloat16),
            pltpu.VMEM((4, total, inner), jnp.bfloat16),
        ],
        compiler_params=PARAMS,
        cost_estimate=cost(6, total, width, inner, 6e-6),
    )(names, *in_vmem(packed), *in_vmem(factors), *in_vmem(weights))
    return list(out)


def added(first, second):
    return (first.astype(jnp.float32) + second.astype(jnp.float32)).astype(jnp.bfloat16)


def joined(block, moved, way):
    if moved is None:
        return block
    half = moved.shape[0]
    if half == block.shape[0]:
        return added(block, moved)
    if way == 0:
        return jnp.concatenate([added(block[:half], moved), block[half:]])
    return jnp.concatenate([block[:half], added(block[half:], moved)])


class Section:
    def __init__(self, sources, names):
        self.sources = sources
        self.names = names
        self.chips = sources // 2
        self.far = self.chips // 2
        order = list(range(0, self.chips, 2)) + list(range(1, self.chips, 2))[::-1]
        following = {order[i]: order[(i + 1) % self.chips] for i in range(self.chips)}
        pairs = [(2 * a + core, 2 * b + core) for a, b in following.items() for core in range(2)]
        self.routes = (pairs, [(b, a) for a, b in pairs])
        self.swap = [(i, i ^ 1) for i in range(sources)]
        self.held, self.made, self.sums, self.starts = {}, {}, {}, {}
        self.weights = None

    def pass_on(self, block, way):
        return lax.ppermute(block, "ep", self.routes[way])

    def gather(self, name, distance, way=None):
        held = self.held[name]
        behind, ahead = held[distance - 1][0], held[distance - 1][-1]
        if distance == self.far and way is not None:
            held[distance] = [self.pass_on((behind, ahead)[way], way)]
            return
        if distance == self.far:
            half = behind.shape[0] // 2
            behind, ahead = behind[:half], ahead[half:]
        held[distance] = [self.pass_on(behind, 0), self.pass_on(ahead, 1)]

    def prepare(self, distances):
        blocks = [block for d in distances for block in self.held["fall"][d]]
        key, start = f"factors{distances[0]}", 0
        self.held[key] = {0: [factor_call(blocks, self.weights)]}
        for d in distances:
            count = sum(block.shape[0] for block in self.held["fall"][d])
            self.starts[d] = (key, start, count)
            start += count

    def work(self, kind, distances):
        packed = [block for d in distances for block in self.held["cot"][d]]
        if kind == "backward":
            runs = []
            for key, start, count in [self.starts[d] for d in distances]:
                if runs and runs[-1][0] == key and sum(runs[-1][1:]) == start:
                    runs[-1][2] += count
                else:
                    runs.append([key, start, count])
            factors = [self.held[key][0][0] for key, _, _ in runs]
            pieces = tuple((start, count) for _, start, count in runs)
            outs = backward_call(
                self.names, packed, factors, pieces, self.weights, self.sources
            )
        else:
            blocks = [block for d in distances for block in self.held["rise"][d]]
            outs = forward_call(self.names, packed, blocks, self.weights, self.sources)
        made = self.made.setdefault(kind, {})
        for d in distances:
            count = len(self.held["cot"][d])
            made[d], outs = outs[:count], outs[count:]

    def scatter(self, kind, step, way=None):
        distance = self.far + 1 - step
        pieces = self.made[kind].pop(distance)
        if step == 1 and len(pieces) == 1:
            half = pieces[0].shape[0] // 2
            if way is None:
                pieces = [pieces[0][:half], pieces[0][half:]]
            else:
                pieces = [pieces[0] if way == i else None for i in range(2)]
        elif step > 1:
            moved = self.sums[kind]
            pieces = [joined(pieces[1 - i], moved[i], i) for i in range(2)]
        self.sums[kind] = [
            None if piece is None else self.pass_on(piece, i) for i, piece in enumerate(pieces)
        ]

    def total(self, kind):
        pieces = self.made[kind][0] + self.sums[kind]
        return sum(piece.astype(jnp.float32) for piece in pieces)

    def fence(self, *others):
        state = (self.held, self.made, self.sums, others)
        state = lax.optimization_barrier(state)
        self.held, self.made, self.sums, others = state
        return others


def local(
    entering,
    rising_prev,
    falling_cot,
    falling_saved,
    targets,
    norm_gain,
    exit_gain,
    w_gate,
    w_up,
    w_down,
    route_ids,
    route_gates,
    exit_list,
):
    section_index = lax.axis_index("pipe")
    sections = lax.axis_size("pipe")
    sources = lax.axis_size("ep")
    here = lax.axis_index("ep")
    names = jnp.stack([here, here + 1 - 2 * (here % 2)]).astype(jnp.int32)
    norm_row = norm_gain[0]
    exit_row = exit_gain[0]
    ring = Section(sources, names)
    far = ring.far
    planned = far == 4

    fall_wide = falling_saved[0].astype(jnp.float32)
    fall_normal = normed_rows(falling_saved[0], norm_gain)
    fall_normal, leaving_cot, leaving_rise = lax.optimization_barrier(
        (fall_normal, falling_cot[0], rising_prev[0])
    )
    ring.held["fall"] = {0: [fall_normal]}
    ring.gather("fall", 1)
    moved_cot = passed_along(leaving_cot, "pipe", 1)
    own = (w_gate[0, 0], w_up[0, 0], w_down[0, 0])

    def swapped(weight):
        return lax.ppermute(weight, "ep", ring.swap)

    at_start = section_index == 0
    cot_in = jnp.where(at_start, entering[1], moved_cot)

    def entered(moved_rise):
        return jnp.where(at_start, entering[0], moved_rise)

    ring.held["cot"] = {0: [packed_rows(cot_in, route_ids[:, 0], route_gates[:, 0], sources)]}
    ring.held["rise"] = {}

    head_rise = jnp.take(exit_list[0], section_index).astype(jnp.float32)
    head_fall = jnp.take(exit_list[1], sections - 1 - section_index).astype(jnp.float32)

    def exit_heads(rise_in, cot_in, head_rise, head_fall):
        rise_wide = rise_in.astype(jnp.float32)
        rise_diff = normed(rise_wide, exit_row) - targets[0].astype(jnp.float32)
        loss_rise = head_rise * 0.5 * jnp.mean(rise_diff * rise_diff, axis=-1)
        fall_diff = normed(fall_wide, exit_row) - targets[1].astype(jnp.float32)
        loss_fall = head_fall * 0.5 * jnp.mean(fall_diff * fall_diff, axis=-1)
        kept = cot_in.astype(jnp.float32)
        kept = kept + head_fall * norm_pullback(fall_wide, exit_row, fall_diff)
        return kept, jnp.stack([loss_rise, loss_fall])[:, None, :]

    def falling(kept):
        return kept + norm_pullback(fall_wide, norm_row, ring.total("backward"))

    if planned:
        ring.gather("fall", 2)
        own_gate, own_up, own_down = own
        other_gate, other_up = swapped(own_gate), swapped(own_up)
        packed, leaving_rise = lax.optimization_barrier((ring.held["cot"][0][0], leaving_rise))
        ring.held["cot"][0] = [packed]
        moved_rise = passed_along(leaving_rise, "pipe", 1)
        heads = (head_rise, head_fall)
        cot_in, own, own_down, other_gate, other_up, heads, ring.names = ring.fence(
            cot_in, own, own_down, other_gate, other_up, heads, names
        )
        ring.gather("fall", 3)
        ring.gather("cot", 1)
        own = fetched(own)
        moved_rise, own, own_down = ring.fence(moved_rise, own, own_down)
        ring.gather("fall", 4)
        ring.gather("cot", 2)
        ring.weights = own + (other_gate, other_up, None)
        ring.prepare([0, 1, 2, 3])
        other_down = swapped(own_down)
        rise_in = entered(moved_rise)
        rise_normal = normed(rise_in.astype(jnp.float32), norm_row).astype(jnp.bfloat16)
        kept, exit_loss = exit_heads(rise_in, cot_in, *heads)
        rise_normal, kept, exit_loss, other_down = ring.fence(
            rise_normal, kept, exit_loss, other_down
        )
        ring.weights = own + (other_gate, other_up, other_down)
        ring.held["rise"] = {0: [rise_normal]}
        ring.gather("cot", 3)
        ring.gather("rise", 1)
        ring.work("backward", [0, 1, 2])
        ring.prepare([4])
        ring.fence()
        ring.gather("cot", 4)
        ring.gather("rise", 2)
        ring.work("forward", [0, 1])
        ring.fence()
        ring.gather("rise", 3)
        ring.work("backward", [3, 4])
        ring.fence()
        ring.gather("rise", 4)
        ring.scatter("backward", 1)
        ring.work("forward", [2])
        ring.fence()
        ring.scatter("backward", 2)
        ring.work("forward", [3, 4])
        ring.fence()
        ring.scatter("backward", 3)
        ring.scatter("forward", 1)
        ring.fence()
        ring.scatter("backward", 4)
        ring.scatter("forward", 2)
        ring.fence()
        ring.scatter("forward", 3)
        fall_total = falling(kept).astype(jnp.bfloat16)
        (fall_total,) = ring.fence(fall_total)
        ring.scatter("forward", 4)
    else:
        rise_in = entered(passed_along(leaving_rise, "pipe", 1))
        ring.weights = own + tuple(swapped(own))
        kept, exit_loss = exit_heads(rise_in, cot_in, head_rise, head_fall)
        rise_normal = normed(rise_in.astype(jnp.float32), norm_row).astype(jnp.bfloat16)
        ring.held["rise"] = {0: [rise_normal]}
        for name in ("fall", "cot", "rise"):
            for distance in range(1 if name != "fall" else 2, far + 1):
                ring.gather(name, distance)
        groups = [[0, 1]] + [[distance] for distance in range(2, far + 1)]
        for group in groups:
            ring.prepare(group)
            ring.work("backward", group)
        for group in groups:
            ring.work("forward", group)
        for kind in ("backward", "forward"):
            for step in range(1, far + 1):
                ring.scatter(kind, step)
        fall_total = falling(kept).astype(jnp.bfloat16)
    layer_out = (rise_in.astype(jnp.float32) + ring.total("forward")).astype(jnp.bfloat16)
    return (layer_out[None], fall_total[None], exit_loss)


def solution(mesh):
    placed = (
        P(None, "ep", None),
        P("pipe", "ep", None),
        P("pipe", "ep", None),
        P("pipe", "ep", None),
        P(None, "ep", None),
        P("pipe", None),
        P("pipe", None),
        P("pipe", "ep", None, None),
        P("pipe", "ep", None, None),
        P("pipe", "ep", None, None),
        P(None, "pipe", "ep", None),
        P(None, "pipe", "ep", None),
        P(),
    )
    return jax.shard_map(
        local,
        mesh=mesh,
        in_specs=placed,
        out_specs=(P("pipe", "ep", None), P("pipe", "ep", None), P(None, "pipe", "ep")),
        check_vma=False,
    )
```

```python
import functools
import jax
import jax.numpy as jnp
from jax import lax
from jax.experimental import pallas as pl
from jax.experimental.pallas import tpu as pltpu
from jax.sharding import PartitionSpec as P

EPSILON = 1e-06
VMEM_LIMIT = 16 * 1024 * 1024
NT = (((1,), (1,)), ((), ()))


def passed_along(block, axis, distance):
    devices = range(lax.axis_size(axis))
    route = [(i - distance, i) for i in devices if i - distance in devices]
    return lax.ppermute(block, axis, route)


def normed(values, gain_row):
    return (
        values * lax.rsqrt(jnp.mean(values * values, axis=-1, keepdims=True) + EPSILON) * gain_row
    )


def norm_pullback(values, gain_row, upstream):
    _, pullback = jax.vjp(lambda argument: normed(argument, gain_row), values)
    return pullback(upstream)[0]


def norm_kernel(rows_ref, gain_ref, out_ref):
    out_ref[...] = normed(rows_ref[...].astype(jnp.float32), gain_ref[...]).astype(jnp.bfloat16)


def normed_rows(rows, gain_row):
    count, width = rows.shape
    return pl.pallas_call(
        norm_kernel,
        out_shape=jax.ShapeDtypeStruct((count, width), jnp.bfloat16),
        compiler_params=pltpu.CompilerParams(vmem_limit_bytes=VMEM_LIMIT),
        cost_estimate=pl.CostEstimate(flops=0, bytes_accessed=count * width * 4, transcendentals=0),
    )(*in_hbm([rows, gain_row]))


def pack_kernel(experts, rows_ref, ids_ref, gates_ref, out_ref):
    width = rows_ref.shape[1]
    out_ref[:, :width] = rows_ref[...]
    count, extra = rows_ref.shape[0], out_ref.shape[1] - width
    lane = lax.broadcasted_iota(jnp.int32, (count, extra), 1)
    table = jnp.zeros((count, extra), jnp.float32)
    for m in range(2):
        for k in range(ids_ref.shape[2]):
            place = ids_ref[m, :, k : k + 1] + 2 * m * experts
            gate = gates_ref[m, :, k : k + 1]
            high = gate.astype(jnp.bfloat16).astype(jnp.float32)
            table = jnp.where(lane == place, high, table)
            table = jnp.where(lane == place + experts, gate - high, table)
    out_ref[:, width:] = table.astype(jnp.bfloat16)


def packed_rows(rows, ids, gates, experts):
    count, width = rows.shape
    extra = -(-4 * experts // 128) * 128
    return pl.pallas_call(
        functools.partial(pack_kernel, experts),
        out_shape=jax.ShapeDtypeStruct((count, width + extra), jnp.bfloat16),
        compiler_params=pltpu.CompilerParams(vmem_limit_bytes=VMEM_LIMIT),
        cost_estimate=pl.CostEstimate(flops=0, bytes_accessed=count * width * 8, transcendentals=0),
    )(rows, ids, gates)


def gate_column(table, micro, experts, expert):
    lane = lax.broadcasted_iota(jnp.int32, table.shape, 1)
    place = 2 * micro * experts + expert
    chosen = (lane == place) | (lane == place + experts)
    return jnp.sum(jnp.where(chosen, table, 0.0), axis=1, keepdims=True)


def start_all(copies):
    for copy in copies:
        copy.start()


def wait_all(copies):
    for copy in copies:
        copy.wait()


def block_copies(sources, target, sems, columns=None):
    copies, start = [], 0
    for i, source in enumerate(sources):
        count = source.shape[0]
        view = source if columns is None else source.at[:, columns]
        copies.append(
            pltpu.make_async_copy(view, target.at[pl.ds(start, count)], sems.at[i])
        )
        start += count
    return copies


def write_tiles(tile, outs, columns):
    start = 0
    for out in outs:
        count = out.shape[0]
        out[:, columns] = tile[start : start + count].astype(out.dtype)
        start += count


def dot(first, second):
    return jnp.dot(first, second, preferred_element_type=jnp.float32)


def dot_nt(first, second):
    return lax.dot_general(first, second, NT, preferred_element_type=jnp.float32)


def forward_kernel(parts, experts, width, tile, names_ref, *refs):
    packed, rows = refs[:parts], refs[parts : 2 * parts]
    weights = refs[2 * parts : 2 * parts + 6]
    outs = refs[2 * parts + 6 : 3 * parts + 6]
    table, held, hidden, table_sem, row_sem = refs[3 * parts + 6 :]
    extra = table.shape[1]
    inner = weights[0].shape[1]
    copies = block_copies(rows, held, row_sem)
    copies += block_copies(packed, table, table_sem, pl.ds(width, extra))
    start_all(copies)
    wait_all(copies)
    for e in range(2):
        gate = gate_column(table[...].astype(jnp.float32), 0, experts, names_ref[e])
        first = dot(held[...], weights[3 * e][...])
        second = dot(held[...], weights[3 * e + 1][...])
        made = gate * (jax.nn.silu(first) * second)
        hidden[:, pl.ds(e * inner, inner)] = made.astype(jnp.bfloat16)

    @pl.loop(0, width // tile)
    def _(n):
        columns = pl.ds(pl.multiple_of(n * tile, tile), tile)
        total = dot(hidden[:, :inner], weights[2][:, columns])
        total = total + dot(hidden[:, inner:], weights[5][:, columns])
        write_tiles(total, outs, columns)


def factor_kernel(parts, *refs):
    rows, weights, out = refs[:parts], refs[parts : parts + 4], refs[parts + 4]
    held, row_sem = refs[parts + 5 :]
    copies = block_copies(rows, held, row_sem)
    start_all(copies)
    wait_all(copies)
    for e in range(2):
        first = dot(held[...], weights[2 * e][...])
        second = dot(held[...], weights[2 * e + 1][...])
        sigmoid_part = jax.nn.sigmoid(first)
        out[2 * e] = (
            second * sigmoid_part * (1.0 + first * (1.0 - sigmoid_part))
        ).astype(jnp.bfloat16)
        out[2 * e + 1] = (first * sigmoid_part).astype(jnp.bfloat16)


def backward_kernel(parts, experts, width, tile, pieces, names_ref, *refs):
    packed, factors = refs[:parts], refs[parts : parts + len(pieces)]
    weights = refs[parts + len(pieces) :][:6]
    outs = refs[parts + len(pieces) + 6 :][:parts]
    slot, grads = refs[2 * parts + len(pieces) + 6 :]
    for e in range(2):
        row = 0
        for block in packed:
            count = block.shape[0]
            table = block[:, width:].astype(jnp.float32)
            gate = gate_column(table, 1, experts, names_ref[e])
            made = gate * block[:, :width].astype(jnp.float32)
            slot[row : row + count] = made.astype(jnp.bfloat16)
            row += count
        back = dot_nt(slot[...], weights[3 * e + 2][...])
        row = 0
        for factor, (start, count) in zip(factors, pieces):
            part = back[row : row + count]
            for i in range(2):
                made = part * factor[2 * e + i, start : start + count].astype(jnp.float32)
                grads[2 * e + i, row : row + count] = made.astype(jnp.bfloat16)
            row += count

    @pl.loop(0, width // tile)
    def _(n):
        columns = pl.ds(pl.multiple_of(n * tile, tile), tile)
        total = None
        for e in range(2):
            for i in range(2):
                term = dot_nt(grads[2 * e + i], weights[3 * e + i][columns, :])
                total = term if total is None else total + term
        write_tiles(total, outs, columns)


HBM = pl.BlockSpec(memory_space=pl.ANY)
TILE = 512


WHOLE = pl.BlockSpec(memory_space=pltpu.VMEM)


def in_vmem(weights):
    return [pltpu.with_memory_space_constraint(weight, pltpu.VMEM) for weight in weights]


def in_hbm(blocks):
    return [pltpu.with_memory_space_constraint(block, pltpu.HBM) for block in blocks]


def fetch_kernel(count, *refs):
    sems = refs[2 * count]
    copies = [
        pltpu.make_async_copy(refs[i], refs[count + i], sems.at[i]) for i in range(count)
    ]
    start_all(copies)
    wait_all(copies)


def fetched(weights):
    count = len(weights)
    return tuple(
        pl.pallas_call(
            functools.partial(fetch_kernel, count),
            out_shape=[pltpu.VMEM(weight.shape, weight.dtype) for weight in weights],
            in_specs=[HBM] * count,
            out_specs=[WHOLE] * count,
            scratch_shapes=[pltpu.SemaphoreType.DMA((count,))],
            compiler_params=PARAMS,
            cost_estimate=pl.CostEstimate(
                flops=0, bytes_accessed=8 * 2**20, transcendentals=0
            ),
        )(*in_hbm(weights))
    )


def cost(units, rows, width, inner, fixed):
    return pl.CostEstimate(
        flops=2 * units * rows * width * inner + int(fixed * 1.1e15),
        bytes_accessed=12 * width * inner,
        transcendentals=2 * rows * inner,
    )


PARAMS = pltpu.CompilerParams(vmem_limit_bytes=VMEM_LIMIT)


def forward_call(names, packed, rows, weights, experts):
    parts = len(rows)
    counts = [block.shape[0] for block in rows]
    total, width = sum(counts), rows[0].shape[1]
    full, inner = packed[0].shape[1], weights[0].shape[1]
    out = pl.pallas_call(
        functools.partial(forward_kernel, parts, experts, width, TILE),
        out_shape=[jax.ShapeDtypeStruct((count, width), jnp.bfloat16) for count in counts],
        in_specs=[pl.BlockSpec(memory_space=pltpu.SMEM)] + [HBM] * (2 * parts) + [WHOLE] * 6,
        scratch_shapes=[
            pltpu.VMEM((total, full - width), jnp.bfloat16),
            pltpu.VMEM((total, width), jnp.bfloat16),
            pltpu.VMEM((total, 2 * inner), jnp.bfloat16),
        ]
        + [pltpu.SemaphoreType.DMA((parts,)) for _ in range(2)],
        compiler_params=PARAMS,
        cost_estimate=cost(6, total, width, inner, 6e-6),
    )(names, *packed, *rows, *in_vmem(weights))
    return list(out)


def factor_call(rows, weights):
    parts = len(rows)
    total, width = sum(block.shape[0] for block in rows), rows[0].shape[1]
    inner = weights[0].shape[1]
    return pl.pallas_call(
        functools.partial(factor_kernel, parts),
        out_shape=jax.ShapeDtypeStruct((4, total, inner), jnp.bfloat16),
        in_specs=[HBM] * parts + [WHOLE] * 4,
        scratch_shapes=[
            pltpu.VMEM((total, width), jnp.bfloat16),
            pltpu.SemaphoreType.DMA((parts,)),
        ],
        compiler_params=PARAMS,
        cost_estimate=cost(4, total, width, inner, 5e-6),
    )(*in_hbm(rows), *in_vmem([weights[i] for i in (0, 1, 3, 4)]))


def backward_call(names, packed, factors, pieces, weights, experts):
    parts = len(packed)
    counts = [block.shape[0] for block in packed]
    total = sum(counts)
    width, inner = weights[0].shape
    out = pl.pallas_call(
        functools.partial(backward_kernel, parts, experts, width, TILE, pieces),
        out_shape=[jax.ShapeDtypeStruct((count, width), jnp.bfloat16) for count in counts],
        in_specs=[pl.BlockSpec(memory_space=pltpu.SMEM)] + [WHOLE] * (parts + len(pieces) + 6),
        scratch_shapes=[
            pltpu.VMEM((total, width), jnp.bfloat16),
            pltpu.VMEM((4, total, inner), jnp.bfloat16),
        ],
        compiler_params=PARAMS,
        cost_estimate=cost(6, total, width, inner, 6e-6),
    )(names, *in_vmem(packed), *in_vmem(factors), *in_vmem(weights))
    return list(out)


def added(first, second):
    return (first.astype(jnp.float32) + second.astype(jnp.float32)).astype(jnp.bfloat16)


def joined(block, moved, way):
    if moved is None:
        return block
    half = moved.shape[0]
    if half == block.shape[0]:
        return added(block, moved)
    if way == 0:
        return jnp.concatenate([added(block[:half], moved), block[half:]])
    return jnp.concatenate([block[:half], added(block[half:], moved)])


class Section:
    def __init__(self, sources, names):
        self.sources = sources
        self.names = names
        self.chips = sources // 2
        self.far = self.chips // 2
        order = list(range(0, self.chips, 2)) + list(range(1, self.chips, 2))[::-1]
        following = {order[i]: order[(i + 1) % self.chips] for i in range(self.chips)}
        pairs = [(2 * a + core, 2 * b + core) for a, b in following.items() for core in range(2)]
        self.routes = (pairs, [(b, a) for a, b in pairs])
        self.swap = [(i, i ^ 1) for i in range(sources)]
        self.held, self.made, self.sums, self.starts = {}, {}, {}, {}
        self.weights = None

    def pass_on(self, block, way):
        return lax.ppermute(block, "ep", self.routes[way])

    def gather(self, name, distance, way=None):
        held = self.held[name]
        behind, ahead = held[distance - 1][0], held[distance - 1][-1]
        if distance == self.far and way is not None:
            held[distance] = [self.pass_on((behind, ahead)[way], way)]
            return
        if distance == self.far:
            half = behind.shape[0] // 2
            behind, ahead = behind[:half], ahead[half:]
        held[distance] = [self.pass_on(behind, 0), self.pass_on(ahead, 1)]

    def prepare(self, distances):
        blocks = [block for d in distances for block in self.held["fall"][d]]
        key, start = f"factors{distances[0]}", 0
        self.held[key] = {0: [factor_call(blocks, self.weights)]}
        for d in distances:
            count = sum(block.shape[0] for block in self.held["fall"][d])
            self.starts[d] = (key, start, count)
            start += count

    def work(self, kind, distances):
        packed = [block for d in distances for block in self.held["cot"][d]]
        if kind == "backward":
            runs = []
            for key, start, count in [self.starts[d] for d in distances]:
                if runs and runs[-1][0] == key and sum(runs[-1][1:]) == start:
                    runs[-1][2] += count
                else:
                    runs.append([key, start, count])
            factors = [self.held[key][0][0] for key, _, _ in runs]
            pieces = tuple((start, count) for _, start, count in runs)
            outs = backward_call(
                self.names, packed, factors, pieces, self.weights, self.sources
            )
        else:
            blocks = [block for d in distances for block in self.held["rise"][d]]
            outs = forward_call(self.names, packed, blocks, self.weights, self.sources)
        made = self.made.setdefault(kind, {})
        for d in distances:
            count = len(self.held["cot"][d])
            made[d], outs = outs[:count], outs[count:]

    def scatter(self, kind, step, way=None):
        distance = self.far + 1 - step
        pieces = self.made[kind].pop(distance)
        if step == 1 and len(pieces) == 1:
            half = pieces[0].shape[0] // 2
            if way is None:
                pieces = [pieces[0][:half], pieces[0][half:]]
            else:
                pieces = [pieces[0] if way == i else None for i in range(2)]
        elif step > 1:
            moved = self.sums[kind]
            pieces = [joined(pieces[1 - i], moved[i], i) for i in range(2)]
        self.sums[kind] = [
            None if piece is None else self.pass_on(piece, i) for i, piece in enumerate(pieces)
        ]

    def total(self, kind):
        pieces = self.made[kind][0] + self.sums[kind]
        return sum(piece.astype(jnp.float32) for piece in pieces)

    def fence(self, *others):
        state = (self.held, self.made, self.sums, others)
        state = lax.optimization_barrier(state)
        self.held, self.made, self.sums, others = state
        return others


def local(
    entering,
    rising_prev,
    falling_cot,
    falling_saved,
    targets,
    norm_gain,
    exit_gain,
    w_gate,
    w_up,
    w_down,
    route_ids,
    route_gates,
    exit_list,
):
    section_index = lax.axis_index("pipe")
    sections = lax.axis_size("pipe")
    sources = lax.axis_size("ep")
    here = lax.axis_index("ep")
    names = jnp.stack([here, here + 1 - 2 * (here % 2)]).astype(jnp.int32)
    norm_row = norm_gain[0]
    exit_row = exit_gain[0]
    ring = Section(sources, names)
    far = ring.far
    planned = far == 4

    fall_wide = falling_saved[0].astype(jnp.float32)
    fall_normal = normed_rows(falling_saved[0], norm_gain)
    fall_normal, leaving_cot, leaving_rise = lax.optimization_barrier(
        (fall_normal, falling_cot[0], rising_prev[0])
    )
    ring.held["fall"] = {0: [fall_normal]}
    ring.gather("fall", 1)
    moved_cot = passed_along(leaving_cot, "pipe", 1)
    own = (w_gate[0, 0], w_up[0, 0], w_down[0, 0])

    def swapped(weight):
        return lax.ppermute(weight, "ep", ring.swap)

    at_start = section_index == 0
    cot_in = jnp.where(at_start, entering[1], moved_cot)

    def entered(moved_rise):
        return jnp.where(at_start, entering[0], moved_rise)

    ring.held["cot"] = {0: [packed_rows(cot_in, route_ids[:, 0], route_gates[:, 0], sources)]}
    ring.held["rise"] = {}

    head_rise = jnp.take(exit_list[0], section_index).astype(jnp.float32)
    head_fall = jnp.take(exit_list[1], sections - 1 - section_index).astype(jnp.float32)

    def exit_heads(rise_in, cot_in, head_rise, head_fall):
        rise_wide = rise_in.astype(jnp.float32)
        rise_diff = normed(rise_wide, exit_row) - targets[0].astype(jnp.float32)
        loss_rise = head_rise * 0.5 * jnp.mean(rise_diff * rise_diff, axis=-1)
        fall_diff = normed(fall_wide, exit_row) - targets[1].astype(jnp.float32)
        loss_fall = head_fall * 0.5 * jnp.mean(fall_diff * fall_diff, axis=-1)
        kept = cot_in.astype(jnp.float32)
        kept = kept + head_fall * norm_pullback(fall_wide, exit_row, fall_diff)
        return kept, jnp.stack([loss_rise, loss_fall])[:, None, :]

    def falling(kept):
        return kept + norm_pullback(fall_wide, norm_row, ring.total("backward"))

    if planned:
        ring.gather("fall", 2)
        own_gate, own_up, own_down = own
        other_gate, other_up = swapped(own_gate), swapped(own_up)
        packed, leaving_rise = lax.optimization_barrier((ring.held["cot"][0][0], leaving_rise))
        ring.held["cot"][0] = [packed]
        moved_rise = passed_along(leaving_rise, "pipe", 1)
        heads = (head_rise, head_fall)
        cot_in, own, own_down, other_gate, other_up, heads, ring.names = ring.fence(
            cot_in, own, own_down, other_gate, other_up, heads, names
        )
        ring.gather("fall", 3)
        ring.gather("cot", 1)
        own = fetched(own)
        ring.weights = own + (other_gate, other_up, None)
        ring.prepare([0, 1, 2])
        moved_rise, own, own_down = ring.fence(moved_rise, own, own_down)
        ring.gather("fall", 4)
        ring.gather("cot", 2)
        other_down = swapped(own_down)
        rise_in = entered(moved_rise)
        rise_normal = normed(rise_in.astype(jnp.float32), norm_row).astype(jnp.bfloat16)
        kept, exit_loss = exit_heads(rise_in, cot_in, *heads)
        rise_normal, kept, exit_loss, other_down = ring.fence(
            rise_normal, kept, exit_loss, other_down
        )
        ring.weights = own + (other_gate, other_up, other_down)
        ring.held["rise"] = {0: [rise_normal]}
        ring.gather("cot", 3)
        ring.gather("rise", 1)
        ring.work("backward", [0, 1, 2])
        ring.prepare([3, 4])
        ring.fence()
        ring.gather("cot", 4)
        ring.gather("rise", 2)
        ring.work("forward", [0, 1])
        ring.fence()
        ring.gather("rise", 3)
        ring.work("backward", [3, 4])
        ring.fence()
        ring.gather("rise", 4)
        ring.scatter("backward", 1)
        ring.work("forward", [2])
        ring.fence()
        ring.scatter("backward", 2)
        ring.work("forward", [3, 4])
        ring.fence()
        ring.scatter("backward", 3)
        ring.scatter("forward", 1)
        ring.fence()
        ring.scatter("backward", 4)
        ring.scatter("forward", 2)
        ring.fence()
        ring.scatter("forward", 3)
        fall_total = falling(kept).astype(jnp.bfloat16)
        (fall_total,) = ring.fence(fall_total)
        ring.scatter("forward", 4)
    else:
        rise_in = entered(passed_along(leaving_rise, "pipe", 1))
        ring.weights = own + tuple(swapped(own))
        kept, exit_loss = exit_heads(rise_in, cot_in, head_rise, head_fall)
        rise_normal = normed(rise_in.astype(jnp.float32), norm_row).astype(jnp.bfloat16)
        ring.held["rise"] = {0: [rise_normal]}
        for name in ("fall", "cot", "rise"):
            for distance in range(1 if name != "fall" else 2, far + 1):
                ring.gather(name, distance)
        groups = [[0, 1]] + [[distance] for distance in range(2, far + 1)]
        for group in groups:
            ring.prepare(group)
            ring.work("backward", group)
        for group in groups:
            ring.work("forward", group)
        for kind in ("backward", "forward"):
            for step in range(1, far + 1):
                ring.scatter(kind, step)
        fall_total = falling(kept).astype(jnp.bfloat16)
    layer_out = (rise_in.astype(jnp.float32) + ring.total("forward")).astype(jnp.bfloat16)
    return (layer_out[None], fall_total[None], exit_loss)


def solution(mesh):
    placed = (
        P(None, "ep", None),
        P("pipe", "ep", None),
        P("pipe", "ep", None),
        P("pipe", "ep", None),
        P(None, "ep", None),
        P("pipe", None),
        P("pipe", None),
        P("pipe", "ep", None, None),
        P("pipe", "ep", None, None),
        P("pipe", "ep", None, None),
        P(None, "pipe", "ep", None),
        P(None, "pipe", "ep", None),
        P(),
    )
    return jax.shard_map(
        local,
        mesh=mesh,
        in_specs=placed,
        out_specs=(P("pipe", "ep", None), P("pipe", "ep", None), P(None, "pipe", "ep")),
        check_vma=False,
    )
```

```python
import functools
import jax
import jax.numpy as jnp
from jax import lax
from jax.experimental import pallas as pl
from jax.experimental.pallas import tpu as pltpu
from jax.sharding import PartitionSpec as P

EPSILON = 1e-06
VMEM_LIMIT = 16 * 1024 * 1024
NT = (((1,), (1,)), ((), ()))


def passed_along(block, axis, distance):
    devices = range(lax.axis_size(axis))
    route = [(i - distance, i) for i in devices if i - distance in devices]
    return lax.ppermute(block, axis, route)


def normed(values, gain_row):
    return (
        values * lax.rsqrt(jnp.mean(values * values, axis=-1, keepdims=True) + EPSILON) * gain_row
    )


def norm_pullback(values, gain_row, upstream):
    _, pullback = jax.vjp(lambda argument: normed(argument, gain_row), values)
    return pullback(upstream)[0]


def norm_kernel(rows_ref, gain_ref, out_ref):
    out_ref[...] = normed(rows_ref[...].astype(jnp.float32), gain_ref[...]).astype(jnp.bfloat16)


def normed_rows(rows, gain_row):
    count, width = rows.shape
    return pl.pallas_call(
        norm_kernel,
        out_shape=jax.ShapeDtypeStruct((count, width), jnp.bfloat16),
        compiler_params=pltpu.CompilerParams(vmem_limit_bytes=VMEM_LIMIT),
        cost_estimate=pl.CostEstimate(flops=0, bytes_accessed=count * width * 4, transcendentals=0),
    )(*in_hbm([rows, gain_row]))


def pack_kernel(experts, rows_ref, ids_ref, gates_ref, out_ref):
    width = rows_ref.shape[1]
    out_ref[:, :width] = rows_ref[...]
    count, extra = rows_ref.shape[0], out_ref.shape[1] - width
    lane = lax.broadcasted_iota(jnp.int32, (count, extra), 1)
    table = jnp.zeros((count, extra), jnp.float32)
    for m in range(2):
        for k in range(ids_ref.shape[2]):
            place = ids_ref[m, :, k : k + 1] + 2 * m * experts
            gate = gates_ref[m, :, k : k + 1]
            high = gate.astype(jnp.bfloat16).astype(jnp.float32)
            table = jnp.where(lane == place, high, table)
            table = jnp.where(lane == place + experts, gate - high, table)
    out_ref[:, width:] = table.astype(jnp.bfloat16)


def packed_rows(rows, ids, gates, experts):
    count, width = rows.shape
    extra = -(-4 * experts // 128) * 128
    return pl.pallas_call(
        functools.partial(pack_kernel, experts),
        out_shape=jax.ShapeDtypeStruct((count, width + extra), jnp.bfloat16),
        compiler_params=pltpu.CompilerParams(vmem_limit_bytes=VMEM_LIMIT),
        cost_estimate=pl.CostEstimate(flops=0, bytes_accessed=count * width * 8, transcendentals=0),
    )(rows, ids, gates)


def gate_column(table, micro, experts, expert):
    lane = lax.broadcasted_iota(jnp.int32, table.shape, 1)
    place = 2 * micro * experts + expert
    chosen = (lane == place) | (lane == place + experts)
    return jnp.sum(jnp.where(chosen, table, 0.0), axis=1, keepdims=True)


def start_all(copies):
    for copy in copies:
        copy.start()


def wait_all(copies):
    for copy in copies:
        copy.wait()


def block_copies(sources, target, sems, columns=None):
    copies, start = [], 0
    for i, source in enumerate(sources):
        count = source.shape[0]
        view = source if columns is None else source.at[:, columns]
        copies.append(
            pltpu.make_async_copy(view, target.at[pl.ds(start, count)], sems.at[i])
        )
        start += count
    return copies


def write_tiles(tile, outs, columns):
    start = 0
    for out in outs:
        count = out.shape[0]
        out[:, columns] = tile[start : start + count].astype(out.dtype)
        start += count


def dot(first, second):
    return jnp.dot(first, second, preferred_element_type=jnp.float32)


def dot_nt(first, second):
    return lax.dot_general(first, second, NT, preferred_element_type=jnp.float32)


def forward_kernel(parts, experts, width, tile, names_ref, *refs):
    packed, rows = refs[:parts], refs[parts : 2 * parts]
    weights = refs[2 * parts : 2 * parts + 6]
    outs = refs[2 * parts + 6 : 3 * parts + 6]
    table, held, hidden, table_sem, row_sem = refs[3 * parts + 6 :]
    extra = table.shape[1]
    inner = weights[0].shape[1]
    copies = block_copies(rows, held, row_sem)
    copies += block_copies(packed, table, table_sem, pl.ds(width, extra))
    start_all(copies)
    wait_all(copies)
    for e in range(2):
        gate = gate_column(table[...].astype(jnp.float32), 0, experts, names_ref[e])
        first = dot(held[...], weights[3 * e][...])
        second = dot(held[...], weights[3 * e + 1][...])
        made = gate * (jax.nn.silu(first) * second)
        hidden[:, pl.ds(e * inner, inner)] = made.astype(jnp.bfloat16)

    @pl.loop(0, width // tile)
    def _(n):
        columns = pl.ds(pl.multiple_of(n * tile, tile), tile)
        total = dot(hidden[:, :inner], weights[2][:, columns])
        total = total + dot(hidden[:, inner:], weights[5][:, columns])
        write_tiles(total, outs, columns)


def factor_kernel(parts, *refs):
    rows, weights, out = refs[:parts], refs[parts : parts + 4], refs[parts + 4]
    held, row_sem = refs[parts + 5 :]
    copies = block_copies(rows, held, row_sem)
    start_all(copies)
    wait_all(copies)
    for e in range(2):
        first = dot(held[...], weights[2 * e][...])
        second = dot(held[...], weights[2 * e + 1][...])
        sigmoid_part = jax.nn.sigmoid(first)
        out[2 * e] = (
            second * sigmoid_part * (1.0 + first * (1.0 - sigmoid_part))
        ).astype(jnp.bfloat16)
        out[2 * e + 1] = (first * sigmoid_part).astype(jnp.bfloat16)


def backward_kernel(parts, experts, width, tile, pieces, names_ref, *refs):
    packed, factors = refs[:parts], refs[parts : parts + len(pieces)]
    weights = refs[parts + len(pieces) :][:6]
    outs = refs[parts + len(pieces) + 6 :][:parts]
    slot, grads = refs[2 * parts + len(pieces) + 6 :]
    for e in range(2):
        row = 0
        for block in packed:
            count = block.shape[0]
            table = block[:, width:].astype(jnp.float32)
            gate = gate_column(table, 1, experts, names_ref[e])
            made = gate * block[:, :width].astype(jnp.float32)
            slot[row : row + count] = made.astype(jnp.bfloat16)
            row += count
        back = dot_nt(slot[...], weights[3 * e + 2][...])
        row = 0
        for factor, (start, count) in zip(factors, pieces):
            part = back[row : row + count]
            for i in range(2):
                made = part * factor[2 * e + i, start : start + count].astype(jnp.float32)
                grads[2 * e + i, row : row + count] = made.astype(jnp.bfloat16)
            row += count

    @pl.loop(0, width // tile)
    def _(n):
        columns = pl.ds(pl.multiple_of(n * tile, tile), tile)
        total = None
        for e in range(2):
            for i in range(2):
                term = dot_nt(grads[2 * e + i], weights[3 * e + i][columns, :])
                total = term if total is None else total + term
        write_tiles(total, outs, columns)


HBM = pl.BlockSpec(memory_space=pl.ANY)
TILE = 512


WHOLE = pl.BlockSpec(memory_space=pltpu.VMEM)


def in_vmem(weights):
    return [pltpu.with_memory_space_constraint(weight, pltpu.VMEM) for weight in weights]


def in_hbm(blocks):
    return [pltpu.with_memory_space_constraint(block, pltpu.HBM) for block in blocks]


def fetch_kernel(count, *refs):
    sems = refs[2 * count]
    copies = [
        pltpu.make_async_copy(refs[i], refs[count + i], sems.at[i]) for i in range(count)
    ]
    start_all(copies)
    wait_all(copies)


def fetched(weights):
    count = len(weights)
    return tuple(
        pl.pallas_call(
            functools.partial(fetch_kernel, count),
            out_shape=[pltpu.VMEM(weight.shape, weight.dtype) for weight in weights],
            in_specs=[HBM] * count,
            out_specs=[WHOLE] * count,
            scratch_shapes=[pltpu.SemaphoreType.DMA((count,))],
            compiler_params=PARAMS,
            cost_estimate=pl.CostEstimate(
                flops=0, bytes_accessed=8 * 2**20, transcendentals=0
            ),
        )(*in_hbm(weights))
    )


def cost(units, rows, width, inner, fixed):
    return pl.CostEstimate(
        flops=2 * units * rows * width * inner + int(fixed * 1.1e15),
        bytes_accessed=12 * width * inner,
        transcendentals=2 * rows * inner,
    )


PARAMS = pltpu.CompilerParams(vmem_limit_bytes=VMEM_LIMIT)


def forward_call(names, packed, rows, weights, experts):
    parts = len(rows)
    counts = [block.shape[0] for block in rows]
    total, width = sum(counts), rows[0].shape[1]
    full, inner = packed[0].shape[1], weights[0].shape[1]
    out = pl.pallas_call(
        functools.partial(forward_kernel, parts, experts, width, TILE),
        out_shape=[jax.ShapeDtypeStruct((count, width), jnp.bfloat16) for count in counts],
        in_specs=[pl.BlockSpec(memory_space=pltpu.SMEM)] + [HBM] * (2 * parts) + [WHOLE] * 6,
        scratch_shapes=[
            pltpu.VMEM((total, full - width), jnp.bfloat16),
            pltpu.VMEM((total, width), jnp.bfloat16),
            pltpu.VMEM((total, 2 * inner), jnp.bfloat16),
        ]
        + [pltpu.SemaphoreType.DMA((parts,)) for _ in range(2)],
        compiler_params=PARAMS,
        cost_estimate=cost(6, total, width, inner, 6e-6),
    )(names, *packed, *rows, *in_vmem(weights))
    return list(out)


def factor_call(rows, weights):
    parts = len(rows)
    total, width = sum(block.shape[0] for block in rows), rows[0].shape[1]
    inner = weights[0].shape[1]
    return pl.pallas_call(
        functools.partial(factor_kernel, parts),
        out_shape=jax.ShapeDtypeStruct((4, total, inner), jnp.bfloat16),
        in_specs=[HBM] * parts + [WHOLE] * 4,
        scratch_shapes=[
            pltpu.VMEM((total, width), jnp.bfloat16),
            pltpu.SemaphoreType.DMA((parts,)),
        ],
        compiler_params=PARAMS,
        cost_estimate=cost(4, total, width, inner, 5e-6),
    )(*in_hbm(rows), *in_vmem([weights[i] for i in (0, 1, 3, 4)]))


def backward_call(names, packed, factors, pieces, weights, experts):
    parts = len(packed)
    counts = [block.shape[0] for block in packed]
    total = sum(counts)
    width, inner = weights[0].shape
    out = pl.pallas_call(
        functools.partial(backward_kernel, parts, experts, width, TILE, pieces),
        out_shape=[jax.ShapeDtypeStruct((count, width), jnp.bfloat16) for count in counts],
        in_specs=[pl.BlockSpec(memory_space=pltpu.SMEM)] + [WHOLE] * (parts + len(pieces) + 6),
        scratch_shapes=[
            pltpu.VMEM((total, width), jnp.bfloat16),
            pltpu.VMEM((4, total, inner), jnp.bfloat16),
        ],
        compiler_params=PARAMS,
        cost_estimate=cost(6, total, width, inner, 6e-6),
    )(names, *in_vmem(packed), *in_vmem(factors), *in_vmem(weights))
    return list(out)


def added(first, second):
    return (first.astype(jnp.float32) + second.astype(jnp.float32)).astype(jnp.bfloat16)


def joined(block, moved, way):
    if moved is None:
        return block
    half = moved.shape[0]
    if half == block.shape[0]:
        return added(block, moved)
    if way == 0:
        return jnp.concatenate([added(block[:half], moved), block[half:]])
    return jnp.concatenate([block[:half], added(block[half:], moved)])


class Section:
    def __init__(self, sources, names):
        self.sources = sources
        self.names = names
        self.chips = sources // 2
        self.far = self.chips // 2
        order = list(range(0, self.chips, 2)) + list(range(1, self.chips, 2))[::-1]
        following = {order[i]: order[(i + 1) % self.chips] for i in range(self.chips)}
        pairs = [(2 * a + core, 2 * b + core) for a, b in following.items() for core in range(2)]
        self.routes = (pairs, [(b, a) for a, b in pairs])
        self.swap = [(i, i ^ 1) for i in range(sources)]
        self.held, self.made, self.sums, self.starts = {}, {}, {}, {}
        self.weights = None

    def pass_on(self, block, way):
        return lax.ppermute(block, "ep", self.routes[way])

    def gather(self, name, distance, way=None):
        held = self.held[name]
        behind, ahead = held[distance - 1][0], held[distance - 1][-1]
        if distance == self.far and way is not None:
            held[distance] = [self.pass_on((behind, ahead)[way], way)]
            return
        if distance == self.far:
            half = behind.shape[0] // 2
            behind, ahead = behind[:half], ahead[half:]
        held[distance] = [self.pass_on(behind, 0), self.pass_on(ahead, 1)]

    def prepare(self, distances):
        blocks = [block for d in distances for block in self.held["fall"][d]]
        key, start = f"factors{distances[0]}", 0
        self.held[key] = {0: [factor_call(blocks, self.weights)]}
        for d in distances:
            count = sum(block.shape[0] for block in self.held["fall"][d])
            self.starts[d] = (key, start, count)
            start += count

    def work(self, kind, distances):
        packed = [block for d in distances for block in self.held["cot"][d]]
        if kind == "backward":
            runs = []
            for key, start, count in [self.starts[d] for d in distances]:
                if runs and runs[-1][0] == key and sum(runs[-1][1:]) == start:
                    runs[-1][2] += count
                else:
                    runs.append([key, start, count])
            factors = [self.held[key][0][0] for key, _, _ in runs]
            pieces = tuple((start, count) for _, start, count in runs)
            outs = backward_call(
                self.names, packed, factors, pieces, self.weights, self.sources
            )
        else:
            blocks = [block for d in distances for block in self.held["rise"][d]]
            outs = forward_call(self.names, packed, blocks, self.weights, self.sources)
        made = self.made.setdefault(kind, {})
        for d in distances:
            count = len(self.held["cot"][d])
            made[d], outs = outs[:count], outs[count:]

    def scatter(self, kind, step, way=None):
        distance = self.far + 1 - step
        pieces = self.made[kind].pop(distance)
        if step == 1 and len(pieces) == 1:
            half = pieces[0].shape[0] // 2
            if way is None:
                pieces = [pieces[0][:half], pieces[0][half:]]
            else:
                pieces = [pieces[0] if way == i else None for i in range(2)]
        elif step > 1:
            moved = self.sums[kind]
            pieces = [joined(pieces[1 - i], moved[i], i) for i in range(2)]
        self.sums[kind] = [
            None if piece is None else self.pass_on(piece, i) for i, piece in enumerate(pieces)
        ]

    def total(self, kind):
        pieces = self.made[kind][0] + self.sums[kind]
        return sum(piece.astype(jnp.float32) for piece in pieces)

    def fence(self, *others):
        state = (self.held, self.made, self.sums, others)
        state = lax.optimization_barrier(state)
        self.held, self.made, self.sums, others = state
        return others


def local(
    entering,
    rising_prev,
    falling_cot,
    falling_saved,
    targets,
    norm_gain,
    exit_gain,
    w_gate,
    w_up,
    w_down,
    route_ids,
    route_gates,
    exit_list,
):
    section_index = lax.axis_index("pipe")
    sections = lax.axis_size("pipe")
    sources = lax.axis_size("ep")
    here = lax.axis_index("ep")
    names = jnp.stack([here, here + 1 - 2 * (here % 2)]).astype(jnp.int32)
    norm_row = norm_gain[0]
    exit_row = exit_gain[0]
    ring = Section(sources, names)
    far = ring.far
    planned = far == 4

    fall_wide = falling_saved[0].astype(jnp.float32)
    fall_normal = normed_rows(falling_saved[0], norm_gain)
    fall_normal, leaving_cot, leaving_rise = lax.optimization_barrier(
        (fall_normal, falling_cot[0], rising_prev[0])
    )
    ring.held["fall"] = {0: [fall_normal]}
    ring.gather("fall", 1)
    moved_cot = passed_along(leaving_cot, "pipe", 1)
    own = (w_gate[0, 0], w_up[0, 0], w_down[0, 0])

    def swapped(weight):
        return lax.ppermute(weight, "ep", ring.swap)

    at_start = section_index == 0
    cot_in = jnp.where(at_start, entering[1], moved_cot)

    def entered(moved_rise):
        return jnp.where(at_start, entering[0], moved_rise)

    ring.held["cot"] = {0: [packed_rows(cot_in, route_ids[:, 0], route_gates[:, 0], sources)]}
    ring.held["rise"] = {}

    head_rise = jnp.take(exit_list[0], section_index).astype(jnp.float32)
    head_fall = jnp.take(exit_list[1], sections - 1 - section_index).astype(jnp.float32)

    def exit_heads(rise_in, cot_in, head_rise, head_fall):
        rise_wide = rise_in.astype(jnp.float32)
        rise_diff = normed(rise_wide, exit_row) - targets[0].astype(jnp.float32)
        loss_rise = head_rise * 0.5 * jnp.mean(rise_diff * rise_diff, axis=-1)
        fall_diff = normed(fall_wide, exit_row) - targets[1].astype(jnp.float32)
        loss_fall = head_fall * 0.5 * jnp.mean(fall_diff * fall_diff, axis=-1)
        kept = cot_in.astype(jnp.float32)
        kept = kept + head_fall * norm_pullback(fall_wide, exit_row, fall_diff)
        return kept, jnp.stack([loss_rise, loss_fall])[:, None, :]

    def falling(kept):
        return kept + norm_pullback(fall_wide, norm_row, ring.total("backward"))

    if planned:
        ring.gather("fall", 2)
        own_gate, own_up, own_down = own
        other_gate, other_up = swapped(own_gate), swapped(own_up)
        packed, leaving_rise = lax.optimization_barrier((ring.held["cot"][0][0], leaving_rise))
        ring.held["cot"][0] = [packed]
        moved_rise = passed_along(leaving_rise, "pipe", 1)
        heads = (head_rise, head_fall)
        cot_in, own, own_down, other_gate, other_up, heads, ring.names = ring.fence(
            cot_in, own, own_down, other_gate, other_up, heads, names
        )
        ring.gather("fall", 3)
        ring.gather("cot", 1)
        own = fetched(own)
        moved_rise, own, own_down = ring.fence(moved_rise, own, own_down)
        ring.gather("fall", 4, 0)
        ring.gather("cot", 2)
        ring.weights = own + (other_gate, other_up, None)
        ring.prepare([0, 1, 2, 3])
        other_down = swapped(own_down)
        rise_in = entered(moved_rise)
        rise_normal = normed(rise_in.astype(jnp.float32), norm_row).astype(jnp.bfloat16)
        kept, exit_loss = exit_heads(rise_in, cot_in, *heads)
        rise_normal, kept, exit_loss, other_down = ring.fence(
            rise_normal, kept, exit_loss, other_down
        )
        ring.weights = own + (other_gate, other_up, other_down)
        ring.held["rise"] = {0: [rise_normal]}
        ring.gather("cot", 3)
        ring.gather("rise", 1)
        ring.work("backward", [0, 1, 2])
        ring.prepare([4])
        ring.fence()
        ring.gather("cot", 4)
        ring.gather("rise", 2)
        ring.work("forward", [0, 1])
        ring.fence()
        ring.gather("rise", 3)
        ring.work("backward", [3, 4])
        ring.fence()
        ring.gather("rise", 4)
        ring.scatter("backward", 1)
        ring.work("forward", [2])
        ring.fence()
        ring.scatter("backward", 2)
        ring.work("forward", [3, 4])
        ring.fence()
        ring.scatter("backward", 3)
        ring.scatter("forward", 1)
        ring.fence()
        ring.scatter("backward", 4)
        ring.scatter("forward", 2)
        ring.fence()
        ring.scatter("forward", 3)
        fall_total = falling(kept).astype(jnp.bfloat16)
        (fall_total,) = ring.fence(fall_total)
        ring.scatter("forward", 4)
    else:
        rise_in = entered(passed_along(leaving_rise, "pipe", 1))
        ring.weights = own + tuple(swapped(own))
        kept, exit_loss = exit_heads(rise_in, cot_in, head_rise, head_fall)
        rise_normal = normed(rise_in.astype(jnp.float32), norm_row).astype(jnp.bfloat16)
        ring.held["rise"] = {0: [rise_normal]}
        for name in ("fall", "cot", "rise"):
            for distance in range(1 if name != "fall" else 2, far + 1):
                ring.gather(name, distance)
        groups = [[0, 1]] + [[distance] for distance in range(2, far + 1)]
        for group in groups:
            ring.prepare(group)
            ring.work("backward", group)
        for group in groups:
            ring.work("forward", group)
        for kind in ("backward", "forward"):
            for step in range(1, far + 1):
                ring.scatter(kind, step)
        fall_total = falling(kept).astype(jnp.bfloat16)
    layer_out = (rise_in.astype(jnp.float32) + ring.total("forward")).astype(jnp.bfloat16)
    return (layer_out[None], fall_total[None], exit_loss)


def solution(mesh):
    placed = (
        P(None, "ep", None),
        P("pipe", "ep", None),
        P("pipe", "ep", None),
        P("pipe", "ep", None),
        P(None, "ep", None),
        P("pipe", None),
        P("pipe", None),
        P("pipe", "ep", None, None),
        P("pipe", "ep", None, None),
        P("pipe", "ep", None, None),
        P(None, "pipe", "ep", None),
        P(None, "pipe", "ep", None),
        P(),
    )
    return jax.shard_map(
        local,
        mesh=mesh,
        in_specs=placed,
        out_specs=(P("pipe", "ep", None), P("pipe", "ep", None), P(None, "pipe", "ep")),
        check_vma=False,
    )
```
